32 devices in a mesh: batch: 4 (over y, x), seq: 8 (over z, core).
Axes of the slice: x: 2, y: 2, z: 4, core: 2. Of those that a mesh axis runs over, the one named last changes fastest.
Arguments:
- tokens: bfloat16 [4, 4096, 768], P('batch', 'seq'), may hold values from -6 to 6
- cotangent: bfloat16 [4, 4096, 768], P('batch', 'seq'), may hold values from -6 to 6
- norm_gains: bfloat16 [2, 2, 768], P(None, None, ('batch', 'seq')), may hold values from 0.25 to 1.75
- w_in: bfloat16 [2, 768, 2304], P(None, ('batch', 'seq')), may hold values from -0.21875 to 0.21875
- short_conv: bfloat16 [2, 3, 2304], P(None, None, ('batch', 'seq')), may hold values from -3.5 to 3.5
- w_out: bfloat16 [2, 768, 768], P(None, ('batch', 'seq')), may hold values from -0.21875 to 0.21875
- w_fc: bfloat16 [2, 768, 3072], P(None, ('batch', 'seq')), may hold values from -0.21875 to 0.21875
- w_proj: bfloat16 [2, 3072, 768], P(None, ('batch', 'seq')), may hold values from -0.109375 to 0.109375
- filt_w1: float32 [2, 33, 64], replicated, may hold values from -2.5 to 2.5
- filt_b1: float32 [2, 64], replicated, may hold values from -3.140625 to 3.140625
- filt_w2: float32 [2, 64, 64], replicated, may hold values from -1.25 to 1.25
- filt_b2: float32 [2, 64], replicated, may hold values from -3.140625 to 3.140625
- filt_w3: float32 [2, 64, 768], P(None, None, 'seq'), may hold values from -0.75 to 0.75
- skip_gain: float32 [2, 768], P(None, 'seq'), may hold values from -4 to 4
- decay_rate: float32 [2, 768], P(None, 'seq'), may hold values from 0.3 to 300
Outputs:
- mixed_out: bfloat16 [4, 4096, 768], P('batch', 'seq')
- grad_tokens: float32 [4, 4096, 768], P('batch', 'seq')
- grad_gains: float32 [2, 2, 768], P(None, None, ('batch', 'seq'))
- grad_w_in: float32 [2, 768, 2304], P(None, ('batch', 'seq'))
- grad_short_conv: float32 [2, 3, 2304], P(None, None, ('batch', 'seq'))
- grad_w_out: float32 [2, 768, 768], P(None, ('batch', 'seq'))
- grad_w_fc: float32 [2, 768, 3072], P(None, ('batch', 'seq'))
- grad_w_proj: float32 [2, 3072, 768], P(None, ('batch', 'seq'))
- grad_filt_w1: float32 [2, 33, 64], replicated
- grad_filt_b1: float32 [2, 64], replicated
- grad_filt_w2: float32 [2, 64, 64], replicated
- grad_filt_b2: float32 [2, 64], replicated
- grad_filt_w3: float32 [2, 64, 768], P(None, None, 'seq')
- grad_skip: float32 [2, 768], P(None, 'seq')
The draws below stay inside these ranges and needn't reach their ends.
All inputs are finite; a program needn't handle non-finite values.
Results may differ from the reference program's by a relative error of at most 0.02.
Values may be sent and summed in bfloat16 or wider, within the bound.
A program may use at most 384 MiB of HBM per device.

```python
import math
import jax
import jax.numpy as jnp
from jax import lax

D = 768
FF = 3072
EMB = 33
FILT = 64
LAYERS = 2
LEN = 4096
SEQS = 4


def signed_band(key, shape, lower, upper):
    size_key, sign_key = jax.random.split(key)
    magnitude = jax.random.uniform(size_key, shape, jnp.float32, lower, upper)
    positive = jax.random.bernoulli(sign_key, 0.5, shape)
    return jnp.where(positive, magnitude, -magnitude)


def draw_filt_w1(key, part):
    key = jax.random.fold_in(key, 11)
    return signed_band(key, (LAYERS, EMB, FILT), 1.0, 2.5).astype(jnp.float32)


def draw_filt_w2(key, part):
    key = jax.random.fold_in(key, 23)
    return signed_band(key, (LAYERS, FILT, FILT), 0.75, 1.25).astype(jnp.float32)


def steps_of(own_key, shape, cuts, smallest, top_value):
    def one(dim, parts):
        heights = jax.random.uniform(jax.random.fold_in(jax.random.fold_in(own_key, 6), dim), (parts,), jnp.float32, smallest / len(cuts), top_value / len(cuts))
        return jnp.repeat(jnp.exp(heights), shape[dim] // parts).reshape((-1,) + (1,) * (len(shape) - dim - 1))

    factor_of = one(*cuts[0])
    for cut in cuts[1:]:
        factor_of = factor_of * one(*cut)
    return factor_of


def centred(stream_key, extent, deviation, most, cuts=(), kind=jnp.bfloat16):
    array = jax.random.normal(stream_key, extent, jnp.float32) * deviation
    if len(cuts) > 0:
        array = steps_of(stream_key, extent, cuts, -0.22, 0.18) * array
    return jnp.clip(array, min=-most, max=most).astype(kind)


def setup_inputs(seed: int = 0) -> dict:
    seeds = jax.random.split(jax.random.key(seed), 16)
    tokens = centred(seeds[0], (SEQS, LEN, D), 1.0, 6.0, ((0, 4), (1, 8)))
    cotangent = centred(seeds[1], (SEQS, LEN, D), 1.0, 6.0, ((0, 4), (1, 8)))
    norm_gains = jnp.clip(1.0 + 0.15 * jax.random.normal(seeds[2], (LAYERS, 2, D), jnp.float32), 0.25, 1.75).astype(jnp.bfloat16)
    w_in = centred(seeds[3], (LAYERS, D, 3 * D), D ** -0.5, 0.21875, ((1, 32),))
    short_conv = centred(seeds[4], (LAYERS, 3, 3 * D), 3 ** -0.5, 3.5, ((2, 32),))
    w_out = centred(seeds[5], (LAYERS, D, D), D ** -0.5, 0.21875, ((1, 32),))
    w_fc = centred(seeds[6], (LAYERS, D, FF), D ** -0.5, 0.21875, ((1, 32),))
    w_proj = centred(seeds[7], (LAYERS, FF, D), FF ** -0.5, 0.109375, ((1, 32),))
    filt_w1 = draw_filt_w1(jax.random.fold_in(seeds[15], 71), 0)
    filt_b1 = jnp.clip(jax.random.uniform(seeds[9], (LAYERS, FILT), jnp.float32, -3.140625, 3.140625), -3.140625, 3.140625)
    filt_w2 = draw_filt_w2(jax.random.fold_in(seeds[15], 71), 0)
    filt_b2 = jnp.clip(jax.random.uniform(seeds[11], (LAYERS, FILT), jnp.float32, -3.140625, 3.140625), -3.140625, 3.140625)
    filt_w3 = centred(seeds[12], (LAYERS, FILT, D), FILT ** -0.5, 0.75, ((2, 8),), jnp.float32)
    skip_gain = centred(seeds[13], (LAYERS, D), 1.0, 4.0, ((1, 8),), jnp.float32)
    decay_rate = jnp.clip(jnp.exp(math.log(300.0) - 6.9077552 * jax.random.uniform(seeds[14], (LAYERS, D), jnp.float32) ** steps_of(seeds[14], (LAYERS, D), ((1, 8),), -0.2, 0.2)), 0.3, 300.0)
    return {"tokens": tokens, "cotangent": cotangent, "norm_gains": norm_gains, "w_in": w_in, "short_conv": short_conv, "w_out": w_out, "w_fc": w_fc, "w_proj": w_proj, "filt_w1": filt_w1, "filt_b1": filt_b1, "filt_w2": filt_w2, "filt_b2": filt_b2, "filt_w3": filt_w3, "skip_gain": skip_gain, "decay_rate": decay_rate}


@jax.custom_vjp
def low(v):
    return lax.optimization_barrier(v.astype(jnp.bfloat16)).astype(jnp.float32)

@jax.custom_vjp
def low_back(v):
    return v

def low_keep(v):
    return (low(v), None)

def low_pass(kept, grad):
    return (grad,)

def back_keep(v):
    return (v, None)

def back_low(kept, grad):
    return (low(grad),)
low.defvjp(low_keep, low_pass)
low_back.defvjp(back_keep, back_low)

def matmul_hi(left_mat, right_mat):
    return jnp.dot(left_mat, right_mat, precision=lax.Precision.HIGHEST)

def position_table(length, emb_width):
    positions = jnp.arange(length, dtype=jnp.int32)
    band_ids = jnp.arange(1, (emb_width - 1) // 2 + 1, dtype=jnp.int32)
    phases = positions[:, None] * band_ids[None, :] % length
    angles = 2.0 * math.pi / length * phases.astype(jnp.float32)
    ramp_col = positions.astype(jnp.float32)[:, None] / length
    return jnp.concatenate([ramp_col, jnp.cos(angles), jnp.sin(angles)], axis=1)

def make_filter(pos_table, decay_row, first_w, first_b, second_w, second_b, third_w):
    length = pos_table.shape[0]
    first_act = jnp.sin(matmul_hi(pos_table, first_w) + first_b)
    second_act = jnp.sin(matmul_hi(first_act, second_w) + second_b)
    raw_taps = matmul_hi(second_act, third_w)
    ramp_col = jnp.arange(length, dtype=jnp.float32)[:, None] / length
    shaped = raw_taps * jnp.exp(-ramp_col * decay_row[None, :])
    norm_scale = lax.rsqrt(lax.optimization_barrier(jnp.mean(shaped * shaped, axis=0, keepdims=True)) + 1e-05)
    return shaped * norm_scale * length ** (-0.5)

def long_conv(signal, filter_taps):
    padded_len = 2 * signal.shape[0]
    spectrum = jnp.fft.rfft(signal, n=padded_len, axis=0) * jnp.fft.rfft(filter_taps, n=padded_len, axis=0)
    return jnp.fft.irfft(spectrum, n=padded_len, axis=0)[:signal.shape[0]]

def layer_norm(stream, gain_row):
    mean_val = lax.optimization_barrier(jnp.mean(stream, axis=-1, keepdims=True))
    centered = stream - mean_val
    variance = lax.optimization_barrier(jnp.mean(centered * centered, axis=-1, keepdims=True))
    return centered * lax.rsqrt(variance + 1e-05) * gain_row

def layer(stream, gain_pair, in_mat, conv_weights, out_mat, fc_mat, proj_mat, first_w, first_b, second_w, second_b, third_w, skip_row, decay_row, pos_table):
    model_width = stream.shape[1]
    length = stream.shape[0]
    normed_in = low(layer_norm(stream, gain_pair[0]))
    mixed_in = low(low_back(matmul_hi(normed_in, in_mat)))
    padded = jnp.pad(mixed_in, ((2, 0), (0, 0)))
    short_out = conv_weights[0] * padded[:length] + conv_weights[1] * padded[1:length + 1] + conv_weights[2] * padded[2:]
    queries = short_out[:, :model_width]
    keys_part = short_out[:, model_width:2 * model_width]
    values_part = short_out[:, 2 * model_width:]
    signal = low(low_back(keys_part * values_part))
    filter_taps = make_filter(pos_table, decay_row, first_w, first_b, second_w, second_b, third_w)
    long_out = low(low_back(long_conv(signal, filter_taps) + skip_row * signal))
    gated_out = low(queries * long_out)
    middle = stream + low_back(matmul_hi(gated_out, out_mat))
    hidden_in = low(layer_norm(middle, gain_pair[1]))
    hidden_pre = low_back(matmul_hi(hidden_in, fc_mat))
    hidden_act = low(jax.nn.gelu(hidden_pre))
    return middle + low_back(matmul_hi(hidden_act, proj_mat))

def reference(tokens, cotangent, norm_gains, w_in, short_conv, w_out, w_fc, w_proj, filt_w1, filt_b1, filt_w2, filt_b2, filt_w3, skip_gain, decay_rate):
    params = tuple((member_arr.astype(jnp.float32) for member_arr in (norm_gains, w_in, short_conv, w_out, w_fc, w_proj, filt_w1, filt_b1, filt_w2, filt_b2, filt_w3, skip_gain)))
    decay_rows = decay_rate.astype(jnp.float32)
    pos_table = position_table(LEN, EMB)

    def forward(stream, weights):
        for layer_idx in range(LAYERS):
            stream = layer(stream, *[member[layer_idx] for member in weights], decay_rows[layer_idx], pos_table)
        return stream

    def per_sequence(totals, sequence_pair):
        sequence, cot_rows = sequence_pair
        result, pullback = jax.vjp(forward, sequence.astype(jnp.float32), params)
        grad_stream, grad_params = pullback(cot_rows.astype(jnp.float32))
        return (jax.tree.map(jnp.add, totals, grad_params), (result.astype(jnp.bfloat16), grad_stream))
    start_grads = jax.tree.map(jnp.zeros_like, params)
    totals, outputs = lax.scan(per_sequence, start_grads, (tokens, cotangent))
    return (outputs[0], outputs[1], totals[0], totals[1], totals[2], totals[3], totals[4], totals[5], totals[6], totals[7], totals[8], totals[9], totals[10], totals[11])
```

```python
import functools
import math

import jax
import jax.numpy as jnp
import numpy as np
from jax import lax
from jax.experimental import pallas as pl
from jax.experimental.pallas import tpu as pltpu
from jax.sharding import PartitionSpec as P

MESH = pl.DeviceIdType.MESH
LANES = 128
VMEM_LIMIT = 56 * 1024 * 1024
f32 = jnp.float32
bf16 = jnp.bfloat16
HIGH = lax.Precision.HIGHEST


def product(left_mat, right_mat):
    return jnp.dot(left_mat, right_mat, preferred_element_type=f32)


def contract(left_mat, right_mat, left_dim, right_dim):
    return lax.dot_general(
        left_mat, right_mat, (((left_dim,), (right_dim,)), ((), ())), preferred_element_type=f32
    )


def layer_norm_parts(stream):
    mean_val = jnp.mean(stream, axis=-1, keepdims=True)
    centered = stream - mean_val
    inv_std = lax.rsqrt(jnp.mean(centered * centered, axis=-1, keepdims=True) + 1e-05)
    return (centered * inv_std, inv_std)


def norm_back(grad_normed, normed, inv_std):
    mean_grad = jnp.mean(grad_normed, axis=-1, keepdims=True)
    mean_cross = jnp.mean(grad_normed * normed, axis=-1, keepdims=True)
    return inv_std * (grad_normed - mean_grad - normed * mean_cross)


def shifted(value, axis, steps):
    count = lax.axis_size(axis)
    first, last = (max(0, -steps), min(count, count - steps))
    return lax.ppermute(value, axis, [(source, source + steps) for source in range(first, last)])


def split_bf16(table):
    high = table.astype(np.float32).astype(jnp.bfloat16)
    low = (table - high.astype(np.float64)).astype(np.float32).astype(jnp.bfloat16)
    return jnp.asarray(high), jnp.asarray(low)


def transform_tables(blocks):
    length = blocks * LANES
    n1 = np.arange(blocks)
    n2 = np.arange(LANES)
    outer = 2 * np.pi * ((n1[:, None] * (4 * n1[None, :] + 1)) % (4 * blocks)) / (4 * blocks)
    eye = np.eye(8)
    forward = np.concatenate([np.cos(outer).T, -np.sin(outer).T], axis=0)
    left_fwd = np.kron(forward, eye)
    left_inv = np.kron(np.concatenate([np.cos(outer), -np.sin(outer)], axis=1), eye) / length
    inner = 2 * np.pi * ((n2[:, None] * n2[None, :]) % LANES) / LANES
    cos2, sin2 = np.cos(inner), np.sin(inner)
    right_fwd = np.block([[cos2, -sin2], [sin2, cos2]])
    right_inv = np.block([[cos2, sin2], [-sin2, cos2]])
    twist = 2 * np.pi * (n2[None, :] * (4 * n1[:, None] + 1)) / (4 * length)
    twist_cos = np.repeat(np.cos(twist), 8, axis=0).astype(np.float32)
    twist_sin = np.repeat(np.sin(twist), 8, axis=0).astype(np.float32)
    tables = []
    for table in (left_fwd, right_fwd, left_inv, right_inv):
        tables.extend(split_bf16(table))
    return tuple(tables) + (jnp.asarray(twist_cos), jnp.asarray(twist_sin))


def dot_split(left_high, left_low, right):
    high = right.astype(bf16)
    low = (right - high.astype(f32)).astype(bf16)
    return product(left_high, high) + product(left_low, high) + product(left_high, low)


def dot_right_split(left, right_high, right_low):
    high = left.astype(bf16)
    low = (left - high.astype(f32)).astype(bf16)
    return product(high, right_high) + product(high, right_low) + product(low, right_high)


def to_points(x, tables, exact):
    left_high, left_low, right_high, right_low = [t[...] for t in tables[:4]]
    twist_cos, twist_sin = tables[8][...], tables[9][...]
    rows = x.shape[0] * 8
    flat = x.reshape(rows, LANES)
    if exact:
        flat = flat.astype(bf16)
        turned = product(left_high, flat) + product(left_low, flat)
    else:
        turned = dot_split(left_high, left_low, flat)
    re, im = turned[:rows], turned[rows:]
    both = jnp.concatenate([re * twist_cos + im * twist_sin, im * twist_cos - re * twist_sin], axis=1)
    points = dot_right_split(both, right_high, right_low)
    return points[:, :LANES], points[:, LANES:]


def from_points(re, im, tables):
    left_high, left_low, right_high, right_low = [t[...] for t in tables[4:8]]
    twist_cos, twist_sin = tables[8][...], tables[9][...]
    rows = re.shape[0]
    back = dot_right_split(jnp.concatenate([re, im], axis=1), right_high, right_low)
    re, im = back[:, :LANES], back[:, LANES:]
    both = jnp.concatenate([re * twist_cos - im * twist_sin, re * twist_sin + im * twist_cos], axis=0)
    return dot_split(left_high, left_low, both).reshape(rows // 8, 8, LANES)


def position_rows(length, emb_width):
    positions = np.arange(length, dtype=np.int64)
    bands = np.arange(1, (emb_width - 1) // 2 + 1, dtype=np.int64)
    angles = 2.0 * np.pi / length * ((bands[:, None] * positions[None, :]) % length)
    table = np.concatenate([positions[None, :] / length, np.cos(angles), np.sin(angles)], axis=0)
    return jnp.asarray(table.astype(np.float32))


def filter_forward(pos_rows, first_w, first_b, second_w, second_b, third_w, decay_col):
    length = pos_rows.shape[1]
    first_arg = jnp.dot(first_w.T, pos_rows, precision=HIGH) + first_b[:, None]
    first_act = jnp.sin(first_arg)
    second_arg = jnp.dot(second_w.T, first_act, precision=HIGH) + second_b[:, None]
    second_act = jnp.sin(second_arg)
    raw = jnp.dot(third_w.T, second_act, precision=HIGH)
    ramp = jnp.arange(length, dtype=f32)[None, :] / length
    window = jnp.exp(-ramp * decay_col[:, None])
    shaped = raw * window
    scale = lax.rsqrt(jnp.mean(shaped * shaped, axis=1, keepdims=True) + 1e-05)
    taps = shaped * scale * length ** (-0.5)
    return taps


class Place:
    def __init__(self, ns):
        self.nz = ns // 2
        self.b = lax.axis_index("batch")
        self.s = lax.axis_index("seq")
        self.z = lax.div(self.s, 2)
        self.c = lax.rem(self.s, 2)
        self.x_peer = (lax.bitwise_xor(self.b, 1), self.s)
        self.y_peer = (lax.bitwise_xor(self.b, 2), self.s)
        self.core_peer = (self.b, lax.bitwise_xor(self.s, 1))
        self.up_peer = (self.b, lax.min(self.s + 2, ns - 1))
        self.down_peer = (self.b, lax.max(self.s - 2, 0))


def remote(src, dst, send, recv, peer):
    return pltpu.make_async_remote_copy(
        src_ref=src, dst_ref=dst, send_sem=send, recv_sem=recv, device_id=peer, device_id_type=MESH
    )


def greet(place, seq_peers):
    bar = pltpu.get_barrier_semaphore()

    def hello(peer):
        pl.semaphore_signal(bar, inc=1, device_id=peer, device_id_type=MESH)

    hello(place.x_peer)
    hello(place.y_peer)
    if seq_peers:
        ns = 2 * place.nz
        for step in range(1, ns):
            hello((place.b, lax.rem(place.s + step, ns)))
        pl.semaphore_wait(bar, 2 + ns - 1)
    else:
        hello(place.core_peer)
        pl.when(place.z + 1 < place.nz)(lambda: hello(place.up_peer))
        pl.when(place.z > 0)(lambda: hello(place.down_peer))
        ends = jnp.where(place.z == 0, 1, 0) + jnp.where(place.z == place.nz - 1, 1, 0)
        pl.semaphore_wait(bar, 5 - ends)


def gather_sems(nz):
    return [
        pltpu.SemaphoreType.DMA((4,)),
        pltpu.SemaphoreType.DMA((2, nz)),
        pltpu.SemaphoreType.DMA((nz,)),
        pltpu.SemaphoreType.DMA((4, nz)),
        pltpu.SemaphoreType.DMA((4, nz)),
    ]


def gather_task(place, src, dst, sems):
    one, chain_send, chain_recv, send, recv = sems
    b, z, c, nz = place.b, place.z, place.c, place.nz
    bx, by, bd = place.x_peer[0], place.y_peer[0], lax.bitwise_xor(b, 3)
    own = dst.at[b, z, c]
    local = pltpu.make_async_copy(src, own, one.at[0])

    def chain(source, shard, up):
        row = 0 if up else 1
        peer = place.up_peer if up else place.down_peer
        return remote(source, dst.at[b, shard, c], chain_send.at[row, shard], chain_recv.at[shard], peer)

    def across(source, shard, along):
        peer = place.y_peer if along else place.x_peer
        return remote(source, dst.at[b, shard, c], send.at[along, shard], recv.at[along, shard], peer)

    def onward(shard, along):
        peer = place.y_peer if along else place.x_peer
        part = dst.at[bx if along else by, shard, c]
        return remote(part, part, send.at[2 + along, shard], recv.at[2 + along, shard], peer)

    local.start()
    pl.when(z + 1 < nz)(lambda: chain(src, z, True).start())
    pl.when(z > 0)(lambda: chain(src, z, False).start())
    across(src, z, 0).start()
    across(src, z, 1).start()
    yield
    for hop in range(1, nz):
        below, above = z - hop, z + hop

        @pl.when(below >= 0)
        def _():
            chain(src, below, True).wait_recv()
            part = dst.at[b, below, c]
            pl.when(z + 1 < nz)(lambda: chain(part, below, True).start())
            across(part, below, 0).start()
            across(part, below, 1).start()

        @pl.when(above < nz)
        def _():
            chain(src, above, False).wait_recv()
            part = dst.at[b, above, c]
            pl.when(z > 0)(lambda: chain(part, above, False).start())
            across(part, above, 0).start()
            across(part, above, 1).start()

        yield

    def pass_on(shard):
        across(src, shard, 0).wait_recv()
        across(src, shard, 1).wait_recv()
        even = lax.rem(shard, 2) == 0
        pl.when(even)(lambda: onward(shard, 1).start())
        pl.when(jnp.logical_not(even))(lambda: onward(shard, 0).start())

    pass_on(z)
    for hop in range(1, nz):
        pl.when(z - hop >= 0)(lambda: pass_on(z - hop))
        pl.when(z + hop < nz)(lambda: pass_on(z + hop))
    yield
    for shard in range(nz):
        onward(shard, 1 - shard % 2).wait_recv()
    local.wait()
    column = dst.at[:, :, c]
    core = remote(column, column, one.at[1], one.at[2], place.core_peer)
    core.start()
    yield
    for shard in range(nz):
        if shard > 0:
            pl.when(jnp.logical_and(z >= shard, z + 1 < nz))(
                lambda: chain(src, z - shard, True).wait_send()
            )
            pl.when(jnp.logical_and(z + shard < nz, z > 0))(
                lambda: chain(src, z + shard, False).wait_send()
            )
        else:
            pl.when(z + 1 < nz)(lambda: chain(src, z, True).wait_send())
            pl.when(z > 0)(lambda: chain(src, z, False).wait_send())
        across(src, shard, 0).wait_send()
        across(src, shard, 1).wait_send()
        onward(shard, 1 - shard % 2).wait_send()
    core.wait()
    yield


def run_staggered(tasks):
    live = []
    waiting = list(tasks)
    while live or waiting:
        if waiting:
            live.append(waiting.pop(0))
        for task in reversed(list(live)):
            if next(task, "end") == "end":
                live.remove(task)


def gather_kernel(ns, picks, *refs):
    count = len(picks)
    srcs, dsts, sems = refs[:count], refs[count : 2 * count], refs[2 * count :]
    place = Place(ns)
    greet(place, False)
    run_staggered(
        gather_task(place, srcs[i].at[layer], dsts[i], sems[5 * i : 5 * i + 5])
        for i, layer in enumerate(picks)
    )


def gather(arrays, picks, collective_id):
    nb, ns = lax.axis_size("batch"), lax.axis_size("seq")
    nz = ns // 2
    count = len(arrays)
    scratch = []
    for _ in arrays:
        scratch.extend(gather_sems(nz))
    results = pl.pallas_call(
        functools.partial(gather_kernel, ns, picks),
        out_shape=[jax.ShapeDtypeStruct((nb, nz, 2) + a.shape[1:], a.dtype) for a in arrays],
        in_specs=[pl.BlockSpec(memory_space=pl.ANY)] * count,
        out_specs=[pl.BlockSpec(memory_space=pl.ANY)] * count,
        scratch_shapes=scratch,
        compiler_params=pltpu.CompilerParams(collective_id=collective_id, has_side_effects=True),
        name="gather_weights",
    )(*arrays)
    return [r.reshape((nb * ns,) + a.shape[1:]) for r, a in zip(results, arrays)]


def reduce_scratch(nz, shape, dtype):
    half = (nz,) + shape
    return [
        pltpu.VMEM((4,) + half, dtype),
        pltpu.VMEM((4,) + half, dtype),
        pltpu.VMEM((5,) + half, dtype),
        pltpu.VMEM(shape, f32),
        pltpu.SemaphoreType.DMA((4,)),
        pltpu.SemaphoreType.DMA((5, nz)),
        pltpu.SemaphoreType.DMA((5, nz)),
    ]


def reduce_task(place, src, out, scratch):
    acc, other, box, total, one, send, recv = scratch
    kind = acc.dtype
    b, z, c, nz = place.b, place.z, place.c, place.nz
    bx, by, bd = place.x_peer[0], place.y_peer[0], lax.bitwise_xor(b, 3)
    far, via_x, via_y, up, down = range(5)

    def add(target, lane, shard):
        acc[target, shard] = (
            acc[target, shard].astype(f32) + box[lane, shard].astype(f32)
        ).astype(kind)

    def move(part, shard, lane, peer):
        return remote(acc.at[part, shard], box.at[lane, shard], send.at[lane, shard], recv.at[lane, shard], peer)

    mine = pltpu.make_async_copy(src.at[:, :, c], acc, one.at[0])
    core = remote(src.at[:, :, 1 - c], other, one.at[1], one.at[2], place.core_peer)
    core.start()
    mine.start()
    yield
    mine.wait()
    core.wait()

    @pl.loop(0, 4 * nz)
    def _(i):
        part, shard = lax.div(i, nz), lax.rem(i, nz)
        acc[part, shard] = (
            acc[part, shard].astype(f32) + other[part, shard].astype(f32)
        ).astype(kind)

    for shard in range(nz):
        if shard % 2 == 0:
            move(bd, shard, far, place.x_peer).start()
            move(bx, shard, via_x, place.x_peer).start()
        else:
            move(bd, shard, far, place.y_peer).start()
            move(by, shard, via_y, place.y_peer).start()
    yield
    for shard in range(nz):
        move(bd, shard, far, place.x_peer).wait_recv()
        if shard % 2 == 0:
            add(by, far, shard)
            move(by, shard, via_y, place.y_peer).start()
        else:
            add(bx, far, shard)
            move(bx, shard, via_x, place.x_peer).start()
    yield
    for shard in range(nz):
        move(bx, shard, via_x, place.x_peer).wait_recv()
        move(by, shard, via_y, place.y_peer).wait_recv()
        acc[b, shard] = (
            acc[b, shard].astype(f32) + box[via_x, shard].astype(f32) + box[via_y, shard].astype(f32)
        ).astype(kind)
    yield
    for shard in reversed(range(nz)):

        @pl.when(z < shard)
        def _():
            @pl.when(z > 0)
            def _():
                move(b, shard, up, place.up_peer).wait_recv()
                add(b, up, shard)

            move(b, shard, up, place.up_peer).start()

    for shard in range(nz):

        @pl.when(z > shard)
        def _():
            @pl.when(z + 1 < nz)
            def _():
                move(b, shard, down, place.down_peer).wait_recv()
                add(b, down, shard)

            move(b, shard, down, place.down_peer).start()

    yield
    total[...] = acc[b, z].astype(f32)

    @pl.when(z > 0)
    def _():
        move(b, z, up, place.up_peer).wait_recv()
        total[...] += box[up, z].astype(f32)

    @pl.when(z + 1 < nz)
    def _():
        move(b, z, down, place.down_peer).wait_recv()
        total[...] += box[down, z].astype(f32)

    result = pltpu.make_async_copy(total, out, one.at[3])
    result.start()
    for shard in range(nz):
        for lane in (far, via_x, via_y):
            move(b, shard, lane, place.x_peer).wait_send()
        pl.when(z < shard)(lambda: move(b, shard, up, place.up_peer).wait_send())
        pl.when(z > shard)(lambda: move(b, shard, down, place.down_peer).wait_send())
    result.wait()
    yield


def reduce_kernel(ns, count, *refs):
    srcs, outs, scratch = refs[:count], refs[count : 2 * count], refs[2 * count :]
    place = Place(ns)
    greet(place, False)
    run_staggered(
        reduce_task(place, srcs[i], outs[i], scratch[7 * i : 7 * i + 7]) for i in range(count)
    )


def total_scratch(nz, shape, shared):
    return [
        pltpu.VMEM((3,) + shape, f32),
        pltpu.VMEM((2,) + shape, f32),
        pltpu.VMEM((2, nz, shared, LANES), f32),
        pltpu.SemaphoreType.DMA((2, 3)),
        pltpu.SemaphoreType.DMA((2, nz)),
    ]


def total_task(place, src, out, scratch):
    box, sums, lines, pair, chain = scratch
    z, c, nz = place.z, place.c, place.nz
    rows = src.shape[0]
    shared = lines.shape[2]
    tail = pl.ds(rows - shared, shared)

    def swap(source, dst, i, peer):
        return remote(source, dst, pair.at[0, i], pair.at[1, i], peer)

    first = swap(src, box.at[0], 0, place.x_peer)
    first.start()
    yield
    first.wait()
    sums[0] = src[...] + box[0]
    second = swap(sums.at[0], box.at[1], 1, place.y_peer)
    second.start()
    yield
    second.wait()
    sums[1] = sums[0] + box[1]
    third = swap(sums.at[1, tail], box.at[2, tail], 2, place.core_peer)
    third.start()
    yield
    third.wait()
    lines[0, z] = sums[1, tail] + box[2, tail]

    def along(step):
        peer = lax.rem(z + step, nz)
        return remote(lines.at[0, z], lines.at[1, z], chain.at[0, step], chain.at[1, step], (place.b, 2 * peer + c))

    for step in range(1, nz):
        along(step).start()
    lines[1, z] = lines[0, z]
    yield
    for step in range(1, nz):
        along(step).wait_recv()
    value = lines[1, 0]
    for shard in range(1, nz):
        value = value + lines[1, shard]
    out[: rows - shared] = sums[1, : rows - shared]
    out[tail] = value
    for step in range(1, nz):
        along(step).wait_send()
    yield


def last_kernel(ns, count, *refs):
    srcs, payload = refs[:count], refs[count]
    outs, totals = refs[count + 1 : 2 * count + 1], refs[2 * count + 1]
    scratch = refs[2 * count + 2 :]
    place = Place(ns)
    greet(place, True)
    tasks = [reduce_task(place, srcs[i], outs[i], scratch[7 * i : 7 * i + 7]) for i in range(count)]
    run_staggered([total_task(place, payload, totals, scratch[7 * count :])] + tasks)


def last_reduce(arrays, payload, shared, collective_id):
    nb, ns = lax.axis_size("batch"), lax.axis_size("seq")
    nz = ns // 2
    count = len(arrays)
    scratch = []
    for a in arrays:
        scratch.extend(reduce_scratch(nz, a.shape[1:], a.dtype))
    scratch.extend(total_scratch(nz, payload.shape, shared))
    hbm = pl.BlockSpec(memory_space=pl.ANY)
    *summed, totals = pl.pallas_call(
        functools.partial(last_kernel, ns, count),
        out_shape=[jax.ShapeDtypeStruct(a.shape[1:], f32) for a in arrays]
        + [jax.ShapeDtypeStruct(payload.shape, f32)],
        in_specs=[hbm] * count + whole(1),
        out_specs=[hbm] * count + whole(1),
        scratch_shapes=scratch,
        compiler_params=pltpu.CompilerParams(
            collective_id=collective_id, has_side_effects=True, vmem_limit_bytes=VMEM_LIMIT
        ),
        name="last_reduce",
    )(*[a.reshape((nb, nz, 2) + a.shape[1:]) for a in arrays], payload)
    return summed, totals


def reduce_scatter(arrays, collective_id):
    nb, ns = lax.axis_size("batch"), lax.axis_size("seq")
    nz = ns // 2
    count = len(arrays)
    scratch = []
    for a in arrays:
        scratch.extend(reduce_scratch(nz, a.shape[1:], a.dtype))
    return pl.pallas_call(
        functools.partial(reduce_kernel, ns, count),
        out_shape=[jax.ShapeDtypeStruct(a.shape[1:], f32) for a in arrays],
        in_specs=[pl.BlockSpec(memory_space=pl.ANY)] * count,
        out_specs=[pl.BlockSpec(memory_space=pl.ANY)] * count,
        scratch_shapes=scratch,
        compiler_params=pltpu.CompilerParams(
            collective_id=collective_id, has_side_effects=True, vmem_limit_bytes=VMEM_LIMIT
        ),
        name="reduce_grads",
    )(*[a.reshape((nb, nz, 2) + a.shape[1:]) for a in arrays])


def conv_lanes(value, rim_near, rim_far):
    lane = lax.broadcasted_iota(jnp.int32, value.shape, 1)
    near = jnp.where(lane == 0, rim_near, pltpu.roll(value, 1, 1))
    far = jnp.where(lane == 0, rim_far, jnp.where(lane == 1, rim_near, pltpu.roll(value, 2, 1)))
    return near, far


def short_out(mixed, aux, stream, block):
    value = mixed[stream, block].astype(f32)
    side = aux[stream, block]
    near, far = conv_lanes(value, side[:, 3:4], side[:, 4:5])
    return side[:, 0:1] * far + side[:, 1:2] * near + side[:, 2:3] * value


def rows_of(refs, group, index):
    return [ref[group, index] for ref in refs]


def sub_rows(chans):
    return 16 if chans % 16 == 0 else chans


def seq_send(place, ns, step, src_of, dst, send, recv):
    peer = lax.rem(place.s + step, ns)
    return remote(src_of(peer), dst, send, recv, (place.b, peer))


def mix_kernel(ns, groups, mixed, aux, spec_re, spec_im, skip, *refs):
    tables = refs[:10]
    long_out, gated, sig_re, sig_im = refs[10:14]
    signal, chan_in, chan_out, tok_in, send, recv = refs[14:]
    place = Place(ns)
    quarters = signal.shape[2]
    chans = signal.shape[3]
    take = sub_rows(chans)
    greet(place, True)

    def to_chan(g, step):
        peer = lax.rem(place.s + step, ns)
        return remote(
            signal.at[peer, g],
            chan_in.at[g, pl.ds(place.s * quarters, quarters)],
            send.at[0, g, step],
            recv.at[0, g, step],
            (place.b, peer),
        )

    def to_tok(g, step):
        peer = lax.rem(place.s + step, ns)
        return remote(
            chan_out.at[g, pl.ds(peer * quarters, quarters)],
            tok_in.at[place.s, g],
            send.at[1, g, step],
            recv.at[1, g, step],
            (place.b, peer),
        )

    for g in range(groups):

        @pl.loop(1, ns + 1)
        def _(step):
            peer = lax.rem(place.s + step, ns)
            block = peer * groups + g
            value = (
                short_out(mixed, aux, 1, block) * short_out(mixed, aux, 2, block)
            ).astype(bf16)

            @pl.when(step < ns)
            def _():
                for q in range(quarters):
                    signal[peer, g, q] = value[:, q * LANES : (q + 1) * LANES]
                to_chan(g, step).start()

            @pl.when(step == ns)
            def _():
                for q in range(quarters):
                    chan_in[g, place.s * quarters + q] = value[:, q * LANES : (q + 1) * LANES]

    for g in range(groups):

        @pl.loop(1, ns)
        def _(step):
            to_chan(g, step).wait_recv()

        @pl.loop(0, chans // take)
        def _(i):
            at = pl.ds(pl.multiple_of(i * take, take), take)
            block = chan_in[g, :, at, :].astype(f32)
            parts = []
            for j in range(take // 8):
                index = (g * chans) // 8 + i * (take // 8) + j
                x = block[:, 8 * j : 8 * j + 8, :]
                re, im = to_points(x, tables, True)
                sig_re[index] = re
                sig_im[index] = im
                tap_re, tap_im = spec_re[index], spec_im[index]
                y = from_points(re * tap_re - im * tap_im, re * tap_im + im * tap_re, tables)
                parts.append(y + skip[index][None] * x)
            chan_out[g, :, at, :] = jnp.concatenate(parts, axis=1).astype(bf16)

        @pl.loop(1, ns)
        def _(step):
            to_tok(g, step).start()

        for q in range(quarters):
            tok_in[place.s, g, q] = chan_out[g, place.s * quarters + q]

    for g in range(groups):

        @pl.loop(1, ns)
        def _(step):
            to_tok(g, step).wait_recv()

        @pl.loop(0, ns)
        def _(owner):
            block = owner * groups + g
            value = jnp.concatenate([tok_in[owner, g, q] for q in range(quarters)], axis=1)
            long_out[block] = value
            gated[block] = (short_out(mixed, aux, 0, block) * value.astype(f32)).astype(bf16)

    for g in range(groups):

        @pl.loop(1, ns)
        def _(step):
            to_chan(g, step).wait_send()
            to_tok(g, step).wait_send()


def whole(count):
    return [pl.BlockSpec(memory_space=pltpu.VMEM)] * count


def mix(mixed, aux, spec, skip, tables, collective_id):
    ns = lax.axis_size("seq")
    _, nblocks, chans, toks = mixed.shape
    groups, quarters = nblocks // ns, toks // LANES
    n1 = ns * quarters
    rows = (groups * chans // 8, n1 * 8, LANES)
    pieces = (ns, groups, quarters, chans, LANES)
    lines = (groups, n1, chans, LANES)
    return pl.pallas_call(
        functools.partial(mix_kernel, ns, groups),
        out_shape=[
            jax.ShapeDtypeStruct((nblocks, chans, toks), bf16),
            jax.ShapeDtypeStruct((nblocks, chans, toks), bf16),
            jax.ShapeDtypeStruct(rows, f32),
            jax.ShapeDtypeStruct(rows, f32),
        ],
        in_specs=whole(15),
        out_specs=whole(4),
        scratch_shapes=[
            pltpu.VMEM(pieces, bf16),
            pltpu.VMEM(lines, bf16),
            pltpu.VMEM(lines, bf16),
            pltpu.VMEM(pieces, bf16),
            pltpu.SemaphoreType.DMA((2, groups, ns)),
            pltpu.SemaphoreType.DMA((2, groups, ns)),
        ],
        compiler_params=pltpu.CompilerParams(
            collective_id=collective_id, has_side_effects=True, vmem_limit_bytes=VMEM_LIMIT
        ),
        name="mix",
    )(mixed, aux, spec[0], spec[1], skip, *tables)


def unmix_kernel(ns, groups, mixed, aux, long_out, grad_gated, spec_re, spec_im, sig_re, sig_im, skip, *refs):
    tables = refs[:10]
    grad_taps, grad_short, grad_conv = refs[10:13]
    pull, chan_in, chan_out, tok_in, send, recv = refs[13:]
    place = Place(ns)
    quarters = pull.shape[2]
    chans = pull.shape[3]
    take = sub_rows(chans)
    greet(place, True)

    def to_chan(g, step):
        peer = lax.rem(place.s + step, ns)
        return remote(
            pull.at[peer, g],
            chan_in.at[g, pl.ds(place.s * quarters, quarters)],
            send.at[0, g, step],
            recv.at[0, g, step],
            (place.b, peer),
        )

    def to_tok(g, step):
        peer = lax.rem(place.s + step, ns)
        return remote(
            chan_out.at[g, pl.ds(peer * quarters, quarters)],
            tok_in.at[place.s, g],
            send.at[1, g, step],
            recv.at[1, g, step],
            (place.b, peer),
        )

    for g in range(groups):

        @pl.loop(1, ns + 1)
        def _(step):
            peer = lax.rem(place.s + step, ns)
            block = peer * groups + g
            value = (grad_gated[block] * short_out(mixed, aux, 0, block)).astype(bf16)

            @pl.when(step < ns)
            def _():
                for q in range(quarters):
                    pull[peer, g, q] = value[:, q * LANES : (q + 1) * LANES]
                to_chan(g, step).start()

            @pl.when(step == ns)
            def _():
                for q in range(quarters):
                    chan_in[g, place.s * quarters + q] = value[:, q * LANES : (q + 1) * LANES]

    for g in range(groups):

        @pl.loop(1, ns)
        def _(step):
            to_chan(g, step).wait_recv()

        @pl.loop(0, chans // take)
        def _(i):
            at = pl.ds(pl.multiple_of(i * take, take), take)
            block = chan_in[g, :, at, :].astype(f32)
            parts = []
            for j in range(take // 8):
                index = (g * chans) // 8 + i * (take // 8) + j
                x = block[:, 8 * j : 8 * j + 8, :]
                re, im = to_points(x, tables, True)
                tap_re, tap_im = spec_re[index], spec_im[index]
                y = from_points(tap_re * re + tap_im * im, tap_re * im - tap_im * re, tables)
                parts.append(y + skip[index][None] * x)
                own_re, own_im = sig_re[index], sig_im[index]
                grad_taps[index] = from_points(
                    own_re * re + own_im * im, own_re * im - own_im * re, tables
                )
            chan_out[g, :, at, :] = jnp.concatenate(parts, axis=1).astype(bf16)

        @pl.loop(1, ns)
        def _(step):
            to_tok(g, step).start()

        for q in range(quarters):
            tok_in[place.s, g, q] = chan_out[g, place.s * quarters + q]

    def backward(stream, block, grad):
        grad_short[stream, block] = grad
        value = mixed[stream, block].astype(f32)
        side = aux[stream, block]
        near, far = conv_lanes(value, side[:, 3:4], side[:, 4:5])
        sums = [jnp.sum(grad * v, axis=1, keepdims=True) for v in (far, near, value)]
        lane = lax.broadcasted_iota(jnp.int32, side.shape, 1)
        grad_conv[stream, block] = jnp.where(
            lane == 0, sums[0], jnp.where(lane == 1, sums[1], jnp.where(lane == 2, sums[2], 0.0))
        )

    @pl.loop(0, ns * groups)
    def _(block):
        backward(0, block, grad_gated[block] * long_out[block].astype(f32))

    for g in range(groups):

        @pl.loop(1, ns)
        def _(step):
            to_tok(g, step).wait_recv()

        @pl.loop(0, ns)
        def _(owner):
            block = owner * groups + g
            value = jnp.concatenate(
                [tok_in[owner, g, q] for q in range(quarters)], axis=1
            ).astype(f32)
            backward(1, block, value * short_out(mixed, aux, 2, block))
            backward(2, block, value * short_out(mixed, aux, 1, block))

    for g in range(groups):

        @pl.loop(1, ns)
        def _(step):
            to_chan(g, step).wait_send()
            to_tok(g, step).wait_send()


def unmix(mixed, aux, long_out, grad_gated, spec, sig, skip, tables, collective_id):
    ns = lax.axis_size("seq")
    _, nblocks, chans, toks = mixed.shape
    groups, quarters = nblocks // ns, toks // LANES
    n1 = ns * quarters
    pieces = (ns, groups, quarters, chans, LANES)
    lines = (groups, n1, chans, LANES)
    return pl.pallas_call(
        functools.partial(unmix_kernel, ns, groups),
        out_shape=[
            jax.ShapeDtypeStruct((groups * chans // 8, n1, 8, LANES), f32),
            jax.ShapeDtypeStruct(mixed.shape, f32),
            jax.ShapeDtypeStruct(aux.shape, f32),
        ],
        in_specs=whole(19),
        out_specs=whole(3),
        scratch_shapes=[
            pltpu.VMEM(pieces, bf16),
            pltpu.VMEM(lines, bf16),
            pltpu.VMEM(lines, bf16),
            pltpu.VMEM(pieces, bf16),
            pltpu.SemaphoreType.DMA((2, groups, ns)),
            pltpu.SemaphoreType.DMA((2, groups, ns)),
        ],
        compiler_params=pltpu.CompilerParams(
            collective_id=collective_id, has_side_effects=True, vmem_limit_bytes=VMEM_LIMIT
        ),
        name="unmix",
    )(mixed, aux, long_out, grad_gated, spec[0], spec[1], sig[0], sig[1], skip, *tables)


def short_back_kernel(grad_short, aux, grad_mixed):
    toks = grad_short.shape[3]

    @pl.loop(0, grad_short.shape[1])
    def _(block):
        value = grad_short[0, block]
        side = aux[0, block]
        lane = lax.broadcasted_iota(jnp.int32, value.shape, 1)
        near = jnp.where(lane == toks - 1, side[:, 3:4], pltpu.roll(value, toks - 1, 1))
        far = jnp.where(
            lane == toks - 1,
            side[:, 4:5],
            jnp.where(lane == toks - 2, side[:, 3:4], pltpu.roll(value, toks - 2, 1)),
        )
        grad_mixed[0, block] = (
            side[:, 2:3] * value + side[:, 1:2] * near + side[:, 0:1] * far
        ).astype(bf16)


def short_back(grad_short, aux):
    streams, nblocks, chans, toks = grad_short.shape
    at = lambda k: (k, 0, 0, 0)
    return pl.pallas_call(
        short_back_kernel,
        grid=(streams,),
        out_shape=jax.ShapeDtypeStruct(grad_short.shape, bf16),
        in_specs=[
            pl.BlockSpec((1, nblocks, chans, toks), at),
            pl.BlockSpec((1, nblocks, chans, LANES), at),
        ],
        out_specs=pl.BlockSpec((1, nblocks, chans, toks), at),
        compiler_params=pltpu.CompilerParams(vmem_limit_bytes=VMEM_LIMIT),
        name="short_back",
    )(grad_short, aux)


def tap_points_kernel(taps, *refs):
    tables, (out_re, out_im) = refs[:10], refs[10:]
    n1, rows = out_re.shape[1] // 8, 8
    value = taps[...]
    x = jnp.concatenate(
        [value[:, i * LANES : (i + 1) * LANES][None] for i in range(n1)], axis=0
    )
    re, im = to_points(x, tables, False)
    out_re[0] = re
    out_im[0] = im


def tap_points(taps, tables):
    chans, length = taps.shape
    rows = length // LANES * 8
    full = lambda t: pl.BlockSpec(t.shape, lambda i: (0, 0))
    out = jax.ShapeDtypeStruct((chans // 8, rows, LANES), f32)
    return pl.pallas_call(
        tap_points_kernel,
        grid=(chans // 8,),
        out_shape=[out, out],
        in_specs=[pl.BlockSpec((8, length), lambda i: (i, 0))] + [full(t) for t in tables],
        out_specs=[pl.BlockSpec((1, rows, LANES), lambda i: (i, 0, 0))] * 2,
        compiler_params=pltpu.CompilerParams(vmem_limit_bytes=VMEM_LIMIT),
        name="tap_points",
    )(taps, *tables)


def side_table(conv, near, far):
    columns = jnp.concatenate([conv.T, near, far], axis=1)
    return jnp.pad(columns, ((0, 0), (0, LANES - 5)))


def on_device(
    tokens,
    cotangent,
    norm_gains,
    w_in,
    short_conv,
    w_out,
    w_fc,
    w_proj,
    filt_w1,
    filt_b1,
    filt_w2,
    filt_b2,
    filt_w3,
    skip_gain,
    decay_rate,
):
    layers, _, width3 = w_in.shape
    width = width3 // 3
    ns = lax.axis_size("seq")
    devices = lax.axis_size("batch") * ns
    stream = tokens[0].astype(f32)
    toks = stream.shape[0]
    length = toks * ns
    n1 = length // LANES
    own_chans = width // ns
    chans = 32 if own_chans % 32 == 0 else own_chans
    groups = own_chans // chans
    nblocks = ns * groups
    blocked = (3, nblocks, chans)
    tables = transform_tables(n1)
    pos_rows = position_rows(length, filt_w1.shape[1])

    gain_cols, conv_cols = norm_gains.shape[2], short_conv.shape[2]
    small = jnp.concatenate(
        [
            jnp.pad(norm_gains.reshape(2 * layers, gain_cols).astype(f32), ((0, 0), (0, LANES - gain_cols))),
            jnp.pad(short_conv.reshape(3 * layers, conv_cols).astype(f32), ((0, 0), (0, LANES - conv_cols))),
        ],
        axis=0,
    )
    small = jnp.pad(small, ((0, -small.shape[0] % 8), (0, 0)))[None]

    arrays, picks = [small], [0]
    for layer in range(layers):
        arrays += [w_in, w_out, w_fc, w_proj]
        picks += [layer] * 4
    gathered = gather(arrays, tuple(picks), 0)
    small_all = gathered[0]
    gains = jnp.swapaxes(small_all[:, : 2 * layers, :gain_cols], 0, 1).reshape(layers, 2, width)
    convs = jnp.swapaxes(
        small_all[:, 2 * layers : 5 * layers, :conv_cols], 0, 1
    ).reshape(layers, 3, width3)
    weights = []
    for layer in range(layers):
        in_mat, out_mat, fc_mat, proj_mat = gathered[1 + 4 * layer : 5 + 4 * layer]
        weights.append(
            (
                in_mat.reshape(width, width3),
                out_mat.reshape(width, width),
                fc_mat.reshape(width, -1),
                proj_mat.reshape(-1, width),
            )
        )

    make_taps = []
    specs = []
    skips = []
    for layer in range(layers):
        parts = (
            filt_w1[layer],
            filt_b1[layer],
            filt_w2[layer],
            filt_b2[layer],
            filt_w3[layer],
        )
        run = lambda *p, layer=layer: filter_forward(pos_rows, *p, decay_rate[layer])
        taps, pull = jax.vjp(run, *parts)
        make_taps.append(pull)
        specs.append(tap_points(taps, tables))
        skips.append(
            jnp.broadcast_to(skip_gain[layer].reshape(-1, 8, 1), (own_chans // 8, 8, LANES))
        )

    saved = []
    for layer in range(layers):
        in_mat, out_mat, fc_mat, proj_mat = weights[layer]
        normed, inv_std = layer_norm_parts(stream)
        norm_in = (normed * gains[layer, 0]).astype(bf16)
        mixed = contract(in_mat, norm_in, 0, 1).astype(bf16)
        rim = shifted(mixed[:, -2:], "seq", 1).astype(f32)
        aux = side_table(convs[layer], rim[:, 1:2], rim[:, 0:1]).reshape(blocked + (LANES,))
        mixed = mixed.reshape(blocked + (toks,))
        long_out, gated, sig_re, sig_im = mix(
            mixed, aux, specs[layer], skips[layer], tables, 1 + layer
        )
        gated = gated.reshape(width, toks)
        middle = stream + contract(gated, out_mat, 0, 0)
        normed_mid, inv_mid = layer_norm_parts(middle)
        hidden_in = (normed_mid * gains[layer, 1]).astype(bf16)
        hidden_pre = product(hidden_in, fc_mat)
        hidden_act = jax.nn.gelu(hidden_pre).astype(bf16)
        saved.append(
            (normed, inv_std, norm_in, mixed, aux, long_out, gated, (sig_re, sig_im))
            + (normed_mid, inv_mid, hidden_in, hidden_pre, hidden_act)
        )
        stream = middle + product(hidden_act, proj_mat)
    mixed_out = stream.astype(bf16)

    grad = cotangent[0].astype(f32)
    block_grads = [None] * layers
    small_grads = [None] * layers
    for layer in reversed(range(layers)):
        in_mat, out_mat, fc_mat, proj_mat = weights[layer]
        (normed, inv_std, norm_in, mixed, aux, long_out, gated, sig) = saved[layer][:8]
        (normed_mid, inv_mid, hidden_in, hidden_pre, hidden_act) = saved[layer][8:]
        grad_top = grad.astype(bf16)
        grad_act = contract(grad_top, proj_mat, 1, 1)
        grad_proj = contract(hidden_act, grad_top, 0, 0).astype(bf16)
        grad_pre = jax.vjp(jax.nn.gelu, hidden_pre)[1](grad_act)[0].astype(bf16)
        grad_hidden = contract(grad_pre, fc_mat, 1, 1)
        grad_fc = contract(hidden_in, grad_pre, 0, 0).astype(bf16)
        grad_gain_mid = jnp.sum(grad_hidden * normed_mid, axis=0)
        grad_middle = grad + norm_back(grad_hidden * gains[layer, 1], normed_mid, inv_mid)
        grad_mix = grad_middle.astype(bf16)
        grad_gated = contract(out_mat, grad_mix, 1, 1).reshape(nblocks, chans, toks)
        grad_out = contract(gated, grad_mix, 1, 0).astype(bf16)
        grad_taps, grad_short, grad_conv = unmix(
            mixed, aux, long_out, grad_gated, specs[layer], sig, skips[layer], tables, 3 + layer
        )
        rim = shifted(grad_short[..., :2], "seq", -1)
        back_aux = side_table(
            convs[layer], rim[..., 0].reshape(-1, 1), rim[..., 1].reshape(-1, 1)
        ).reshape(blocked + (LANES,))
        grad_mixed = short_back(grad_short, back_aux).reshape(width3, toks)
        grad_norm_in = contract(grad_mixed, in_mat, 0, 1)
        grad_in = contract(norm_in, grad_mixed, 0, 1).astype(bf16)
        grad_gain_in = jnp.sum(grad_norm_in * normed, axis=0)
        grad = grad_middle + norm_back(grad_norm_in * gains[layer, 0], normed, inv_std)
        block_grads[layer] = [
            g.reshape(devices, -1, g.shape[1]) for g in (grad_in, grad_out, grad_fc, grad_proj)
        ]
        taps_rows = jnp.swapaxes(grad_taps, 1, 2).reshape(own_chans, length)
        filter_grads = make_taps[layer](taps_rows)
        small_grads[layer] = (
            jnp.stack([grad_gain_in, grad_gain_mid]),
            jnp.swapaxes(grad_conv.reshape(width3, LANES)[:, :3], 0, 1),
            filter_grads,
            taps_rows[:, 0],
        )

    def rows_for(values, cols):
        pieces = jnp.swapaxes(values.reshape(values.shape[0], devices, cols), 0, 1)
        return jnp.pad(pieces, ((0, 0), (0, 0), (0, LANES - cols)))

    small_rows = jnp.concatenate(
        [rows_for(small_grads[layer][0], gain_cols) for layer in range(layers)]
        + [rows_for(small_grads[layer][1], conv_cols) for layer in range(layers)],
        axis=1,
    )
    small_rows = jnp.pad(small_rows, ((0, 0), (0, -small_rows.shape[1] % 8), (0, 0)))
    hidden = filt_w2.shape[1]
    emb = filt_w1.shape[1]
    payload = []
    for layer in range(layers):
        grad_w3, grad_skip = small_grads[layer][2][4], small_grads[layer][3]
        part = jnp.concatenate([grad_w3, grad_skip[None]], axis=0)
        payload.append(jnp.pad(part, ((0, 7), (0, LANES - own_chans))))
    for layer in range(layers):
        first_w, first_b, second_w, second_b = small_grads[layer][2][:4]
        part = jnp.concatenate([first_w, first_b[None], second_b[None]], axis=0)
        part = jnp.pad(part, ((0, hidden - part.shape[0]), (0, 0)))
        payload.append(jnp.concatenate([part, second_w], axis=1))
    payload = jnp.concatenate(payload, axis=0)

    summed = [None] * layers
    for layer in reversed(range(1, layers)):
        summed[layer] = reduce_scatter(block_grads[layer], 5 + layer)
    last, totals = last_reduce(block_grads[0] + [small_rows], payload, layers * hidden, 5)
    summed[0], small_sum = last[:-1], last[-1]
    columns = totals[: layers * (hidden + 8)].reshape(layers, hidden + 8, LANES)
    shared = totals[layers * (hidden + 8) :].reshape(layers, hidden, LANES)
    block = [jnp.stack([summed[layer][i] for layer in range(layers)]) for i in range(4)]
    gains_grad = small_sum[: 2 * layers, :gain_cols].reshape(layers, 2, gain_cols)
    conv_grad = small_sum[2 * layers : 5 * layers, :conv_cols].reshape(layers, 3, conv_cols)
    return (
        mixed_out[None],
        grad[None],
        gains_grad,
        block[0],
        conv_grad,
        block[1],
        block[2],
        block[3],
        shared[:, :emb, :hidden],
        shared[:, emb, :hidden],
        shared[:, :, hidden:],
        shared[:, emb + 1, :hidden],
        columns[:, :hidden, :own_chans],
        columns[:, hidden, :own_chans],
    )


def solution(mesh):
    both = ("batch", "seq")
    in_specs = (
        P("batch", "seq", None),
        P("batch", "seq", None),
        P(None, None, both),
        P(None, both, None),
        P(None, None, both),
        P(None, both, None),
        P(None, both, None),
        P(None, both, None),
        P(),
        P(),
        P(),
        P(),
        P(None, None, "seq"),
        P(None, "seq"),
        P(None, "seq"),
    )
    out_specs = in_specs[:14]
    return jax.shard_map(
        on_device, mesh=mesh, in_specs=in_specs, out_specs=out_specs, check_vma=False
    )
```

```python
import functools
import itertools
import math

import jax
import jax.numpy as jnp
import numpy as np
from jax import lax
from jax.experimental import pallas as pl
from jax.experimental.pallas import tpu as pltpu
from jax.sharding import PartitionSpec as P

MESH = pl.DeviceIdType.MESH
LANES = 128
VMEM_LIMIT = 58 * 1024 * 1024
GATHER_PLANS = [[0, 1, 3, 5, 7, 9, 12], [0, 1, 3, 5, 7, 9, 12], [0, 2, 4, 6, 8, 10, 12], [0, 2, 5, 8, 10, 12, 14], [0, 3, 6, 9, 12, 14, 16]]
COLUMN_PLANS = [[2, 5, 8, 11, 14], [2, 5, 8, 11, 14], [3, 7, 10, 13, 15], [4, 8, 12, 14, 16]]
PLANE_PLANS = [[0, 3, 5, 7], [0, 4, 6, 8], [2, 6, 8, 10]]
REDUCE_PLANS = [[0, 1, 2, 4, 5, 7, 8, 12], [0, 3, 4, 6, 7, 9, 10, 12], [0, 5, 6, 8, 9, 11, 12, 13]]
LAST_PLANS = [[0, 1, 1, 2, 2, 3, 3, 5], [0, 1, 1, 3, 3, 5, 5, 7], [0, 2, 2, 4, 5, 7, 8, 9]]
f32 = jnp.float32
bf16 = jnp.bfloat16


def product(left_mat, right_mat):
    return jnp.dot(left_mat, right_mat, preferred_element_type=f32)


def contract(left_mat, right_mat, left_dim, right_dim):
    return lax.dot_general(
        left_mat, right_mat, (((left_dim,), (right_dim,)), ((), ())), preferred_element_type=f32
    )


def layer_norm_parts(stream):
    mean_val = jnp.mean(stream, axis=-1, keepdims=True)
    centered = stream - mean_val
    inv_std = lax.rsqrt(jnp.mean(centered * centered, axis=-1, keepdims=True) + 1e-05)
    return (centered * inv_std, inv_std)


def norm_back(grad_normed, normed, inv_std):
    mean_grad = jnp.mean(grad_normed, axis=-1, keepdims=True)
    mean_cross = jnp.mean(grad_normed * normed, axis=-1, keepdims=True)
    return inv_std * (grad_normed - mean_grad - normed * mean_cross)


def split_bf16(table):
    high = table.astype(np.float32).astype(jnp.bfloat16)
    return high, (table - high.astype(np.float64)).astype(np.float32).astype(jnp.bfloat16)


def transform_tables(length):
    blocks = min(length // LANES, 32)
    inside = length // blocks
    n1 = np.arange(blocks)
    n2 = np.arange(inside)
    outer = 2 * np.pi * ((n1[:, None] * (4 * n1[None, :] + 1)) % (4 * blocks)) / (4 * blocks)
    eye = np.eye(8)
    forward = np.concatenate([np.cos(outer).T, -np.sin(outer).T], axis=0)
    left_fwd = np.kron(forward, eye)
    left_inv = np.kron(np.concatenate([np.cos(outer), -np.sin(outer)], axis=1), eye) / length
    inner = 2 * np.pi * ((n2[:, None] * n2[None, :]) % inside) / inside
    cos2, sin2 = np.cos(inner), np.sin(inner)
    right_fwd = np.block([[cos2, -sin2], [sin2, cos2]])
    right_inv = np.block([[cos2, sin2], [-sin2, cos2]])
    twist = 2 * np.pi * (n2[None, :] * (4 * n1[:, None] + 1)) / (4 * length)
    twist_cos = np.repeat(np.cos(twist), 8, axis=0).astype(np.float32)
    twist_sin = np.repeat(np.sin(twist), 8, axis=0).astype(np.float32)
    tables = []
    for table, axis in ((left_fwd, 1), (right_fwd, 0), (left_inv, 1), (right_inv, 0)):
        high, low = split_bf16(table)
        tables.append(jnp.asarray(np.concatenate([high, low, high], axis=axis)))
    return tuple(tables) + (jnp.asarray(twist_cos), jnp.asarray(twist_sin))


TABLES = 6


def in_two(value):
    high = value.astype(bf16)
    return high, (value - high.astype(f32)).astype(bf16)


def left_product(left, right):
    high, low = in_two(right)
    return product(left[...], jnp.concatenate([high, high, low], axis=0))


def right_product(left, right):
    high, low = in_two(left)
    return product(jnp.concatenate([high, high, low], axis=1), right[...])


def to_points(x, tables, exact):
    left, right, _, _, twist_cos, twist_sin = tables
    rows, inside = twist_cos.shape
    split = x.reshape(rows // 8, inside // LANES, 8, LANES)
    flat = jnp.concatenate([split[:, k] for k in range(inside // LANES)], axis=2).reshape(rows, inside)
    if exact:
        flat = flat.astype(bf16)
        turned = product(left[:, : 2 * rows], jnp.concatenate([flat, flat], axis=0))
    else:
        turned = left_product(left, flat)
    re, im = turned[:rows], turned[rows:]
    cos, sin = twist_cos[...], twist_sin[...]
    both = jnp.concatenate([re * cos + im * sin, im * cos - re * sin], axis=1)
    points = right_product(both, right)
    return points[:, :inside], points[:, inside:]


def from_points(re, im, tables):
    _, _, left, right, twist_cos, twist_sin = tables
    rows, inside = twist_cos.shape
    back = right_product(jnp.concatenate([re, im], axis=1), right)
    re, im = back[:, :inside], back[:, inside:]
    cos, sin = twist_cos[...], twist_sin[...]
    both = jnp.concatenate([re * cos - im * sin, re * sin + im * cos], axis=0)
    flat = left_product(left, both).reshape(rows // 8, 8, inside)
    split = [flat[:, None, :, k * LANES : (k + 1) * LANES] for k in range(inside // LANES)]
    return jnp.concatenate(split, axis=1).reshape(-1, 8, LANES)


FEATURES = 48
SPAN = 512


def position_rows(length, emb_width):
    positions = np.arange(length, dtype=np.int64)
    bands = np.arange(1, (emb_width - 1) // 2 + 1, dtype=np.int64)
    angles = 2.0 * np.pi / length * ((bands[:, None] * positions[None, :]) % length)
    table = np.zeros((FEATURES, length), np.float32)
    table[0] = positions / length
    table[1 : 1 + bands.size] = np.cos(angles)
    table[1 + bands.size : emb_width] = np.sin(angles)
    table[emb_width] = 1.0
    return jnp.asarray(table)


def near_dot(left, right, left_dim, right_dim):
    left_high, left_low = in_two(left)
    right_high, right_low = in_two(right)
    return contract(
        jnp.concatenate([left_high, left_high, left_low], axis=left_dim),
        jnp.concatenate([right_high, right_low, right_high], axis=right_dim),
        left_dim,
        right_dim,
    )


def in_three(value):
    high = value.astype(bf16)
    rest = value - high.astype(f32)
    middle = rest.astype(bf16)
    return high, middle, (rest - middle.astype(f32)).astype(bf16)


def full_dot(left, right):
    a, b, c = in_three(left)
    d, e, f = in_three(right)
    return contract(
        jnp.concatenate([a, a, a, b, b, c], axis=0), jnp.concatenate([d, e, f, d, e, d], axis=0), 0, 0
    )


def sin_cos(x):
    turns = jnp.round(x * (2.0 / math.pi))
    r = ((x - turns * 1.5703125) - turns * 4.837512969970703125e-4) - turns * 7.54978995489188216e-8
    z = r * r
    sine = r + r * z * (-1.6666654611e-1 + z * (8.3321608736e-3 - z * 1.9515295891e-4))
    cosine = 1.0 - 0.5 * z + z * z * (
        4.166664568298827e-2 + z * (-1.388731625493765e-3 + z * 2.443315711809948e-5)
    )
    turn = lax.bitwise_and(turns.astype(jnp.int32), 3)
    odd = lax.bitwise_and(turn, 1) == 1
    first = jnp.where(odd, cosine, sine)
    second = jnp.where(odd, sine, cosine)
    return (
        jnp.where(turn >= 2, -first, first),
        jnp.where(jnp.logical_or(turn == 1, turn == 2), -second, second),
    )


def window_of(decay, start, shape, length):
    lane = lax.broadcasted_iota(jnp.int32, shape, 1) + start
    return jnp.exp(lane.astype(f32) * (-1.0 / length) * decay)


def filter_span(layer, start, pos, first_w, second_w, third_w, cols, decay, acts, shaped, squares):
    length = pos.shape[1]
    at = pl.ds(start, SPAN)
    act, slope = sin_cos(full_dot(first_w[layer], pos[:, at]))
    acts[layer, 0, :, at] = act
    acts[layer, 1, :, at] = slope
    act, slope = sin_cos(full_dot(second_w[layer], act) + cols[layer][:, :1])
    acts[layer, 2, :, at] = act
    acts[layer, 3, :, at] = slope
    raw = near_dot(third_w[layer], act, 0, 0)
    value = raw * window_of(decay[layer][:, :1], start, raw.shape, length)
    shaped[layer, :, at] = value
    squares[layer] += jnp.sum(value * value, axis=1, keepdims=True)


def filter_points(layer, group, tables, shaped, squares, spec_re, spec_im):
    length = shaped.shape[2]
    rows = pl.ds(pl.multiple_of(group * 8, 8), 8)
    scale = lax.rsqrt(squares[layer, rows, :1] * (1.0 / length) + 1e-05) * length ** (-0.5)
    value = shaped[layer, rows, :] * scale
    x = jnp.concatenate(
        [value[:, i * LANES : (i + 1) * LANES][None] for i in range(length // LANES)], axis=0
    )
    re, im = to_points(x, tables, False)
    spec_re[group] = re
    spec_im[group] = im


def filter_back_dot(layer, start, shaped, grad_taps, dots):
    at = pl.ds(start, SPAN)
    grad = taps_span(grad_taps, start)
    dots[layer] += jnp.sum(shaped[layer, :, at] * grad, axis=1, keepdims=True)


def taps_span(grad_taps, start):
    first = lax.div(start, LANES)
    pieces = []
    for i in range(SPAN // LANES):
        piece = grad_taps[:, first + i]
        pieces.append(piece.reshape(-1, LANES))
    return jnp.concatenate(pieces, axis=1)


def filter_back_span(
    layer, start, pos, second_w, third_w, decay, acts, shaped, squares, grad_taps, dots, grads
):
    length = pos.shape[1]
    at = pl.ds(start, SPAN)
    grad_third, grad_second, grad_first = grads
    mean_square = squares[layer][:, :1] * (1.0 / length)
    scale = lax.rsqrt(mean_square + 1e-05)
    cross = dots[layer][:, :1] * (1.0 / length) * scale * scale
    grad = taps_span(grad_taps, start)
    value = shaped[layer, :, at]
    grad = (grad - value * cross) * (scale * length ** (-0.5))
    grad = grad * window_of(decay[layer][:, :1], start, grad.shape, length)
    grad_third[layer] += near_dot(acts[layer, 2, :, at], grad, 1, 1)
    second = near_dot(third_w[layer], grad, 1, 0) * acts[layer, 3, :, at]
    grad_second[layer] += near_dot(acts[layer, 0, :, at], second, 1, 1)
    first = near_dot(second_w[layer], second, 1, 0) * acts[layer, 1, :, at]
    grad_first[layer] += near_dot(pos[:, at], jnp.concatenate([first, second], axis=0), 1, 1)


class Place:
    def __init__(self, ns):
        self.nz = ns // 2
        self.b = lax.axis_index("batch")
        self.s = lax.axis_index("seq")
        self.z = lax.div(self.s, 2)
        self.c = lax.rem(self.s, 2)
        self.x_peer = (lax.bitwise_xor(self.b, 1), self.s)
        self.y_peer = (lax.bitwise_xor(self.b, 2), self.s)
        self.core_peer = (self.b, lax.bitwise_xor(self.s, 1))
        self.up_peer = (self.b, lax.min(self.s + 2, ns - 1))
        self.down_peer = (self.b, lax.max(self.s - 2, 0))


def remote(src, dst, send, recv, peer):
    return pltpu.make_async_remote_copy(
        src_ref=src, dst_ref=dst, send_sem=send, recv_sem=recv, device_id=peer, device_id_type=MESH
    )


def greet(place, seq_peers):
    bar = pltpu.get_barrier_semaphore()

    def hello(peer):
        pl.semaphore_signal(bar, inc=1, device_id=peer, device_id_type=MESH)

    hello(place.x_peer)
    hello(place.y_peer)
    if seq_peers:
        ns = 2 * place.nz
        for step in range(1, ns):
            hello((place.b, lax.rem(place.s + step, ns)))
        pl.semaphore_wait(bar, 2 + ns - 1)
    else:
        hello(place.core_peer)
        pl.when(place.z + 1 < place.nz)(lambda: hello(place.up_peer))
        pl.when(place.z > 0)(lambda: hello(place.down_peer))
        ends = jnp.where(place.z == 0, 1, 0) + jnp.where(place.z == place.nz - 1, 1, 0)
        pl.semaphore_wait(bar, 5 - ends)


class Job:
    def __init__(self, arrays, results, scratch, task, plan):
        self.arrays, self.results, self.scratch, self.task = arrays, results, scratch, task
        self.plan = plan


class Runner:
    def __init__(self, tasks, plans):
        self.tasks = [[task, list(plan)] for task, plan in zip(tasks, plans, strict=True)]
        self.now = 0

    def add(self, task):
        self.tasks.insert(0, [task, []])

    def step(self, entry):
        if next(entry[0], "end") == "end":
            self.tasks.remove(entry)

    def phase(self):
        for entry in list(self.tasks):
            while entry[1] and entry[1][0] <= self.now:
                entry[1].pop(0)
                self.step(entry)
        self.now += 1

    def finish(self):
        while any(entry[1] for entry in self.tasks):
            self.phase()
        while self.tasks:
            for entry in list(self.tasks):
                self.step(entry)


def room(items):
    total = 0
    for item in items:
        if len(item.shape) < 2 or not jnp.issubdtype(item.dtype, jnp.floating):
            continue
        size = jnp.dtype(item.dtype).itemsize
        *outer, rows, lanes = item.shape
        tile = 32 // size
        total += math.prod(outer) * -(-rows // tile) * tile * -(-lanes // LANES) * LANES * size
    return total


def fused_call(name, body, arrays, results, scratch, jobs, seq_peers, ids):
    free = VMEM_LIMIT - room([*arrays, *results, *scratch])
    if body is not None and room([item for job in jobs for item in job.scratch]) > free:
        found, _ = fused_call(name, body, arrays, results, scratch, [], seq_peers, ids)
        alone = [fused_call(name + "_job", None, [], [], [], [job], seq_peers, ids)[1][0] for job in jobs]
        return found, alone
    collective_id = next(ids)
    ns = lax.axis_size("seq")
    counts = [len(arrays)] + [len(j.arrays) for j in jobs]
    counts += [len(results)] + [len(j.results) for j in jobs]
    counts += [len(scratch)] + [len(j.scratch) for j in jobs]
    n = 1 + len(jobs)

    def kernel(*refs):
        parts, start = [], 0
        for count in counts:
            parts.append(refs[start : start + count])
            start += count
        place = Place(ns)
        greet(place, seq_peers)
        tasks = [
            job.task(place, *parts[1 + k], *parts[n + 1 + k], parts[2 * n + 1 + k])
            for k, job in enumerate(jobs)
        ]
        runner = Runner(tasks, [job.plan for job in jobs])
        if body is not None:
            body(place, runner, parts[0], parts[n], parts[2 * n])
        runner.finish()

    hbm = pl.BlockSpec(memory_space=pl.ANY)
    flat = lambda pick: [item for job in jobs for item in pick(job)]
    found = pl.pallas_call(
        kernel,
        out_shape=list(results) + flat(lambda j: j.results),
        in_specs=whole(counts[0]) + [hbm] * sum(counts[1:n]),
        out_specs=whole(counts[n]) + [hbm] * sum(counts[n + 1 : 2 * n]),
        scratch_shapes=list(scratch) + flat(lambda j: j.scratch),
        compiler_params=pltpu.CompilerParams(
            collective_id=collective_id, has_side_effects=True, vmem_limit_bytes=VMEM_LIMIT
        ),
        name=name,
    )(*arrays, *flat(lambda j: j.arrays))
    return found[: counts[n]], found[counts[n] :]


def whole(count):
    return [pl.BlockSpec(memory_space=pltpu.VMEM)] * count


def gather_sems(nz):
    return [
        pltpu.SemaphoreType.DMA((1,)),
        pltpu.SemaphoreType.DMA((2, nz)),
        pltpu.SemaphoreType.DMA((nz,)),
        pltpu.SemaphoreType.DMA((4, nz)),
        pltpu.SemaphoreType.DMA((4, nz)),
        pltpu.SemaphoreType.DMA((4,)),
        pltpu.SemaphoreType.DMA((4,)),
    ]


def gather_task(place, src, dst, sems):
    one, chain_send, chain_recv, send, recv, core_send, core_recv = sems
    b, z, c, nz = place.b, place.z, place.c, place.nz
    bx, by, bd = place.x_peer[0], place.y_peer[0], lax.bitwise_xor(b, 3)
    local = pltpu.make_async_copy(src, dst.at[b, z, c], one.at[0])

    def chain(source, shard, up):
        row = 0 if up else 1
        peer = place.up_peer if up else place.down_peer
        return remote(source, dst.at[b, shard, c], chain_send.at[row, shard], chain_recv.at[shard], peer)

    def across(source, shard, along):
        peer = place.y_peer if along else place.x_peer
        return remote(source, dst.at[b, shard, c], send.at[along, shard], recv.at[along, shard], peer)

    def onward(shard, along):
        peer = place.y_peer if along else place.x_peer
        part = dst.at[bx if along else by, shard, c]
        return remote(part, part, send.at[2 + along, shard], recv.at[2 + along, shard], peer)

    def core(batch, i):
        part = dst.at[batch, :, c]
        return remote(part, part, core_send.at[i], core_recv.at[i], place.core_peer)

    def pass_on(shard):
        across(src, shard, 0).wait_recv()
        across(src, shard, 1).wait_recv()
        even = lax.rem(shard, 2) == 0
        pl.when(even)(lambda: onward(shard, 1).start())
        pl.when(jnp.logical_not(even))(lambda: onward(shard, 0).start())

    def pass_on_from(hop):
        if hop == 0:
            pass_on(z)
        else:
            pl.when(z - hop >= 0)(lambda: pass_on(z - hop))
            pl.when(z + hop < nz)(lambda: pass_on(z + hop))

    local.start()
    pl.when(z + 1 < nz)(lambda: chain(src, z, True).start())
    pl.when(z > 0)(lambda: chain(src, z, False).start())
    across(src, z, 0).start()
    across(src, z, 1).start()
    yield
    for hop in range(1, nz):
        below, above = z - hop, z + hop

        @pl.when(below >= 0)
        def _():
            chain(src, below, True).wait_recv()
            part = dst.at[b, below, c]
            pl.when(z + 1 < nz)(lambda: chain(part, below, True).start())
            across(part, below, 0).start()
            across(part, below, 1).start()

        @pl.when(above < nz)
        def _():
            chain(src, above, False).wait_recv()
            part = dst.at[b, above, c]
            pl.when(z > 0)(lambda: chain(part, above, False).start())
            across(part, above, 0).start()
            across(part, above, 1).start()

        pass_on_from(hop - 1)
        yield
    local.wait()
    core(b, 0).start()
    pass_on_from(nz - 1)
    core(bx, 1).start()
    core(by, 2).start()
    yield
    for shard in range(nz):
        onward(shard, 1 - shard % 2).wait_recv()
    core(bd, 3).start()
    yield
    for hop in range(nz):
        pl.when(jnp.logical_and(z >= hop, z + 1 < nz))(lambda: chain(src, z - hop, True).wait_send())
        pl.when(jnp.logical_and(z + hop < nz, z > 0))(lambda: chain(src, z + hop, False).wait_send())
    for shard in range(nz):
        across(src, shard, 0).wait_send()
        across(src, shard, 1).wait_send()
        onward(shard, 1 - shard % 2).wait_send()
    for i in range(4):
        core(b, i).wait()
    yield


def gather_job(array, layer, plan):
    nz = lax.axis_size("seq") // 2
    result = jax.ShapeDtypeStruct((4, nz, 2) + array.shape[1:], array.dtype)
    task = lambda place, src, dst, sems: gather_task(place, src.at[layer], dst, sems)
    return Job([array], [result], gather_sems(nz), task, plan)


def column_task(place, src, dst, sems):
    one, chain_send, chain_recv = sems
    z, nz = place.z, place.nz
    local = pltpu.make_async_copy(src, dst.at[z], one.at[0])

    def chain(source, shard, up):
        row = 0 if up else 1
        peer = place.up_peer if up else place.down_peer
        return remote(source, dst.at[shard], chain_send.at[row, shard], chain_recv.at[shard], peer)

    local.start()
    pl.when(z + 1 < nz)(lambda: chain(src, z, True).start())
    pl.when(z > 0)(lambda: chain(src, z, False).start())
    yield
    for hop in range(1, nz):
        below, above = z - hop, z + hop

        @pl.when(below >= 0)
        def _():
            chain(src, below, True).wait_recv()
            pl.when(z + 1 < nz)(lambda: chain(dst.at[below], below, True).start())

        @pl.when(above < nz)
        def _():
            chain(src, above, False).wait_recv()
            pl.when(z > 0)(lambda: chain(dst.at[above], above, False).start())

        yield
    for hop in range(nz):
        pl.when(jnp.logical_and(z >= hop, z + 1 < nz))(lambda: chain(src, z - hop, True).wait_send())
        pl.when(jnp.logical_and(z + hop < nz, z > 0))(lambda: chain(src, z + hop, False).wait_send())
    local.wait()
    yield


def column_job(array, layer, plan):
    nz = lax.axis_size("seq") // 2
    result = jax.ShapeDtypeStruct((nz,) + array.shape[1:], array.dtype)
    sems = [
        pltpu.SemaphoreType.DMA((1,)),
        pltpu.SemaphoreType.DMA((2, nz)),
        pltpu.SemaphoreType.DMA((nz,)),
    ]
    task = lambda place, src, dst, sems: column_task(place, src.at[layer], dst, sems)
    return Job([array], [result], sems, task, plan)


def plane_task(place, src, dst, sems):
    one, send, recv, core_send, core_recv = sems
    b, c, nz = place.b, place.c, place.nz
    bx, by, bd = place.x_peer[0], place.y_peer[0], lax.bitwise_xor(b, 3)
    half = nz // 2
    local = pltpu.make_async_copy(src, dst.at[b, :, c], one.at[0])
    over_x = remote(src, dst.at[b, :, c], send.at[0], recv.at[0], place.x_peer)
    over_y = remote(src, dst.at[b, :, c], send.at[1], recv.at[1], place.y_peer)
    low, high = pl.ds(0, half), pl.ds(half, nz - half)
    far_y = remote(dst.at[bx, low, c], dst.at[bx, low, c], send.at[2], recv.at[2], place.y_peer)
    far_x = remote(dst.at[by, high, c], dst.at[by, high, c], send.at[3], recv.at[3], place.x_peer)

    def core(source, batch, i):
        return remote(source, dst.at[batch, :, c], core_send.at[i], core_recv.at[i], place.core_peer)

    over_x.start()
    over_y.start()
    core(src, b, 0).start()
    local.start()
    yield
    over_x.wait_recv()
    far_y.start()
    over_y.wait_recv()
    far_x.start()
    core(dst.at[bx, :, c], bx, 1).start()
    core(dst.at[by, :, c], by, 2).start()
    yield
    far_y.wait_recv()
    far_x.wait_recv()
    core(dst.at[bd, :, c], bd, 3).start()
    yield
    for copy in (over_x, over_y, far_y, far_x):
        copy.wait_send()
    local.wait()
    for i in range(4):
        core(src, b, i).wait()
    yield


def plane_job(array, plan):
    nz = array.shape[0]
    result = jax.ShapeDtypeStruct((4, nz, 2) + array.shape[1:], array.dtype)
    sems = [pltpu.SemaphoreType.DMA((1,))] + [pltpu.SemaphoreType.DMA((4,))] * 4
    return Job([array], [result], sems, plane_task, plan)


def reduce_scratch(nz, shape, dtype):
    half = (nz,) + shape
    return [
        pltpu.VMEM((4,) + half, dtype),
        pltpu.VMEM((4,) + half, dtype),
        pltpu.VMEM((5,) + half, dtype),
        pltpu.VMEM(shape, f32),
        pltpu.SemaphoreType.DMA((1,)),
        pltpu.SemaphoreType.DMA((3, nz)),
        pltpu.SemaphoreType.DMA((5, nz)),
        pltpu.SemaphoreType.DMA((5, nz)),
    ]


def far_first(place):
    nz = place.nz
    tables = [sorted(range(nz), key=lambda k: (-abs(k - z), k)) for z in range(nz)]
    order = []
    for j in range(nz):
        shard = jnp.int32(tables[0][j])
        for z in range(1, nz):
            shard = jnp.where(place.z == z, tables[z][j], shard)
        order.append(shard)
    return order


def reduce_task(place, src, out, scratch):
    acc, other, box, total, one, near, send, recv = scratch
    kind = acc.dtype
    b, z, c, nz = place.b, place.z, place.c, place.nz
    bx, by, bd = place.x_peer[0], place.y_peer[0], lax.bitwise_xor(b, 3)
    far, via_x, via_y, up, down = range(5)
    order = far_first(place)
    halves = [range(0, nz // 2), range(nz // 2, nz)]

    def add(target, shard, *lanes):
        value = acc[target, shard].astype(f32)
        for lane in lanes:
            value += box[lane, shard].astype(f32)
        acc[target, shard] = value.astype(kind)

    def move(part, shard, lane, peer):
        return remote(acc.at[part, shard], box.at[lane, shard], send.at[lane, shard], recv.at[lane, shard], peer)

    def mine(shard):
        return pltpu.make_async_copy(src.at[:, shard, c], acc.at[:, shard], near.at[0, shard])

    def core(shard):
        return remote(src.at[:, shard, 1 - c], other.at[:, shard], near.at[1, shard], near.at[2, shard], place.core_peer)

    for shard in order:
        core(shard).start()
        mine(shard).start()
    yield
    for half in halves:
        for j in half:
            shard = order[j]
            mine(shard).wait()
            core(shard).wait_recv()

            @pl.loop(0, 4)
            def _(part):
                acc[part, shard] = (
                    acc[part, shard].astype(f32) + other[part, shard].astype(f32)
                ).astype(kind)

            if j % 2 == 0:
                move(bd, shard, far, place.x_peer).start()
                move(bx, shard, via_x, place.x_peer).start()
            else:
                move(bd, shard, far, place.y_peer).start()
                move(by, shard, via_y, place.y_peer).start()
        yield
    for half in halves:
        for j in half:
            shard = order[j]
            move(bd, shard, far, place.x_peer).wait_recv()
            if j % 2 == 0:
                add(by, shard, far)
                move(by, shard, via_y, place.y_peer).start()
            else:
                add(bx, shard, far)
                move(bx, shard, via_x, place.x_peer).start()
        yield
    for half in halves:
        for j in half:
            shard = order[j]
            move(bx, shard, via_x, place.x_peer).wait_recv()
            move(by, shard, via_y, place.y_peer).wait_recv()
            add(b, shard, via_x, via_y)

            @pl.when(z < shard)
            def _():
                @pl.when(z > 0)
                def _():
                    move(b, shard, up, place.up_peer).wait_recv()
                    add(b, shard, up)

                move(b, shard, up, place.up_peer).start()

            @pl.when(z > shard)
            def _():
                @pl.when(z + 1 < nz)
                def _():
                    move(b, shard, down, place.down_peer).wait_recv()
                    add(b, shard, down)

                move(b, shard, down, place.down_peer).start()

        yield
    total[...] = acc[b, z].astype(f32)

    @pl.when(z > 0)
    def _():
        move(b, z, up, place.up_peer).wait_recv()
        total[...] += box[up, z].astype(f32)

    @pl.when(z + 1 < nz)
    def _():
        move(b, z, down, place.down_peer).wait_recv()
        total[...] += box[down, z].astype(f32)

    result = pltpu.make_async_copy(total, out, one.at[0])
    result.start()
    for shard in range(nz):
        core(shard).wait_send()
        for lane in (far, via_x, via_y):
            move(b, shard, lane, place.x_peer).wait_send()
        pl.when(z < shard)(lambda: move(b, shard, up, place.up_peer).wait_send())
        pl.when(z > shard)(lambda: move(b, shard, down, place.down_peer).wait_send())
    result.wait()
    yield


def reduce_job(array, plan):
    nz = lax.axis_size("seq") // 2
    shape = array.shape[1:]
    return Job(
        [array.reshape((4, nz, 2) + shape)],
        [jax.ShapeDtypeStruct(shape, f32)],
        reduce_scratch(nz, shape, array.dtype),
        reduce_task,
        plan,
    )


def total_scratch(nz, shape, shared):
    return [
        pltpu.VMEM((3,) + shape, f32),
        pltpu.VMEM((2,) + shape, f32),
        pltpu.VMEM((2, nz, shared, LANES), f32),
        pltpu.SemaphoreType.DMA((2, 3)),
        pltpu.SemaphoreType.DMA((2, nz)),
    ]


def total_task(place, src, out, scratch):
    box, sums, lines, pair, chain = scratch
    z, c, nz = place.z, place.c, place.nz
    rows = src.shape[0]
    shared = lines.shape[2]
    tail = pl.ds(rows - shared, shared)

    def swap(source, dst, i, peer):
        return remote(source, dst, pair.at[0, i], pair.at[1, i], peer)

    first = swap(src, box.at[0], 0, place.x_peer)
    first.start()
    yield
    first.wait()
    sums[0] = src[...] + box[0]
    second = swap(sums.at[0], box.at[1], 1, place.y_peer)
    second.start()
    yield
    second.wait()
    sums[1] = sums[0] + box[1]
    third = swap(sums.at[1, tail], box.at[2, tail], 2, place.core_peer)
    third.start()
    yield
    third.wait()
    lines[0, z] = sums[1, tail] + box[2, tail]

    def along(step):
        peer = lax.rem(z + step, nz)
        return remote(lines.at[0, z], lines.at[1, z], chain.at[0, step], chain.at[1, step], (place.b, 2 * peer + c))

    for step in range(1, nz):
        along(step).start()
    lines[1, z] = lines[0, z]
    yield
    for step in range(1, nz):
        along(step).wait_recv()
    value = lines[1, 0]
    for shard in range(1, nz):
        value = value + lines[1, shard]
    out[: rows - shared] = sums[1, : rows - shared]
    out[tail] = value
    for step in range(1, nz):
        along(step).wait_send()
    yield


def prepare(jobs, pos_rows, first_w, second_w, third_w, cols, decay, tables, ids):
    layers, hidden, own = third_w.shape
    length = pos_rows.shape[1]
    rows = (own // 8,) + tables[4].shape
    results = [
        jax.ShapeDtypeStruct((layers, 4, hidden, length), f32),
        jax.ShapeDtypeStruct((layers, own, length), f32),
        jax.ShapeDtypeStruct((layers, own, LANES), f32),
    ] + [jax.ShapeDtypeStruct(rows, f32)] * (2 * layers)

    def body(place, runner, ins, outs, scratch):
        pos, first, second, third, bias, rate = ins[:6]
        factors = ins[6:]
        acts, shaped, squares = outs[:3]
        specs = outs[3:]
        spans, groups = length // SPAN, own // 8
        squares[...] = jnp.zeros_like(squares)
        for part in range(8):
            runner.phase()

            @pl.loop(part * spans // 8, (part + 1) * spans // 8)
            def _(i):
                for layer in range(layers):
                    filter_span(
                        layer, pl.multiple_of(i * SPAN, SPAN), pos, first, second, third, bias, rate, acts, shaped, squares
                    )

        for part in range(6):
            runner.phase()

            @pl.loop(part * groups // 6, (part + 1) * groups // 6)
            def _(group):
                for layer in range(layers):
                    filter_points(layer, group, factors, shaped, squares, *specs[2 * layer : 2 * layer + 2])

    return fused_call(
        "prepare",
        body,
        [pos_rows, first_w, second_w, third_w, cols, decay, *tables],
        results,
        [],
        jobs,
        False,
        ids,
    )


def last(jobs, pos_rows, second_w, third_w, decay, kept, grad_taps, ids):
    layers, hidden, own = third_w.shape
    length = pos_rows.shape[1]
    nz = lax.axis_size("seq") // 2
    each, shared = hidden + 8, FEATURES + hidden
    payload = jax.ShapeDtypeStruct((layers * (each + shared), LANES), f32)

    def body(place, runner, ins, outs, scratch):
        pos, second, third, rate, acts, shaped, squares = ins[:7]
        taps = ins[7:]
        dots, grad_third, grad_second, grad_first, payload_in = scratch[:5]
        for ref in (dots, grad_third, grad_second, grad_first, payload_in):
            ref[...] = jnp.zeros_like(ref)
        runner.phase()
        spans = length // SPAN

        @pl.loop(0, spans)
        def _(i):
            for layer in range(layers):
                filter_back_dot(layer, pl.multiple_of(i * SPAN, SPAN), shaped, taps[layer], dots)

        for part in range(8):
            runner.phase()

            @pl.loop(part * spans // 8, (part + 1) * spans // 8)
            def _(i):
                for layer in range(layers):
                    filter_back_span(
                        layer, pl.multiple_of(i * SPAN, SPAN), pos, second, third, rate, acts, shaped, squares,
                        taps[layer], dots, (grad_third, grad_second, grad_first)
                    )

        for layer in range(layers):
            start = layer * each
            payload_in[start : start + hidden, :own] = grad_third[layer]
            lag = taps[layer][:, 0].reshape(own, LANES)
            pick = jnp.where(lax.broadcasted_iota(jnp.int32, (8, LANES), 1) == 0, 1.0, 0.0)
            payload_in[start + hidden : start + each, :own] = near_dot(pick, lag, 1, 1)
            start = layers * each + layer * shared
            payload_in[start : start + FEATURES, : 2 * hidden] = grad_first[layer]
            payload_in[start + FEATURES : start + shared, :hidden] = grad_second[layer]
        runner.add(total_task(place, payload_in, outs[0], scratch[5:]))

    return fused_call(
        "last",
        body,
        [pos_rows, second_w, third_w, decay, *kept, *grad_taps],
        [payload],
        [
            pltpu.VMEM((layers, own, LANES), f32),
            pltpu.VMEM((layers, hidden, own), f32),
            pltpu.VMEM((layers, hidden, hidden), f32),
            pltpu.VMEM((layers, FEATURES, 2 * hidden), f32),
            pltpu.VMEM(payload.shape, f32),
        ]
        + total_scratch(nz, payload.shape, layers * shared),
        jobs,
        True,
        ids,
    )


def conv_lanes(value, rim_near, rim_far):
    lane = lax.broadcasted_iota(jnp.int32, value.shape, 1)
    near = jnp.where(lane == 0, rim_near, pltpu.roll(value, 1, 1))
    far = jnp.where(lane == 0, rim_far, jnp.where(lane == 1, rim_near, pltpu.roll(value, 2, 1)))
    return near, far


def rows_of(ref, stream, block, count):
    value = ref[stream, pl.ds(block, count)].astype(f32)
    return value.reshape(-1, value.shape[-1])


def short_out(mixed, conv, rim, stream, block, count=1):
    value = rows_of(mixed, stream, block, count)
    side, edge = rows_of(conv, stream, block, count), rows_of(rim, stream, block, count)
    near, far = conv_lanes(value, edge[:, 1:2], edge[:, 0:1])
    return side[:, 0:1] * far + side[:, 1:2] * near + side[:, 2:3] * value


def by_blocks(nblocks, most):
    return max(k for k in range(1, most + 1) if nblocks % k == 0)


def edge_scratch(streams, nblocks, chans):
    rows = pltpu.VMEM((streams, 16, nblocks * chans), f32)
    return [rows, rows, pltpu.VMEM((streams, nblocks, chans, LANES), f32), pltpu.SemaphoreType.DMA((2,))]


def edge_copy(place, scratch, to_right):
    out, came, _, sems = scratch
    ns = 2 * place.nz
    peer = lax.min(place.s + 1, ns - 1) if to_right else lax.max(place.s - 1, 0)
    return remote(out, came, sems.at[0], sems.at[1], (place.b, peer))


def send_edge(place, scratch, tiles_of, first, to_right):
    out = scratch[0]
    row = lax.broadcasted_iota(jnp.int32, (16, LANES), 0)
    lane = lax.broadcasted_iota(jnp.int32, (16, LANES), 1)
    pick = jnp.where(jnp.logical_and(lane == row + first, row < 2), 1.0, 0.0).astype(bf16)
    for stream in range(out.shape[0]):
        high, low = in_two(tiles_of(stream).reshape(-1, LANES))
        out[stream] = contract(
            jnp.concatenate([pick, pick], axis=1), jnp.concatenate([high, low], axis=1), 1, 1
        )
    has = place.s + 1 < 2 * place.nz if to_right else place.s > 0
    pl.when(has)(lambda: edge_copy(place, scratch, to_right).start())


def take_edge(place, scratch, to_right):
    _, came, cols, _ = scratch
    _, nblocks, chans, _ = cols.shape
    comes = place.s > 0 if to_right else place.s + 1 < 2 * place.nz
    sends = place.s + 1 < 2 * place.nz if to_right else place.s > 0

    @pl.when(comes)
    def _():
        edge_copy(place, scratch, to_right).wait_recv()
        row = lax.broadcasted_iota(jnp.int32, (16, LANES), 0)
        lane = lax.broadcasted_iota(jnp.int32, (16, LANES), 1)
        spread = jnp.where(jnp.logical_and(lane == row, row < 2), 1.0, 0.0).astype(bf16)
        both = jnp.concatenate([spread, spread], axis=0)
        for stream in range(cols.shape[0]):
            pair = jnp.concatenate(in_two(came[stream]), axis=0)
            cols[stream] = contract(pair, both, 0, 0).reshape(nblocks, chans, LANES)

    @pl.when(jnp.logical_not(comes))
    def _():
        cols[...] = jnp.zeros_like(cols)

    pl.when(sends)(lambda: edge_copy(place, scratch, to_right).wait_send())


def sub_rows(chans):
    return 16 if chans % 16 == 0 else chans


def mix_body(place, runner, ins, outs, scratch, layer):
    mixed, conv, spec_re, spec_im, skip = ins[:5]
    tables = ins[5:]
    long_out, gated, sig_re, sig_im, rim = outs
    signal, chan_in, chan_out, tok_in, send, recv = scratch[:6]
    edge = [scratch[6], scratch[7], rim, scratch[8]]
    toks = mixed.shape[3]
    ns, groups, quarters, chans, _ = signal.shape
    take = sub_rows(chans)

    def to_chan(g, step):
        peer = lax.rem(place.s + step, ns)
        return remote(
            signal.at[peer, g],
            chan_in.at[g, pl.ds(place.s * quarters, quarters)],
            send.at[0, g, step],
            recv.at[0, g, step],
            (place.b, peer),
        )

    def send_pieces(step, first, value):
        peer = lax.rem(place.s + step, ns)
        count = value.shape[0] // chans
        for k in range(count):
            for q in range(quarters):
                piece = value[k * chans : (k + 1) * chans, q * LANES : (q + 1) * LANES]
                signal[peer, first + k, q] = piece

        @pl.when(step < ns)
        def _():
            for k in range(count):
                to_chan(first + k, step).start()

        @pl.when(step == ns)
        def _():
            for k in range(count):
                for q in range(quarters):
                    chan_in[first + k, place.s * quarters + q] = signal[peer, first + k, q]

    def to_tok(g, step):
        peer = lax.rem(place.s + step, ns)
        return remote(
            chan_out.at[g, pl.ds(peer * quarters, quarters)],
            tok_in.at[place.s, g],
            send.at[1, g, step],
            recv.at[1, g, step],
            (place.b, peer),
        )

    send_edge(place, edge, lambda k: mixed[k, :, :, toks - LANES :].astype(f32), LANES - 2, True)
    runner.phase()
    take_edge(place, edge, True)
    share = by_blocks(groups, 3)
    for first in range(0, groups, share):

        @pl.loop(1, ns + 1)
        def _(step):
            peer = lax.rem(place.s + step, ns)
            block = peer * groups + first
            value = short_out(mixed, conv, rim, 1, block, share) * short_out(mixed, conv, rim, 2, block, share)
            send_pieces(step, first, value.astype(bf16))

    runner.phase()
    for g in range(groups):

        @pl.loop(1, ns)
        def _(step):
            to_chan(g, step).wait_recv()

        @pl.loop(0, chans // take)
        def _(i):
            at = pl.ds(pl.multiple_of(i * take, take), take)
            block = chan_in[g, :, at, :].astype(f32)
            parts = []
            for j in range(take // 8):
                index = (g * chans) // 8 + i * (take // 8) + j
                x = block[:, 8 * j : 8 * j + 8, :]
                re, im = to_points(x, tables, True)
                sig_re[index] = re
                sig_im[index] = im
                tap_re, tap_im = spec_re[index], spec_im[index]
                y = from_points(re * tap_re - im * tap_im, re * tap_im + im * tap_re, tables)
                parts.append(y + skip[layer, index][None] * x)
            chan_out[g, :, at, :] = jnp.concatenate(parts, axis=1).astype(bf16)

        @pl.loop(1, ns)
        def _(step):
            to_tok(g, step).start()

        for q in range(quarters):
            tok_in[place.s, g, q] = chan_out[g, place.s * quarters + q]
        runner.phase()

    for g in range(groups):

        @pl.loop(1, ns)
        def _(step):
            to_tok(g, step).wait_recv()

        @pl.loop(0, ns, unroll=4)
        def _(owner):
            block = owner * groups + g
            value = jnp.concatenate([tok_in[owner, g, q] for q in range(quarters)], axis=1)
            long_out[block] = value
            gated[block] = (short_out(mixed, conv, rim, 0, block) * value.astype(f32)).astype(bf16)

        if g % 2:
            runner.phase()

    for g in range(groups):

        @pl.loop(1, ns)
        def _(step):
            to_chan(g, step).wait_send()
            to_tok(g, step).wait_send()


def mixer_scratch(ns, groups, quarters, chans):
    pieces = pltpu.VMEM((ns, groups, quarters, chans, LANES), bf16)
    lines = pltpu.VMEM((groups, ns * quarters, chans, LANES), bf16)
    sems = pltpu.SemaphoreType.DMA((2, groups, ns))
    return [pieces, lines, lines, pieces, sems, sems]


def mix(jobs, layer, mixed, conv, spec, skip, tables, ids):
    ns = lax.axis_size("seq")
    _, nblocks, chans, toks = mixed.shape
    groups, quarters = nblocks // ns, toks // LANES
    rows = jax.ShapeDtypeStruct((groups * chans // 8,) + tables[4].shape, f32)
    tokens = jax.ShapeDtypeStruct((nblocks, chans, toks), bf16)
    edges = edge_scratch(3, nblocks, chans)
    return fused_call(
        "mix",
        functools.partial(mix_body, layer=layer),
        [mixed, conv, *spec, skip, *tables],
        [tokens, tokens, rows, rows, jax.ShapeDtypeStruct(conv.shape, f32)],
        mixer_scratch(ns, groups, quarters, chans) + edges[:2] + edges[3:],
        jobs,
        True,
        ids,
    )


def unmix_body(place, runner, ins, outs, scratch, layer):
    mixed, conv, rim, long_out, grad_gated, spec_re, spec_im, sig_re, sig_im, skip = ins[:10]
    tables = ins[10:]
    grad_taps, grad_mixed, grad_conv = outs
    pull, chan_in, chan_out, tok_in, send, recv, grad_short, partials = scratch[:8]
    edge = scratch[8:]
    toks = mixed.shape[3]
    runner.phase()
    ns, groups, quarters, chans, _ = pull.shape
    take = sub_rows(chans)

    def to_chan(g, step):
        peer = lax.rem(place.s + step, ns)
        return remote(
            pull.at[peer, g],
            chan_in.at[g, pl.ds(place.s * quarters, quarters)],
            send.at[0, g, step],
            recv.at[0, g, step],
            (place.b, peer),
        )

    def send_pieces(step, first, value):
        peer = lax.rem(place.s + step, ns)
        count = value.shape[0] // chans
        for k in range(count):
            for q in range(quarters):
                piece = value[k * chans : (k + 1) * chans, q * LANES : (q + 1) * LANES]
                pull[peer, first + k, q] = piece

        @pl.when(step < ns)
        def _():
            for k in range(count):
                to_chan(first + k, step).start()

        @pl.when(step == ns)
        def _():
            for k in range(count):
                for q in range(quarters):
                    chan_in[first + k, place.s * quarters + q] = pull[peer, first + k, q]

    def to_tok(g, step):
        peer = lax.rem(place.s + step, ns)
        return remote(
            chan_out.at[g, pl.ds(peer * quarters, quarters)],
            tok_in.at[place.s, g],
            send.at[1, g, step],
            recv.at[1, g, step],
            (place.b, peer),
        )

    share = by_blocks(groups, 3)
    for first in range(0, groups, share):

        @pl.loop(1, ns + 1)
        def _(step):
            block = lax.rem(place.s + step, ns) * groups + first
            gated = grad_gated[pl.ds(block, share)].reshape(share * chans, toks)
            send_pieces(step, first, (gated * short_out(mixed, conv, rim, 0, block, share)).astype(bf16))

    runner.phase()
    for g in range(groups):

        @pl.loop(1, ns)
        def _(step):
            to_chan(g, step).wait_recv()

        @pl.loop(0, chans // take)
        def _(i):
            at = pl.ds(pl.multiple_of(i * take, take), take)
            block = chan_in[g, :, at, :].astype(f32)
            parts = []
            for j in range(take // 8):
                index = (g * chans) // 8 + i * (take // 8) + j
                x = block[:, 8 * j : 8 * j + 8, :]
                re, im = to_points(x, tables, True)
                tap_re, tap_im = spec_re[index], spec_im[index]
                y = from_points(tap_re * re + tap_im * im, tap_re * im - tap_im * re, tables)
                parts.append(y + skip[layer, index][None] * x)
                own_re, own_im = sig_re[index], sig_im[index]
                grad_taps[index] = from_points(
                    own_re * re + own_im * im, own_re * im - own_im * re, tables
                )
            chan_out[g, :, at, :] = jnp.concatenate(parts, axis=1).astype(bf16)

        @pl.loop(1, ns)
        def _(step):
            to_tok(g, step).start()

        for q in range(quarters):
            tok_in[place.s, g, q] = chan_out[g, place.s * quarters + q]
        runner.phase()

    @pl.loop(0, ns * groups, unroll=4)
    def _(block):
        grad_short[0, block] = grad_gated[block] * long_out[block].astype(f32)

    for g in range(groups):

        @pl.loop(1, ns)
        def _(step):
            to_tok(g, step).wait_recv()

        @pl.loop(0, ns, unroll=4)
        def _(owner):
            block = owner * groups + g
            value = jnp.concatenate(
                [tok_in[owner, g, q] for q in range(quarters)], axis=1
            ).astype(f32)
            grad_short[1, block] = value * short_out(mixed, conv, rim, 2, block)
            grad_short[2, block] = value * short_out(mixed, conv, rim, 1, block)

        if g % 2:
            runner.phase()

    send_edge(place, edge, lambda k: grad_short[k, :, :, :LANES], 0, False)
    many = by_blocks(ns * groups, 4)
    ones = jnp.ones((2 * LANES, LANES), bf16)
    for stream in range(3):

        @pl.loop(0, ns * groups // many, unroll=2)
        def _(i):
            at = pl.ds(i * many, many)
            grad = rows_of(grad_short, stream, i * many, many)
            value = rows_of(mixed, stream, i * many, many)
            side = rows_of(rim, stream, i * many, many)
            near, far = conv_lanes(value, side[:, 1:2], side[:, 0:1])
            for k, moved in enumerate((far, near, value)):
                terms = grad * moved
                partial = terms[:, :LANES]
                for q in range(1, quarters):
                    partial += terms[:, q * LANES : (q + 1) * LANES]
                partials[k, at] = partial.reshape(many, chans, LANES)

        sums = [
            product(jnp.concatenate(in_two(partials[k].reshape(-1, LANES)), axis=1), ones)
            for k in range(3)
        ]
        lane = lax.broadcasted_iota(jnp.int32, sums[0].shape, 1)
        found = jnp.where(lane == 0, sums[0], jnp.where(lane == 1, sums[1], sums[2]))
        grad_conv[stream] = found.reshape(ns * groups, chans, LANES)
    runner.phase()
    take_edge(place, edge, False)
    edge_cols = edge[2]
    for stream in range(3):

        @pl.loop(0, ns * groups // many, unroll=2)
        def _(i):
            value = rows_of(grad_short, stream, i * many, many)
            side, after = rows_of(conv, stream, i * many, many), rows_of(edge_cols, stream, i * many, many)
            lane = lax.broadcasted_iota(jnp.int32, value.shape, 1)
            near = jnp.where(lane == toks - 1, after[:, 0:1], pltpu.roll(value, toks - 1, 1))
            far = jnp.where(
                lane == toks - 1,
                after[:, 1:2],
                jnp.where(lane == toks - 2, after[:, 0:1], pltpu.roll(value, toks - 2, 1)),
            )
            total = side[:, 2:3] * value + side[:, 1:2] * near + side[:, 0:1] * far
            grad_mixed[stream, pl.ds(i * many, many)] = total.astype(bf16).reshape(many, chans, toks)

    for g in range(groups):

        @pl.loop(1, ns)
        def _(step):
            to_chan(g, step).wait_send()
            to_tok(g, step).wait_send()


def unmix(jobs, layer, mixed, conv, rim, long_out, grad_gated, spec, sig, skip, tables, ids):
    ns = lax.axis_size("seq")
    _, nblocks, chans, toks = mixed.shape
    groups, quarters = nblocks // ns, toks // LANES
    return fused_call(
        "unmix",
        functools.partial(unmix_body, layer=layer),
        [mixed, conv, rim, long_out, grad_gated, *spec, *sig, skip, *tables],
        [
            jax.ShapeDtypeStruct((groups * chans // 8, ns * quarters, 8, LANES), f32),
            jax.ShapeDtypeStruct(mixed.shape, bf16),
            jax.ShapeDtypeStruct(conv.shape, f32),
        ],
        mixer_scratch(ns, groups, quarters, chans)
        + [pltpu.VMEM(mixed.shape, f32), pltpu.VMEM(conv.shape, f32)]
        + edge_scratch(3, nblocks, chans),
        jobs,
        True,
        ids,
    )


def on_device(
    tokens,
    cotangent,
    norm_gains,
    w_in,
    short_conv,
    w_out,
    w_fc,
    w_proj,
    filt_w1,
    filt_b1,
    filt_w2,
    filt_b2,
    filt_w3,
    skip_gain,
    decay_rate,
):
    layers, _, width3 = w_in.shape
    width = width3 // 3
    ns = lax.axis_size("seq")
    devices = lax.axis_size("batch") * ns
    stream = tokens[0].astype(f32)
    toks = stream.shape[0]
    length = toks * ns
    own_chans = width // ns
    chans = 16 if own_chans % 16 == 0 else own_chans
    groups = own_chans // chans
    nblocks = ns * groups
    blocked = (3, nblocks, chans)
    tables = transform_tables(length)
    pos_rows = position_rows(length, filt_w1.shape[1])

    gain_cols, conv_cols = norm_gains.shape[2], short_conv.shape[2]
    small = jnp.concatenate(
        [
            jnp.pad(norm_gains.reshape(2 * layers, gain_cols).astype(f32), ((0, 0), (0, LANES - gain_cols))),
            jnp.pad(short_conv.reshape(3 * layers, conv_cols).astype(f32), ((0, 0), (0, LANES - conv_cols))),
        ],
        axis=0,
    )
    small = jnp.pad(small, ((0, -small.shape[0] % 8), (0, 0)))[None]

    first_w = jnp.pad(
        jnp.concatenate([filt_w1, filt_b1[:, None]], axis=1),
        ((0, 0), (0, FEATURES - filt_w1.shape[1] - 1), (0, 0)),
    )
    cols = jnp.broadcast_to(filt_b2[:, :, None], filt_b2.shape + (LANES,))
    decay = jnp.broadcast_to(decay_rate[:, :, None], (layers, own_chans, LANES))
    skips = jnp.broadcast_to(
        skip_gain.reshape(layers, -1, 8, 1), (layers, own_chans // 8, 8, LANES)
    )

    mats = (w_in, w_out, w_fc, w_proj)
    jobs = [gather_job(small, 0, GATHER_PLANS[0])]
    jobs += [gather_job(mat, 0, plan) for mat, plan in zip(mats, GATHER_PLANS[1:])]
    jobs += [
        column_job(mat, layer, plan)
        for layer in range(1, layers)
        for mat, plan in zip(mats, COLUMN_PLANS)
    ]
    ids = itertools.count()
    sets = [list(range(layers))] if length <= 8192 else [[layer] for layer in range(layers)]
    kept, specs = [], []
    for part in sets:
        of = slice(part[0], part[-1] + 1)
        filters, found = prepare(
            jobs, pos_rows, first_w[of], filt_w2[of], filt_w3[of], cols[of], decay[of], tables, ids
        )
        kept.append(filters[:3])
        specs += [filters[3 + 2 * k : 5 + 2 * k] for k in range(len(part))]
        gathered = found if part is sets[0] else gathered
        jobs = []
    small_all = gathered[0].reshape(devices, -1, LANES)
    gains = jnp.swapaxes(small_all[:, : 2 * layers, :gain_cols], 0, 1).reshape(layers, 2, width)
    convs = jnp.swapaxes(
        small_all[:, 2 * layers : 5 * layers, :conv_cols], 0, 1
    ).reshape(layers, 3, width3)
    conv_cols_of = [
        jnp.pad(convs[layer].T, ((0, 0), (0, LANES - 3))).reshape(blocked + (LANES,))
        for layer in range(layers)
    ]
    plain = lambda parts: parts.reshape(-1, parts.shape[-1])
    weights = {(i, 0): plain(gathered[1 + i]) for i in range(4)}
    columns = {
        (i, layer): gathered[1 + 4 * layer + i] for layer in range(1, layers) for i in range(4)
    }

    def plane_jobs(layer):
        keys = [(3, layer)] if layer else []
        keys = [key for key in keys + [(0, layer + 1), (1, layer + 1), (2, layer + 1)] if key in columns]
        return keys, [plane_job(columns[key], plan) for key, plan in zip(keys, PLANE_PLANS)]

    saved = []
    for layer in range(layers):
        in_mat = weights[0, layer]
        normed, inv_std = layer_norm_parts(stream)
        norm_in = (normed * gains[layer, 0]).astype(bf16)
        mixed = contract(in_mat, norm_in, 0, 1).astype(bf16)
        mixed = mixed.reshape(blocked + (toks,))
        keys, jobs = plane_jobs(layer)
        (long_out, gated, sig_re, sig_im, rim), arrived = mix(
            jobs, layer, mixed, conv_cols_of[layer], specs[layer], skips, tables, ids
        )
        weights.update({key: plain(parts) for key, parts in zip(keys, arrived)})
        out_mat, fc_mat, proj_mat = (weights[i, layer] for i in (1, 2, 3))
        gated = gated.reshape(width, toks)
        middle = stream + contract(gated, out_mat, 0, 0)
        normed_mid, inv_mid = layer_norm_parts(middle)
        hidden_in = (normed_mid * gains[layer, 1]).astype(bf16)
        hidden_pre = product(hidden_in, fc_mat)
        hidden_act = jax.nn.gelu(hidden_pre).astype(bf16)
        saved.append(
            (normed, inv_std, norm_in, mixed, rim, long_out, gated, (sig_re, sig_im))
            + (normed_mid, inv_mid, hidden_in, hidden_pre, hidden_act)
        )
        stream = middle + product(hidden_act, proj_mat)
    mixed_out = stream.astype(bf16)

    grad = cotangent[0].astype(f32)
    summed = {}
    left_over = []
    small_grads = [None] * layers
    taps_grads = [None] * layers

    def parts_of(grad_mat):
        return grad_mat.reshape(devices, -1, grad_mat.shape[1])

    for layer in reversed(range(layers)):
        in_mat, out_mat, fc_mat, proj_mat = (weights[i, layer] for i in range(4))
        (normed, inv_std, norm_in, mixed, rim, long_out, gated, sig) = saved[layer][:8]
        (normed_mid, inv_mid, hidden_in, hidden_pre, hidden_act) = saved[layer][8:]
        grad_top = grad.astype(bf16)
        grad_act = contract(grad_top, proj_mat, 1, 1)
        grad_proj = contract(hidden_act, grad_top, 0, 0).astype(bf16)
        grad_pre = jax.vjp(jax.nn.gelu, hidden_pre)[1](grad_act)[0].astype(bf16)
        grad_hidden = contract(grad_pre, fc_mat, 1, 1)
        grad_fc = contract(hidden_in, grad_pre, 0, 0).astype(bf16)
        grad_gain_mid = jnp.sum(grad_hidden * normed_mid, axis=0)
        grad_middle = grad + norm_back(grad_hidden * gains[layer, 1], normed_mid, inv_mid)
        grad_mix = grad_middle.astype(bf16)
        grad_gated = contract(out_mat, grad_mix, 1, 1).reshape(nblocks, chans, toks)
        grad_out = contract(gated, grad_mix, 1, 0).astype(bf16)
        pending = [
            (key, parts_of(mat)) for key, mat in (((3, layer), grad_proj), ((2, layer), grad_fc), ((1, layer), grad_out))
        ]
        (taps_grads[layer], grad_mixed, grad_conv), arrived = unmix(
            [reduce_job(parts, plan) for (_, parts), plan in zip(pending, REDUCE_PLANS)],
            layer, mixed, conv_cols_of[layer], rim, long_out, grad_gated, specs[layer], sig, skips, tables, ids
        )
        summed.update({key: total for (key, _), total in zip(pending, arrived)})
        grad_mixed = grad_mixed.reshape(width3, toks)
        grad_norm_in = contract(grad_mixed, in_mat, 0, 1)
        grad_in = contract(norm_in, grad_mixed, 0, 1).astype(bf16)
        grad_gain_in = jnp.sum(grad_norm_in * normed, axis=0)
        grad = grad_middle + norm_back(grad_norm_in * gains[layer, 0], normed, inv_std)
        left_over.append(((0, layer), parts_of(grad_in)))
        small_grads[layer] = (
            jnp.stack([grad_gain_in, grad_gain_mid]),
            jnp.swapaxes(grad_conv.reshape(width3, LANES)[:, :3], 0, 1),
        )

    def rows_for(values, cols):
        pieces = jnp.swapaxes(values.reshape(values.shape[0], devices, cols), 0, 1)
        return jnp.pad(pieces, ((0, 0), (0, 0), (0, LANES - cols)))

    small_rows = jnp.concatenate(
        [rows_for(small_grads[layer][0], gain_cols) for layer in range(layers)]
        + [rows_for(small_grads[layer][1], conv_cols) for layer in range(layers)],
        axis=1,
    )
    small_rows = jnp.pad(small_rows, ((0, 0), (0, -small_rows.shape[1] % 8), (0, 0)))
    hidden = filt_w2.shape[1]
    emb = filt_w1.shape[1]
    left_over.insert(0, ("small", small_rows))
    each, shared = hidden + 8, FEATURES + hidden
    by_column, by_all = [], []
    jobs = [reduce_job(parts, plan) for (_, parts), plan in zip(left_over, LAST_PLANS)]
    for part, acts in zip(sets, kept):
        of = slice(part[0], part[-1] + 1)
        (totals,), arrived = last(
            jobs, pos_rows, filt_w2[of], filt_w3[of], decay[of], acts, taps_grads[of], ids
        )
        if part is sets[0]:
            summed.update({key: total for (key, _), total in zip(left_over, arrived)})
        jobs = []
        by_column.append(totals[: len(part) * each].reshape(-1, each, LANES))
        by_all.append(totals[len(part) * each :].reshape(-1, shared, LANES))
    by_column, by_all = jnp.concatenate(by_column), jnp.concatenate(by_all)
    small_sum = summed["small"]
    block = [jnp.stack([summed[i, layer] for layer in range(layers)]) for i in range(4)]
    gains_grad = small_sum[: 2 * layers, :gain_cols].reshape(layers, 2, gain_cols)
    conv_grad = small_sum[2 * layers : 5 * layers, :conv_cols].reshape(layers, 3, conv_cols)
    return (
        mixed_out[None],
        grad[None],
        gains_grad,
        block[0],
        conv_grad,
        block[1],
        block[2],
        block[3],
        by_all[:, :emb, :hidden],
        by_all[:, emb, :hidden],
        by_all[:, FEATURES:, :hidden],
        by_all[:, emb, hidden : 2 * hidden],
        by_column[:, :hidden, :own_chans],
        by_column[:, hidden, :own_chans],
    )


def solution(mesh):
    both = ("batch", "seq")
    in_specs = (
        P("batch", "seq", None),
        P("batch", "seq", None),
        P(None, None, both),
        P(None, both, None),
        P(None, None, both),
        P(None, both, None),
        P(None, both, None),
        P(None, both, None),
        P(),
        P(),
        P(),
        P(),
        P(None, None, "seq"),
        P(None, "seq"),
        P(None, "seq"),
    )
    out_specs = in_specs[:14]
    return jax.shard_map(
        on_device, mesh=mesh, in_specs=in_specs, out_specs=out_specs, check_vma=False
    )
```

```python
import functools
import itertools
import math

import jax
import jax.numpy as jnp
import numpy as np
from jax import lax
from jax.experimental import pallas as pl
from jax.experimental.pallas import tpu as pltpu
from jax.sharding import PartitionSpec as P

MESH = pl.DeviceIdType.MESH
LANES = 128
VMEM_LIMIT = 58 * 1024 * 1024
GATHER_PLANS = [[0, 1, 3, 5, 7, 9, 12], [0, 1, 3, 5, 7, 9, 12], [0, 2, 4, 6, 8, 10, 12], [0, 2, 5, 8, 10, 12, 14], [0, 3, 6, 9, 12, 14, 16]]
COLUMN_PLANS = [[2, 5, 8, 11, 14], [2, 5, 8, 11, 14], [3, 7, 10, 13, 15], [4, 8, 12, 14, 16]]
PLANE_PLANS = [[0, 3, 5, 7], [0, 4, 6, 8], [2, 6, 8, 10]]
REDUCE_PLANS = [[0, 1, 2, 4, 5, 8, 9, 12], [0, 3, 3, 7, 7, 10, 10, 12], [0, 2, 4, 8, 9, 11, 11, 12]]
LAST_PLANS = [[0, 1, 1, 4, 4, 7, 7, 9], [0, 2, 2, 5, 5, 7, 8, 9], [0, 2, 2, 5, 5, 7, 8, 9]]
f32 = jnp.float32
bf16 = jnp.bfloat16


def product(left_mat, right_mat):
    return jnp.dot(left_mat, right_mat, preferred_element_type=f32)


def contract(left_mat, right_mat, left_dim, right_dim):
    return lax.dot_general(
        left_mat, right_mat, (((left_dim,), (right_dim,)), ((), ())), preferred_element_type=f32
    )


def layer_norm_parts(stream):
    mean_val = jnp.mean(stream, axis=-1, keepdims=True)
    centered = stream - mean_val
    inv_std = lax.rsqrt(jnp.mean(centered * centered, axis=-1, keepdims=True) + 1e-05)
    return (centered * inv_std, inv_std)


def norm_back(grad_normed, normed, inv_std):
    mean_grad = jnp.mean(grad_normed, axis=-1, keepdims=True)
    mean_cross = jnp.mean(grad_normed * normed, axis=-1, keepdims=True)
    return inv_std * (grad_normed - mean_grad - normed * mean_cross)


def split_bf16(table):
    high = table.astype(np.float32).astype(jnp.bfloat16)
    return high, (table - high.astype(np.float64)).astype(np.float32).astype(jnp.bfloat16)


def transform_tables(length):
    blocks = min(length // LANES, 32)
    inside = length // blocks
    n1 = np.arange(blocks)
    n2 = np.arange(inside)
    outer = 2 * np.pi * ((n1[:, None] * (4 * n1[None, :] + 1)) % (4 * blocks)) / (4 * blocks)
    eye = np.eye(8)
    forward = np.concatenate([np.cos(outer).T, -np.sin(outer).T], axis=0)
    left_fwd = np.kron(forward, eye)
    left_inv = np.kron(np.concatenate([np.cos(outer), -np.sin(outer)], axis=1), eye) / length
    inner = 2 * np.pi * ((n2[:, None] * n2[None, :]) % inside) / inside
    cos2, sin2 = np.cos(inner), np.sin(inner)
    right_fwd = np.block([[cos2, -sin2], [sin2, cos2]])
    right_inv = np.block([[cos2, sin2], [-sin2, cos2]])
    twist = 2 * np.pi * (n2[None, :] * (4 * n1[:, None] + 1)) / (4 * length)
    twist_cos = np.repeat(np.cos(twist), 8, axis=0).astype(np.float32)
    twist_sin = np.repeat(np.sin(twist), 8, axis=0).astype(np.float32)
    tables = []
    for table, axis in ((left_fwd, 1), (right_fwd, 0), (left_inv, 1), (right_inv, 0)):
        high, low = split_bf16(table)
        tables.append(jnp.asarray(np.concatenate([high, low, high], axis=axis)))
    return tuple(tables) + (jnp.asarray(twist_cos), jnp.asarray(twist_sin))


TABLES = 6


def in_two(value):
    high = value.astype(bf16)
    return high, (value - high.astype(f32)).astype(bf16)


def left_product(left, right):
    high, low = in_two(right)
    return product(left[...], jnp.concatenate([high, high, low], axis=0))


def right_product(left, right):
    high, low = in_two(left)
    return product(jnp.concatenate([high, high, low], axis=1), right[...])


def beside(parts):
    return jnp.concatenate(parts, axis=1) if len(parts) > 1 else parts[0]


def below(parts):
    return jnp.concatenate(parts, axis=0) if len(parts) > 1 else parts[0]


def to_points(xs, tables, exact):
    left, right, _, _, twist_cos, twist_sin = tables
    rows, inside = twist_cos.shape
    flat = []
    for x in xs:
        split = x.reshape(rows // 8, inside // LANES, 8, LANES)
        line = [split[:, k] for k in range(inside // LANES)]
        flat.append((jnp.concatenate(line, axis=2) if len(line) > 1 else line[0]).reshape(rows, inside))
    flat = beside(flat)
    if exact:
        flat = flat.astype(bf16)
        turned = product(left[:, : 2 * rows], jnp.concatenate([flat, flat], axis=0))
    else:
        turned = left_product(left, flat)
    cos, sin = twist_cos[...], twist_sin[...]
    both = []
    for k in range(len(xs)):
        re, im = [turned[part, k * inside : (k + 1) * inside] for part in (slice(0, rows), slice(rows, 2 * rows))]
        both.append(jnp.concatenate([re * cos + im * sin, im * cos - re * sin], axis=1))
    points = right_product(below(both), right)
    return [
        (points[k * rows : (k + 1) * rows, :inside], points[k * rows : (k + 1) * rows, inside:])
        for k in range(len(xs))
    ]


def from_points(pairs, tables):
    _, _, left, right, twist_cos, twist_sin = tables
    rows, inside = twist_cos.shape
    back = right_product(below([jnp.concatenate(pair, axis=1) for pair in pairs]), right)
    cos, sin = twist_cos[...], twist_sin[...]
    both = []
    for k in range(len(pairs)):
        re, im = back[k * rows : (k + 1) * rows, :inside], back[k * rows : (k + 1) * rows, inside:]
        both.append(jnp.concatenate([re * cos - im * sin, re * sin + im * cos], axis=0))
    found = left_product(left, beside(both))
    results = []
    for k in range(len(pairs)):
        flat = found[:, k * inside : (k + 1) * inside].reshape(rows // 8, 8, inside)
        split = [flat[:, None, :, q * LANES : (q + 1) * LANES] for q in range(inside // LANES)]
        line = jnp.concatenate(split, axis=1) if len(split) > 1 else split[0]
        results.append(line.reshape(-1, 8, LANES))
    return results


FEATURES = 48
SPAN = 512


def position_rows(length, emb_width):
    positions = np.arange(length, dtype=np.int64)
    bands = np.arange(1, (emb_width - 1) // 2 + 1, dtype=np.int64)
    angles = 2.0 * np.pi / length * ((bands[:, None] * positions[None, :]) % length)
    table = np.zeros((FEATURES, length), np.float32)
    table[0] = positions / length
    table[1 : 1 + bands.size] = np.cos(angles)
    table[1 + bands.size : emb_width] = np.sin(angles)
    table[emb_width] = 1.0
    return jnp.asarray(table)


def near_dot(left, right, left_dim, right_dim):
    left_high, left_low = in_two(left)
    right_high, right_low = in_two(right)
    return contract(
        jnp.concatenate([left_high, left_high, left_low], axis=left_dim),
        jnp.concatenate([right_high, right_low, right_high], axis=right_dim),
        left_dim,
        right_dim,
    )


def in_three(value):
    high = value.astype(bf16)
    rest = value - high.astype(f32)
    middle = rest.astype(bf16)
    return high, middle, (rest - middle.astype(f32)).astype(bf16)


def full_dot(left, right):
    a, b, c = in_three(left)
    d, e, f = in_three(right)
    return contract(
        jnp.concatenate([a, a, a, b, b, c], axis=0), jnp.concatenate([d, e, f, d, e, d], axis=0), 0, 0
    )


def sin_cos(x):
    turns = jnp.round(x * (2.0 / math.pi))
    r = ((x - turns * 1.5703125) - turns * 4.837512969970703125e-4) - turns * 7.54978995489188216e-8
    z = r * r
    sine = r + r * z * (-1.6666654611e-1 + z * (8.3321608736e-3 - z * 1.9515295891e-4))
    cosine = 1.0 - 0.5 * z + z * z * (
        4.166664568298827e-2 + z * (-1.388731625493765e-3 + z * 2.443315711809948e-5)
    )
    turn = lax.bitwise_and(turns.astype(jnp.int32), 3)
    odd = lax.bitwise_and(turn, 1) == 1
    first = jnp.where(odd, cosine, sine)
    second = jnp.where(odd, sine, cosine)
    return (
        jnp.where(turn >= 2, -first, first),
        jnp.where(jnp.logical_or(turn == 1, turn == 2), -second, second),
    )


def window_of(decay, start, shape, length):
    lane = lax.broadcasted_iota(jnp.int32, shape, 1) + start
    return jnp.exp(lane.astype(f32) * (-1.0 / length) * decay)


def filter_span(layer, start, pos, first_w, second_w, third_w, cols, decay, acts, shaped, squares):
    length = pos.shape[1]
    at = pl.ds(start, SPAN)
    act, slope = sin_cos(full_dot(first_w[layer], pos[:, at]))
    acts[layer, 0, :, at] = act
    acts[layer, 1, :, at] = slope
    act, slope = sin_cos(full_dot(second_w[layer], act) + cols[layer][:, :1])
    acts[layer, 2, :, at] = act
    acts[layer, 3, :, at] = slope
    raw = near_dot(third_w[layer], act, 0, 0)
    value = raw * window_of(decay[layer][:, :1], start, raw.shape, length)
    shaped[layer, :, at] = value
    squares[layer] += jnp.sum(value * value, axis=1, keepdims=True)


def filter_points(group, tables, shaped, squares, specs):
    layers, _, length = shaped.shape
    rows = pl.ds(pl.multiple_of(group * 8, 8), 8)
    xs = []
    for layer in range(layers):
        scale = lax.rsqrt(squares[layer, rows, :1] * (1.0 / length) + 1e-05) * length ** (-0.5)
        value = shaped[layer, rows, :] * scale
        line = [value[:, i * LANES : (i + 1) * LANES][None] for i in range(length // LANES)]
        xs.append(jnp.concatenate(line, axis=0))
    for layer, (re, im) in enumerate(to_points(xs, tables, False)):
        specs[2 * layer][group] = re
        specs[2 * layer + 1][group] = im


def filter_back_dot(layer, start, shaped, grad_taps, dots):
    at = pl.ds(start, SPAN)
    grad = taps_span(grad_taps, start)
    dots[layer] += jnp.sum(shaped[layer, :, at] * grad, axis=1, keepdims=True)


def taps_span(grad_taps, start):
    first = lax.div(start, LANES)
    pieces = []
    for i in range(SPAN // LANES):
        piece = grad_taps[:, first + i]
        pieces.append(piece.reshape(-1, LANES))
    return jnp.concatenate(pieces, axis=1)


def filter_back_span(
    layer, start, pos, second_w, third_w, decay, acts, shaped, squares, grad_taps, dots, grads
):
    length = pos.shape[1]
    at = pl.ds(start, SPAN)
    grad_third, grad_second, grad_first = grads
    mean_square = squares[layer][:, :1] * (1.0 / length)
    scale = lax.rsqrt(mean_square + 1e-05)
    cross = dots[layer][:, :1] * (1.0 / length) * scale * scale
    grad = taps_span(grad_taps, start)
    value = shaped[layer, :, at]
    grad = (grad - value * cross) * (scale * length ** (-0.5))
    grad = grad * window_of(decay[layer][:, :1], start, grad.shape, length)
    grad_third[layer] += near_dot(acts[layer, 2, :, at], grad, 1, 1)
    second = near_dot(third_w[layer], grad, 1, 0) * acts[layer, 3, :, at]
    grad_second[layer] += near_dot(acts[layer, 0, :, at], second, 1, 1)
    first = near_dot(second_w[layer], second, 1, 0) * acts[layer, 1, :, at]
    grad_first[layer] += near_dot(pos[:, at], jnp.concatenate([first, second], axis=0), 1, 1)


class Place:
    def __init__(self, ns):
        self.nz = ns // 2
        self.b = lax.axis_index("batch")
        self.s = lax.axis_index("seq")
        self.z = lax.div(self.s, 2)
        self.c = lax.rem(self.s, 2)
        self.x_peer = (lax.bitwise_xor(self.b, 1), self.s)
        self.y_peer = (lax.bitwise_xor(self.b, 2), self.s)
        self.core_peer = (self.b, lax.bitwise_xor(self.s, 1))
        self.up_peer = (self.b, lax.min(self.s + 2, ns - 1))
        self.down_peer = (self.b, lax.max(self.s - 2, 0))


def remote(src, dst, send, recv, peer):
    return pltpu.make_async_remote_copy(
        src_ref=src, dst_ref=dst, send_sem=send, recv_sem=recv, device_id=peer, device_id_type=MESH
    )


def greet(place, seq_peers):
    bar = pltpu.get_barrier_semaphore()

    def hello(peer):
        pl.semaphore_signal(bar, inc=1, device_id=peer, device_id_type=MESH)

    hello(place.x_peer)
    hello(place.y_peer)
    if seq_peers:
        ns = 2 * place.nz
        for step in range(1, ns):
            hello((place.b, lax.rem(place.s + step, ns)))
        pl.semaphore_wait(bar, 2 + ns - 1)
    else:
        hello(place.core_peer)
        pl.when(place.z + 1 < place.nz)(lambda: hello(place.up_peer))
        pl.when(place.z > 0)(lambda: hello(place.down_peer))
        ends = jnp.where(place.z == 0, 1, 0) + jnp.where(place.z == place.nz - 1, 1, 0)
        pl.semaphore_wait(bar, 5 - ends)


class Job:
    def __init__(self, arrays, results, scratch, task, plan):
        self.arrays, self.results, self.scratch, self.task = arrays, results, scratch, task
        self.plan = plan


class Runner:
    def __init__(self, tasks, plans):
        self.tasks = [[task, list(plan)] for task, plan in zip(tasks, plans, strict=True)]
        self.now = 0

    def add(self, task, steps):
        self.tasks.insert(0, [task, list(range(self.now, self.now + steps))])

    def step(self, entry):
        if next(entry[0], "end") == "end":
            self.tasks.remove(entry)

    def phase(self):
        for entry in list(self.tasks):
            while entry[1] and entry[1][0] <= self.now:
                entry[1].pop(0)
                self.step(entry)
        self.now += 1

    def finish(self):
        while any(entry[1] for entry in self.tasks):
            self.phase()
        while self.tasks:
            for entry in list(self.tasks):
                self.step(entry)


def room(items):
    total = 0
    for item in items:
        if len(item.shape) < 2 or not jnp.issubdtype(item.dtype, jnp.floating):
            continue
        size = jnp.dtype(item.dtype).itemsize
        *outer, rows, lanes = item.shape
        tile = 32 // size
        total += math.prod(outer) * -(-rows // tile) * tile * -(-lanes // LANES) * LANES * size
    return total


def fused_call(name, body, arrays, results, scratch, jobs, seq_peers, ids):
    free = VMEM_LIMIT - room([*arrays, *results, *scratch])
    if body is not None and room([item for job in jobs for item in job.scratch]) > free:
        found, _ = fused_call(name, body, arrays, results, scratch, [], seq_peers, ids)
        alone = [fused_call(name + "_job", None, [], [], [], [job], seq_peers, ids)[1][0] for job in jobs]
        return found, alone
    collective_id = next(ids)
    ns = lax.axis_size("seq")
    stages = [pltpu.VMEM(a.shape, a.dtype) for a in [*arrays, *results]]
    stages.append(pltpu.SemaphoreType.DMA((max(1, len(stages)),)))
    counts = [len(arrays)] + [len(j.arrays) for j in jobs]
    counts += [len(results)] + [len(j.results) for j in jobs]
    counts += [len(scratch)] + [len(j.scratch) for j in jobs] + [len(stages)]
    n = 1 + len(jobs)

    def kernel(*refs):
        parts, start = [], 0
        for count in counts:
            parts.append(refs[start : start + count])
            start += count
        *held, sems = parts[3 * n]
        ins, outs = held[: len(arrays)], held[len(arrays) :]
        staged = Staged(parts[0], ins, outs, parts[n], sems)
        place = Place(ns)
        greet(place, seq_peers)
        tasks = [
            job.task(place, *parts[1 + k], *parts[n + 1 + k], parts[2 * n + 1 + k])
            for k, job in enumerate(jobs)
        ]
        runner = Runner(tasks, [job.plan for job in jobs])
        if body is not None:
            body(place, runner, ins, outs, parts[2 * n], staged)
        runner.finish()
        staged.finish()

    hbm = pl.BlockSpec(memory_space=pl.ANY)
    flat = lambda pick: [item for job in jobs for item in pick(job)]
    found = pl.pallas_call(
        kernel,
        out_shape=list(results) + flat(lambda j: j.results),
        in_specs=[hbm] * sum(counts[:n]),
        out_specs=[hbm] * sum(counts[n : 2 * n]),
        scratch_shapes=list(scratch) + flat(lambda j: j.scratch) + stages,
        compiler_params=pltpu.CompilerParams(
            collective_id=collective_id, has_side_effects=True, vmem_limit_bytes=VMEM_LIMIT
        ),
        name=name,
    )(*arrays, *flat(lambda j: j.arrays))
    return found[: counts[n]], found[counts[n] :]


class Staged:
    def __init__(self, sources, ins, outs, targets, sems):
        self.loads = [pltpu.make_async_copy(a, b, sems.at[k]) for k, (a, b) in enumerate(zip(sources, ins))]
        first = len(self.loads)
        self.stores = [
            pltpu.make_async_copy(a, b, sems.at[first + k]) for k, (a, b) in enumerate(zip(outs, targets))
        ]
        self.loading = set(range(first))
        self.storing = set()
        for load in self.loads:
            load.start()

    def need(self, *which):
        for k in which:
            if k in self.loading:
                self.loading.remove(k)
                self.loads[k].wait()

    def ready(self, *which):
        for k in which:
            self.storing.add(k)
            self.stores[k].start()

    def finish(self):
        self.need(*sorted(self.loading))
        self.ready(*[k for k in range(len(self.stores)) if k not in self.storing])
        for store in self.stores:
            store.wait()


def gather_sems(nz):
    return [
        pltpu.SemaphoreType.DMA((1,)),
        pltpu.SemaphoreType.DMA((2, nz)),
        pltpu.SemaphoreType.DMA((nz,)),
        pltpu.SemaphoreType.DMA((4, nz)),
        pltpu.SemaphoreType.DMA((4, nz)),
        pltpu.SemaphoreType.DMA((4,)),
        pltpu.SemaphoreType.DMA((4,)),
    ]


def gather_task(place, src, dst, sems):
    one, chain_send, chain_recv, send, recv, core_send, core_recv = sems
    b, z, c, nz = place.b, place.z, place.c, place.nz
    bx, by, bd = place.x_peer[0], place.y_peer[0], lax.bitwise_xor(b, 3)
    local = pltpu.make_async_copy(src, dst.at[b, z, c], one.at[0])

    def chain(source, shard, up):
        row = 0 if up else 1
        peer = place.up_peer if up else place.down_peer
        return remote(source, dst.at[b, shard, c], chain_send.at[row, shard], chain_recv.at[shard], peer)

    def across(source, shard, along):
        peer = place.y_peer if along else place.x_peer
        return remote(source, dst.at[b, shard, c], send.at[along, shard], recv.at[along, shard], peer)

    def onward(shard, along):
        peer = place.y_peer if along else place.x_peer
        part = dst.at[bx if along else by, shard, c]
        return remote(part, part, send.at[2 + along, shard], recv.at[2 + along, shard], peer)

    def core(batch, i):
        part = dst.at[batch, :, c]
        return remote(part, part, core_send.at[i], core_recv.at[i], place.core_peer)

    def pass_on(shard):
        across(src, shard, 0).wait_recv()
        across(src, shard, 1).wait_recv()
        even = lax.rem(shard, 2) == 0
        pl.when(even)(lambda: onward(shard, 1).start())
        pl.when(jnp.logical_not(even))(lambda: onward(shard, 0).start())

    def pass_on_from(hop):
        if hop == 0:
            pass_on(z)
        else:
            pl.when(z - hop >= 0)(lambda: pass_on(z - hop))
            pl.when(z + hop < nz)(lambda: pass_on(z + hop))

    local.start()
    pl.when(z + 1 < nz)(lambda: chain(src, z, True).start())
    pl.when(z > 0)(lambda: chain(src, z, False).start())
    across(src, z, 0).start()
    across(src, z, 1).start()
    yield
    for hop in range(1, nz):
        below, above = z - hop, z + hop

        @pl.when(below >= 0)
        def _():
            chain(src, below, True).wait_recv()
            part = dst.at[b, below, c]
            pl.when(z + 1 < nz)(lambda: chain(part, below, True).start())
            across(part, below, 0).start()
            across(part, below, 1).start()

        @pl.when(above < nz)
        def _():
            chain(src, above, False).wait_recv()
            part = dst.at[b, above, c]
            pl.when(z > 0)(lambda: chain(part, above, False).start())
            across(part, above, 0).start()
            across(part, above, 1).start()

        pass_on_from(hop - 1)
        yield
    local.wait()
    core(b, 0).start()
    pass_on_from(nz - 1)
    core(bx, 1).start()
    core(by, 2).start()
    yield
    for shard in range(nz):
        onward(shard, 1 - shard % 2).wait_recv()
    core(bd, 3).start()
    yield
    for hop in range(nz):
        pl.when(jnp.logical_and(z >= hop, z + 1 < nz))(lambda: chain(src, z - hop, True).wait_send())
        pl.when(jnp.logical_and(z + hop < nz, z > 0))(lambda: chain(src, z + hop, False).wait_send())
    for shard in range(nz):
        across(src, shard, 0).wait_send()
        across(src, shard, 1).wait_send()
        onward(shard, 1 - shard % 2).wait_send()
    for i in range(4):
        core(b, i).wait()
    yield


def gather_job(array, layer, plan):
    nz = lax.axis_size("seq") // 2
    result = jax.ShapeDtypeStruct((4, nz, 2) + array.shape[1:], array.dtype)
    task = lambda place, src, dst, sems: gather_task(place, src.at[layer], dst, sems)
    return Job([array], [result], gather_sems(nz), task, plan)


def column_task(place, src, dst, sems):
    one, chain_send, chain_recv = sems
    z, nz = place.z, place.nz
    local = pltpu.make_async_copy(src, dst.at[z], one.at[0])

    def chain(source, shard, up):
        row = 0 if up else 1
        peer = place.up_peer if up else place.down_peer
        return remote(source, dst.at[shard], chain_send.at[row, shard], chain_recv.at[shard], peer)

    local.start()
    pl.when(z + 1 < nz)(lambda: chain(src, z, True).start())
    pl.when(z > 0)(lambda: chain(src, z, False).start())
    yield
    for hop in range(1, nz):
        below, above = z - hop, z + hop

        @pl.when(below >= 0)
        def _():
            chain(src, below, True).wait_recv()
            pl.when(z + 1 < nz)(lambda: chain(dst.at[below], below, True).start())

        @pl.when(above < nz)
        def _():
            chain(src, above, False).wait_recv()
            pl.when(z > 0)(lambda: chain(dst.at[above], above, False).start())

        yield
    for hop in range(nz):
        pl.when(jnp.logical_and(z >= hop, z + 1 < nz))(lambda: chain(src, z - hop, True).wait_send())
        pl.when(jnp.logical_and(z + hop < nz, z > 0))(lambda: chain(src, z + hop, False).wait_send())
    local.wait()
    yield


def column_job(array, layer, plan):
    nz = lax.axis_size("seq") // 2
    result = jax.ShapeDtypeStruct((nz,) + array.shape[1:], array.dtype)
    sems = [
        pltpu.SemaphoreType.DMA((1,)),
        pltpu.SemaphoreType.DMA((2, nz)),
        pltpu.SemaphoreType.DMA((nz,)),
    ]
    task = lambda place, src, dst, sems: column_task(place, src.at[layer], dst, sems)
    return Job([array], [result], sems, task, plan)


def plane_task(place, src, dst, sems):
    one, send, recv, core_send, core_recv = sems
    b, c, nz = place.b, place.c, place.nz
    bx, by, bd = place.x_peer[0], place.y_peer[0], lax.bitwise_xor(b, 3)
    half = nz // 2
    local = pltpu.make_async_copy(src, dst.at[b, :, c], one.at[0])
    over_x = remote(src, dst.at[b, :, c], send.at[0], recv.at[0], place.x_peer)
    over_y = remote(src, dst.at[b, :, c], send.at[1], recv.at[1], place.y_peer)
    low, high = pl.ds(0, half), pl.ds(half, nz - half)
    far_y = remote(dst.at[bx, low, c], dst.at[bx, low, c], send.at[2], recv.at[2], place.y_peer)
    far_x = remote(dst.at[by, high, c], dst.at[by, high, c], send.at[3], recv.at[3], place.x_peer)

    def core(source, batch, i):
        return remote(source, dst.at[batch, :, c], core_send.at[i], core_recv.at[i], place.core_peer)

    over_x.start()
    over_y.start()
    core(src, b, 0).start()
    local.start()
    yield
    over_x.wait_recv()
    far_y.start()
    over_y.wait_recv()
    far_x.start()
    core(dst.at[bx, :, c], bx, 1).start()
    core(dst.at[by, :, c], by, 2).start()
    yield
    far_y.wait_recv()
    far_x.wait_recv()
    core(dst.at[bd, :, c], bd, 3).start()
    yield
    for copy in (over_x, over_y, far_y, far_x):
        copy.wait_send()
    local.wait()
    for i in range(4):
        core(src, b, i).wait()
    yield


def plane_job(array, plan):
    nz = array.shape[0]
    result = jax.ShapeDtypeStruct((4, nz, 2) + array.shape[1:], array.dtype)
    sems = [pltpu.SemaphoreType.DMA((1,))] + [pltpu.SemaphoreType.DMA((4,))] * 4
    return Job([array], [result], sems, plane_task, plan)


def reduce_scratch(nz, shape, dtype):
    half = (nz,) + shape
    return [
        pltpu.VMEM((4,) + half, dtype),
        pltpu.VMEM((4,) + half, dtype),
        pltpu.VMEM((5,) + half, dtype),
        pltpu.VMEM(shape, f32),
        pltpu.SemaphoreType.DMA((1,)),
        pltpu.SemaphoreType.DMA((3, nz)),
        pltpu.SemaphoreType.DMA((5, nz)),
        pltpu.SemaphoreType.DMA((5, nz)),
    ]


def far_first(place):
    nz = place.nz
    tables = [sorted(range(nz), key=lambda k: (-abs(k - z), k)) for z in range(nz)]
    order = []
    for j in range(nz):
        shard = jnp.int32(tables[0][j])
        for z in range(1, nz):
            shard = jnp.where(place.z == z, tables[z][j], shard)
        order.append(shard)
    return order


def reduce_task(place, src, out, scratch):
    acc, other, box, total, one, near, send, recv = scratch
    kind = acc.dtype
    b, z, c, nz = place.b, place.z, place.c, place.nz
    bx, by, bd = place.x_peer[0], place.y_peer[0], lax.bitwise_xor(b, 3)
    far, via_x, via_y, up, down = range(5)
    order = far_first(place)
    halves = [range(0, nz // 2), range(nz // 2, nz)]

    def add(target, shard, *lanes):
        value = acc[target, shard].astype(f32)
        for lane in lanes:
            value += box[lane, shard].astype(f32)
        acc[target, shard] = value.astype(kind)

    def move(part, shard, lane, peer):
        return remote(acc.at[part, shard], box.at[lane, shard], send.at[lane, shard], recv.at[lane, shard], peer)

    def mine(shard):
        return pltpu.make_async_copy(src.at[:, shard, c], acc.at[:, shard], near.at[0, shard])

    def core(shard):
        return remote(src.at[:, shard, 1 - c], other.at[:, shard], near.at[1, shard], near.at[2, shard], place.core_peer)

    for shard in order:
        core(shard).start()
        mine(shard).start()
    yield
    for half in halves:
        for j in half:
            shard = order[j]
            mine(shard).wait()
            core(shard).wait_recv()

            @pl.loop(0, 4)
            def _(part):
                acc[part, shard] = (
                    acc[part, shard].astype(f32) + other[part, shard].astype(f32)
                ).astype(kind)

            if j % 2 == 0:
                move(bd, shard, far, place.x_peer).start()
                move(bx, shard, via_x, place.x_peer).start()
            else:
                move(bd, shard, far, place.y_peer).start()
                move(by, shard, via_y, place.y_peer).start()
        yield
    for half in halves:
        for j in half:
            shard = order[j]
            move(bd, shard, far, place.x_peer).wait_recv()
            if j % 2 == 0:
                add(by, shard, far)
                move(by, shard, via_y, place.y_peer).start()
            else:
                add(bx, shard, far)
                move(bx, shard, via_x, place.x_peer).start()
        yield
    for half in halves:
        for j in half:
            shard = order[j]
            move(bx, shard, via_x, place.x_peer).wait_recv()
            move(by, shard, via_y, place.y_peer).wait_recv()
            add(b, shard, via_x, via_y)

            @pl.when(z < shard)
            def _():
                @pl.when(z > 0)
                def _():
                    move(b, shard, up, place.up_peer).wait_recv()
                    add(b, shard, up)

                move(b, shard, up, place.up_peer).start()

            @pl.when(z > shard)
            def _():
                @pl.when(z + 1 < nz)
                def _():
                    move(b, shard, down, place.down_peer).wait_recv()
                    add(b, shard, down)

                move(b, shard, down, place.down_peer).start()

        yield
    total[...] = acc[b, z].astype(f32)

    @pl.when(z > 0)
    def _():
        move(b, z, up, place.up_peer).wait_recv()
        total[...] += box[up, z].astype(f32)

    @pl.when(z + 1 < nz)
    def _():
        move(b, z, down, place.down_peer).wait_recv()
        total[...] += box[down, z].astype(f32)

    result = pltpu.make_async_copy(total, out, one.at[0])
    result.start()
    for shard in range(nz):
        core(shard).wait_send()
        for lane in (far, via_x, via_y):
            move(b, shard, lane, place.x_peer).wait_send()
        pl.when(z < shard)(lambda: move(b, shard, up, place.up_peer).wait_send())
        pl.when(z > shard)(lambda: move(b, shard, down, place.down_peer).wait_send())
    result.wait()
    yield


def reduce_job(array, plan):
    nz = lax.axis_size("seq") // 2
    shape = array.shape[1:]
    return Job(
        [array.reshape((4, nz, 2) + shape)],
        [jax.ShapeDtypeStruct(shape, f32)],
        reduce_scratch(nz, shape, array.dtype),
        reduce_task,
        plan,
    )


def total_scratch(nz, shape, shared):
    return [
        pltpu.VMEM((3,) + shape, f32),
        pltpu.VMEM((2,) + shape, f32),
        pltpu.VMEM((2, nz, shared, LANES), f32),
        pltpu.SemaphoreType.DMA((2, 3)),
        pltpu.SemaphoreType.DMA((2, nz)),
    ]


def total_task(place, src, out, scratch):
    box, sums, lines, pair, chain = scratch
    z, c, nz = place.z, place.c, place.nz
    rows = src.shape[0]
    shared = lines.shape[2]
    tail = pl.ds(rows - shared, shared)

    def swap(source, dst, i, peer):
        return remote(source, dst, pair.at[0, i], pair.at[1, i], peer)

    first = swap(src, box.at[0], 0, place.x_peer)
    first.start()
    yield
    first.wait()
    sums[0] = src[...] + box[0]
    second = swap(sums.at[0], box.at[1], 1, place.y_peer)
    second.start()
    yield
    second.wait()
    sums[1] = sums[0] + box[1]
    third = swap(sums.at[1, tail], box.at[2, tail], 2, place.core_peer)
    third.start()
    yield
    third.wait()
    lines[0, z] = sums[1, tail] + box[2, tail]

    def along(step):
        peer = lax.rem(z + step, nz)
        return remote(lines.at[0, z], lines.at[1, z], chain.at[0, step], chain.at[1, step], (place.b, 2 * peer + c))

    for step in range(1, nz):
        along(step).start()
    lines[1, z] = lines[0, z]
    yield
    for step in range(1, nz):
        along(step).wait_recv()
    value = lines[1, 0]
    for shard in range(1, nz):
        value = value + lines[1, shard]
    out[: rows - shared] = sums[1, : rows - shared]
    out[tail] = value
    for step in range(1, nz):
        along(step).wait_send()
    yield


def prepare(jobs, pos_rows, first_w, second_w, third_w, cols, decay, tables, ids):
    layers, hidden, own = third_w.shape
    length = pos_rows.shape[1]
    rows = (own // 8,) + tables[4].shape
    results = [
        jax.ShapeDtypeStruct((layers, 4, hidden, length), f32),
        jax.ShapeDtypeStruct((layers, own, length), f32),
        jax.ShapeDtypeStruct((layers, own, LANES), f32),
    ] + [jax.ShapeDtypeStruct(rows, f32)] * (2 * layers)

    def body(place, runner, ins, outs, scratch, staged):
        pos, first, second, third, bias, rate = ins[:6]
        factors = ins[6:]
        acts, shaped, squares = outs[:3]
        specs = outs[3:]
        spans, groups = length // SPAN, own // 8
        squares[...] = jnp.zeros_like(squares)
        staged.need(0, 1, 2, 3, 4, 5)
        for part in range(8):
            runner.phase()

            @pl.loop(part * spans // 8, (part + 1) * spans // 8)
            def _(i):
                for layer in range(layers):
                    filter_span(
                        layer, pl.multiple_of(i * SPAN, SPAN), pos, first, second, third, bias, rate, acts, shaped, squares
                    )

        staged.ready(0, 1, 2)
        staged.need(*range(6, 6 + TABLES))
        for part in range(6):
            runner.phase()

            @pl.loop(part * groups // 6, (part + 1) * groups // 6)
            def _(group):
                filter_points(group, factors, shaped, squares, specs)

    return fused_call(
        "prepare",
        body,
        [pos_rows, first_w, second_w, third_w, cols, decay, *tables],
        results,
        [],
        jobs,
        False,
        ids,
    )


def last(jobs, pos_rows, second_w, third_w, decay, kept, grad_taps, ids):
    layers, hidden, own = third_w.shape
    length = pos_rows.shape[1]
    nz = lax.axis_size("seq") // 2
    each, shared = hidden + 8, FEATURES + hidden
    payload = jax.ShapeDtypeStruct((layers * (each + shared), LANES), f32)

    def body(place, runner, ins, outs, scratch, staged):
        pos, second, third, rate, acts, shaped, squares = ins[:7]
        taps = ins[7:]
        dots, grad_third, grad_second, grad_first, payload_in = scratch[:5]
        for ref in (dots, grad_third, grad_second, grad_first, payload_in):
            ref[...] = jnp.zeros_like(ref)
        runner.phase()
        spans = length // SPAN
        staged.need(5, *range(7, 7 + layers))

        @pl.loop(0, spans)
        def _(i):
            for layer in range(layers):
                filter_back_dot(layer, pl.multiple_of(i * SPAN, SPAN), shaped, taps[layer], dots)

        staged.need(0, 1, 2, 3, 4, 6)
        for part in range(8):
            runner.phase()

            @pl.loop(part * spans // 8, (part + 1) * spans // 8)
            def _(i):
                for layer in range(layers):
                    filter_back_span(
                        layer, pl.multiple_of(i * SPAN, SPAN), pos, second, third, rate, acts, shaped, squares,
                        taps[layer], dots, (grad_third, grad_second, grad_first)
                    )

        for layer in range(layers):
            start = layer * each
            payload_in[start : start + hidden, :own] = grad_third[layer]
            lag = taps[layer][:, 0].reshape(own, LANES)
            pick = jnp.where(lax.broadcasted_iota(jnp.int32, (8, LANES), 1) == 0, 1.0, 0.0)
            payload_in[start + hidden : start + each, :own] = near_dot(pick, lag, 1, 1)
            start = layers * each + layer * shared
            payload_in[start : start + FEATURES, : 2 * hidden] = grad_first[layer]
            payload_in[start + FEATURES : start + shared, :hidden] = grad_second[layer]
        runner.add(total_task(place, payload_in, outs[0], scratch[5:]), 4)

    return fused_call(
        "last",
        body,
        [pos_rows, second_w, third_w, decay, *kept, *grad_taps],
        [payload],
        [
            pltpu.VMEM((layers, own, LANES), f32),
            pltpu.VMEM((layers, hidden, own), f32),
            pltpu.VMEM((layers, hidden, hidden), f32),
            pltpu.VMEM((layers, FEATURES, 2 * hidden), f32),
            pltpu.VMEM(payload.shape, f32),
        ]
        + total_scratch(nz, payload.shape, layers * shared),
        jobs,
        True,
        ids,
    )


def conv_lanes(value, rim_near, rim_far):
    lane = lax.broadcasted_iota(jnp.int32, value.shape, 1)
    near = jnp.where(lane == 0, rim_near, pltpu.roll(value, 1, 1))
    far = jnp.where(lane == 0, rim_far, jnp.where(lane == 1, rim_near, pltpu.roll(value, 2, 1)))
    return near, far


def rows_of(ref, stream, block, count):
    value = ref[stream, pl.ds(block, count)].astype(f32)
    return value.reshape(-1, value.shape[-1])


def short_out(mixed, conv, rim, stream, block, count=1):
    value = rows_of(mixed, stream, block, count)
    side, edge = rows_of(conv, stream, block, count), rows_of(rim, stream, block, count)
    near, far = conv_lanes(value, edge[:, 1:2], edge[:, 0:1])
    return side[:, 0:1] * far + side[:, 1:2] * near + side[:, 2:3] * value


def by_blocks(nblocks, most):
    return max(k for k in range(1, most + 1) if nblocks % k == 0)


def edge_scratch(streams, nblocks, chans):
    rows = pltpu.VMEM((streams, 16, nblocks * chans), f32)
    return [rows, rows, pltpu.VMEM((streams, nblocks, chans, LANES), f32), pltpu.SemaphoreType.DMA((2,))]


def edge_copy(place, scratch, to_right):
    out, came, _, sems = scratch
    ns = 2 * place.nz
    peer = lax.min(place.s + 1, ns - 1) if to_right else lax.max(place.s - 1, 0)
    return remote(out, came, sems.at[0], sems.at[1], (place.b, peer))


def send_edge(place, scratch, tiles_of, first, to_right):
    out = scratch[0]
    row = lax.broadcasted_iota(jnp.int32, (16, LANES), 0)
    lane = lax.broadcasted_iota(jnp.int32, (16, LANES), 1)
    pick = jnp.where(jnp.logical_and(lane == row + first, row < 2), 1.0, 0.0).astype(bf16)
    for stream in range(out.shape[0]):
        high, low = in_two(tiles_of(stream).reshape(-1, LANES))
        out[stream] = contract(
            jnp.concatenate([pick, pick], axis=1), jnp.concatenate([high, low], axis=1), 1, 1
        )
    has = place.s + 1 < 2 * place.nz if to_right else place.s > 0
    pl.when(has)(lambda: edge_copy(place, scratch, to_right).start())


def take_edge(place, scratch, to_right):
    _, came, cols, _ = scratch
    _, nblocks, chans, _ = cols.shape
    comes = place.s > 0 if to_right else place.s + 1 < 2 * place.nz
    sends = place.s + 1 < 2 * place.nz if to_right else place.s > 0

    @pl.when(comes)
    def _():
        edge_copy(place, scratch, to_right).wait_recv()
        row = lax.broadcasted_iota(jnp.int32, (16, LANES), 0)
        lane = lax.broadcasted_iota(jnp.int32, (16, LANES), 1)
        spread = jnp.where(jnp.logical_and(lane == row, row < 2), 1.0, 0.0).astype(bf16)
        both = jnp.concatenate([spread, spread], axis=0)
        for stream in range(cols.shape[0]):
            pair = jnp.concatenate(in_two(came[stream]), axis=0)
            cols[stream] = contract(pair, both, 0, 0).reshape(nblocks, chans, LANES)

    @pl.when(jnp.logical_not(comes))
    def _():
        cols[...] = jnp.zeros_like(cols)

    pl.when(sends)(lambda: edge_copy(place, scratch, to_right).wait_send())


def sub_rows(chans):
    return 16 if chans % 16 == 0 else chans


def mix_body(place, runner, ins, outs, scratch, staged, layer):
    mixed, conv, spec_re, spec_im, skip = ins[:5]
    tables = ins[5:]
    long_out, gated, sig_re, sig_im, rim = outs
    signal, chan_in, chan_out, tok_in, send, recv = scratch[:6]
    edge = [scratch[6], scratch[7], rim, scratch[8]]
    toks = mixed.shape[3]
    ns, groups, quarters, chans, _ = signal.shape
    take = sub_rows(chans)

    def to_chan(g, step):
        peer = lax.rem(place.s + step, ns)
        return remote(
            signal.at[peer, g],
            chan_in.at[g, pl.ds(place.s * quarters, quarters)],
            send.at[0, g, step],
            recv.at[0, g, step],
            (place.b, peer),
        )

    def send_pieces(step, first, value):
        peer = lax.rem(place.s + step, ns)
        count = value.shape[0] // chans
        for k in range(count):
            for q in range(quarters):
                piece = value[k * chans : (k + 1) * chans, q * LANES : (q + 1) * LANES]
                signal[peer, first + k, q] = piece

        @pl.when(step < ns)
        def _():
            for k in range(count):
                to_chan(first + k, step).start()

        @pl.when(step == ns)
        def _():
            for k in range(count):
                for q in range(quarters):
                    chan_in[first + k, place.s * quarters + q] = signal[peer, first + k, q]

    def to_tok(g, step):
        peer = lax.rem(place.s + step, ns)
        return remote(
            chan_out.at[g, pl.ds(peer * quarters, quarters)],
            tok_in.at[place.s, g],
            send.at[1, g, step],
            recv.at[1, g, step],
            (place.b, peer),
        )

    staged.need(0)
    send_edge(place, edge, lambda k: mixed[k, :, :, toks - LANES :].astype(f32), LANES - 2, True)
    runner.phase()
    take_edge(place, edge, True)
    staged.ready(4)
    staged.need(1)
    share = by_blocks(groups, 3)
    for first in range(0, groups, share):

        @pl.loop(1, ns + 1)
        def _(step):
            peer = lax.rem(place.s + step, ns)
            block = peer * groups + first
            value = short_out(mixed, conv, rim, 1, block, share) * short_out(mixed, conv, rim, 2, block, share)
            send_pieces(step, first, value.astype(bf16))

    staged.need(2, 3, 4, *range(5, 5 + TABLES))
    runner.phase()
    for g in range(groups):

        @pl.loop(1, ns)
        def _(step):
            to_chan(g, step).wait_recv()

        @pl.loop(0, chans // take)
        def _(i):
            at = pl.ds(pl.multiple_of(i * take, take), take)
            block = chan_in[g, :, at, :].astype(f32)
            base = (g * chans) // 8 + i * (take // 8)
            xs = [block[:, 8 * j : 8 * j + 8, :] for j in range(take // 8)]
            products = []
            for j, (re, im) in enumerate(to_points(xs, tables, True)):
                sig_re[base + j] = re
                sig_im[base + j] = im
                tap_re, tap_im = spec_re[base + j], spec_im[base + j]
                products.append((re * tap_re - im * tap_im, re * tap_im + im * tap_re))
            found = from_points(products, tables)
            parts = [y + skip[layer, base + j][None] * xs[j] for j, y in enumerate(found)]
            chan_out[g, :, at, :] = jnp.concatenate(parts, axis=1).astype(bf16)

        @pl.loop(1, ns)
        def _(step):
            to_tok(g, step).start()

        for q in range(quarters):
            tok_in[place.s, g, q] = chan_out[g, place.s * quarters + q]
        runner.phase()

    staged.ready(2, 3)
    for g in range(groups):

        @pl.loop(1, ns)
        def _(step):
            to_tok(g, step).wait_recv()

        @pl.loop(0, ns, unroll=4)
        def _(owner):
            block = owner * groups + g
            value = jnp.concatenate([tok_in[owner, g, q] for q in range(quarters)], axis=1)
            long_out[block] = value
            gated[block] = (short_out(mixed, conv, rim, 0, block) * value.astype(f32)).astype(bf16)

        if g % 2:
            runner.phase()

    for g in range(groups):

        @pl.loop(1, ns)
        def _(step):
            to_chan(g, step).wait_send()
            to_tok(g, step).wait_send()


def mixer_scratch(ns, groups, quarters, chans):
    pieces = pltpu.VMEM((ns, groups, quarters, chans, LANES), bf16)
    lines = pltpu.VMEM((groups, ns * quarters, chans, LANES), bf16)
    sems = pltpu.SemaphoreType.DMA((2, groups, ns))
    return [pieces, lines, lines, pieces, sems, sems]


def mix(jobs, layer, mixed, conv, spec, skip, tables, ids):
    ns = lax.axis_size("seq")
    _, nblocks, chans, toks = mixed.shape
    groups, quarters = nblocks // ns, toks // LANES
    rows = jax.ShapeDtypeStruct((groups * chans // 8,) + tables[4].shape, f32)
    tokens = jax.ShapeDtypeStruct((nblocks, chans, toks), bf16)
    edges = edge_scratch(3, nblocks, chans)
    return fused_call(
        "mix",
        functools.partial(mix_body, layer=layer),
        [mixed, conv, *spec, skip, *tables],
        [tokens, tokens, rows, rows, jax.ShapeDtypeStruct(conv.shape, f32)],
        mixer_scratch(ns, groups, quarters, chans) + edges[:2] + edges[3:],
        jobs,
        True,
        ids,
    )


def unmix_body(place, runner, ins, outs, scratch, staged, layer):
    mixed, conv, rim, long_out, grad_gated, spec_re, spec_im, sig_re, sig_im, skip = ins[:10]
    tables = ins[10:]
    grad_taps, grad_mixed, grad_conv = outs
    pull, chan_in, chan_out, tok_in, send, recv, grad_short, partials = scratch[:8]
    edge = scratch[8:]
    toks = mixed.shape[3]
    runner.phase()
    staged.need(0, 1, 2, 4)
    ns, groups, quarters, chans, _ = pull.shape
    take = sub_rows(chans)

    def to_chan(g, step):
        peer = lax.rem(place.s + step, ns)
        return remote(
            pull.at[peer, g],
            chan_in.at[g, pl.ds(place.s * quarters, quarters)],
            send.at[0, g, step],
            recv.at[0, g, step],
            (place.b, peer),
        )

    def send_pieces(step, first, value):
        peer = lax.rem(place.s + step, ns)
        count = value.shape[0] // chans
        for k in range(count):
            for q in range(quarters):
                piece = value[k * chans : (k + 1) * chans, q * LANES : (q + 1) * LANES]
                pull[peer, first + k, q] = piece

        @pl.when(step < ns)
        def _():
            for k in range(count):
                to_chan(first + k, step).start()

        @pl.when(step == ns)
        def _():
            for k in range(count):
                for q in range(quarters):
                    chan_in[first + k, place.s * quarters + q] = pull[peer, first + k, q]

    def to_tok(g, step):
        peer = lax.rem(place.s + step, ns)
        return remote(
            chan_out.at[g, pl.ds(peer * quarters, quarters)],
            tok_in.at[place.s, g],
            send.at[1, g, step],
            recv.at[1, g, step],
            (place.b, peer),
        )

    share = by_blocks(groups, 3)
    for first in range(0, groups, share):

        @pl.loop(1, ns + 1)
        def _(step):
            block = lax.rem(place.s + step, ns) * groups + first
            gated = grad_gated[pl.ds(block, share)].reshape(share * chans, toks)
            send_pieces(step, first, (gated * short_out(mixed, conv, rim, 0, block, share)).astype(bf16))

    staged.need(5, 6, 7, 8, 9, *range(10, 10 + TABLES))
    runner.phase()
    for g in range(groups):

        @pl.loop(1, ns)
        def _(step):
            to_chan(g, step).wait_recv()

        @pl.loop(0, chans // take)
        def _(i):
            at = pl.ds(pl.multiple_of(i * take, take), take)
            block = chan_in[g, :, at, :].astype(f32)
            base = (g * chans) // 8 + i * (take // 8)
            count = take // 8
            xs = [block[:, 8 * j : 8 * j + 8, :] for j in range(count)]
            signals, taps = [], []
            for j, (re, im) in enumerate(to_points(xs, tables, True)):
                tap_re, tap_im = spec_re[base + j], spec_im[base + j]
                own_re, own_im = sig_re[base + j], sig_im[base + j]
                signals.append((tap_re * re + tap_im * im, tap_re * im - tap_im * re))
                taps.append((own_re * re + own_im * im, own_re * im - own_im * re))
            found = from_points(signals + taps, tables)
            parts = [found[j] + skip[layer, base + j][None] * xs[j] for j in range(count)]
            for j in range(count):
                grad_taps[base + j] = found[count + j]
            chan_out[g, :, at, :] = jnp.concatenate(parts, axis=1).astype(bf16)

        @pl.loop(1, ns)
        def _(step):
            to_tok(g, step).start()

        for q in range(quarters):
            tok_in[place.s, g, q] = chan_out[g, place.s * quarters + q]
        runner.phase()

    staged.ready(0)
    staged.need(3)

    @pl.loop(0, ns * groups, unroll=4)
    def _(block):
        grad_short[0, block] = grad_gated[block] * long_out[block].astype(f32)

    for g in range(groups):

        @pl.loop(1, ns)
        def _(step):
            to_tok(g, step).wait_recv()

        @pl.loop(0, ns, unroll=4)
        def _(owner):
            block = owner * groups + g
            value = jnp.concatenate(
                [tok_in[owner, g, q] for q in range(quarters)], axis=1
            ).astype(f32)
            grad_short[1, block] = value * short_out(mixed, conv, rim, 2, block)
            grad_short[2, block] = value * short_out(mixed, conv, rim, 1, block)

        if g % 2:
            runner.phase()

    send_edge(place, edge, lambda k: grad_short[k, :, :, :LANES], 0, False)
    many = by_blocks(ns * groups, 4)
    ones = jnp.ones((2 * LANES, LANES), bf16)
    for stream in range(3):

        @pl.loop(0, ns * groups // many, unroll=2)
        def _(i):
            at = pl.ds(i * many, many)
            grad = rows_of(grad_short, stream, i * many, many)
            value = rows_of(mixed, stream, i * many, many)
            side = rows_of(rim, stream, i * many, many)
            near, far = conv_lanes(value, side[:, 1:2], side[:, 0:1])
            for k, moved in enumerate((far, near, value)):
                terms = grad * moved
                partial = terms[:, :LANES]
                for q in range(1, quarters):
                    partial += terms[:, q * LANES : (q + 1) * LANES]
                partials[k, at] = partial.reshape(many, chans, LANES)

        sums = [
            product(jnp.concatenate(in_two(partials[k].reshape(-1, LANES)), axis=1), ones)
            for k in range(3)
        ]
        lane = lax.broadcasted_iota(jnp.int32, sums[0].shape, 1)
        found = jnp.where(lane == 0, sums[0], jnp.where(lane == 1, sums[1], sums[2]))
        grad_conv[stream] = found.reshape(ns * groups, chans, LANES)
    staged.ready(2)
    runner.phase()
    take_edge(place, edge, False)
    edge_cols = edge[2]
    for stream in range(3):

        @pl.loop(0, ns * groups // many, unroll=2)
        def _(i):
            value = rows_of(grad_short, stream, i * many, many)
            side, after = rows_of(conv, stream, i * many, many), rows_of(edge_cols, stream, i * many, many)
            lane = lax.broadcasted_iota(jnp.int32, value.shape, 1)
            near = jnp.where(lane == toks - 1, after[:, 0:1], pltpu.roll(value, toks - 1, 1))
            far = jnp.where(
                lane == toks - 1,
                after[:, 1:2],
                jnp.where(lane == toks - 2, after[:, 0:1], pltpu.roll(value, toks - 2, 1)),
            )
            total = side[:, 2:3] * value + side[:, 1:2] * near + side[:, 0:1] * far
            grad_mixed[stream, pl.ds(i * many, many)] = total.astype(bf16).reshape(many, chans, toks)

    for g in range(groups):

        @pl.loop(1, ns)
        def _(step):
            to_chan(g, step).wait_send()
            to_tok(g, step).wait_send()


def unmix(jobs, layer, mixed, conv, rim, long_out, grad_gated, spec, sig, skip, tables, ids):
    ns = lax.axis_size("seq")
    _, nblocks, chans, toks = mixed.shape
    groups, quarters = nblocks // ns, toks // LANES
    return fused_call(
        "unmix",
        functools.partial(unmix_body, layer=layer),
        [mixed, conv, rim, long_out, grad_gated, *spec, *sig, skip, *tables],
        [
            jax.ShapeDtypeStruct((groups * chans // 8, ns * quarters, 8, LANES), f32),
            jax.ShapeDtypeStruct(mixed.shape, bf16),
            jax.ShapeDtypeStruct(conv.shape, f32),
        ],
        mixer_scratch(ns, groups, quarters, chans)
        + [pltpu.VMEM(mixed.shape, f32), pltpu.VMEM(conv.shape, f32)]
        + edge_scratch(3, nblocks, chans),
        jobs,
        True,
        ids,
    )


def on_device(
    tokens,
    cotangent,
    norm_gains,
    w_in,
    short_conv,
    w_out,
    w_fc,
    w_proj,
    filt_w1,
    filt_b1,
    filt_w2,
    filt_b2,
    filt_w3,
    skip_gain,
    decay_rate,
):
    layers, _, width3 = w_in.shape
    width = width3 // 3
    ns = lax.axis_size("seq")
    devices = lax.axis_size("batch") * ns
    stream = tokens[0].astype(f32)
    toks = stream.shape[0]
    length = toks * ns
    own_chans = width // ns
    chans = 16 if own_chans % 16 == 0 else own_chans
    groups = own_chans // chans
    nblocks = ns * groups
    blocked = (3, nblocks, chans)
    tables = transform_tables(length)
    pos_rows = position_rows(length, filt_w1.shape[1])

    gain_cols, conv_cols = norm_gains.shape[2], short_conv.shape[2]
    small = jnp.concatenate(
        [
            jnp.pad(norm_gains.reshape(2 * layers, gain_cols).astype(f32), ((0, 0), (0, LANES - gain_cols))),
            jnp.pad(short_conv.reshape(3 * layers, conv_cols).astype(f32), ((0, 0), (0, LANES - conv_cols))),
        ],
        axis=0,
    )
    small = jnp.pad(small, ((0, -small.shape[0] % 8), (0, 0)))[None]

    first_w = jnp.pad(
        jnp.concatenate([filt_w1, filt_b1[:, None]], axis=1),
        ((0, 0), (0, FEATURES - filt_w1.shape[1] - 1), (0, 0)),
    )
    cols = jnp.broadcast_to(filt_b2[:, :, None], filt_b2.shape + (LANES,))
    decay = jnp.broadcast_to(decay_rate[:, :, None], (layers, own_chans, LANES))
    skips = jnp.broadcast_to(
        skip_gain.reshape(layers, -1, 8, 1), (layers, own_chans // 8, 8, LANES)
    )

    mats = (w_in, w_out, w_fc, w_proj)
    jobs = [gather_job(small, 0, GATHER_PLANS[0])]
    jobs += [gather_job(mat, 0, plan) for mat, plan in zip(mats, GATHER_PLANS[1:])]
    jobs += [
        column_job(mat, layer, plan)
        for layer in range(1, layers)
        for mat, plan in zip(mats, COLUMN_PLANS)
    ]
    ids = itertools.count()
    sets = [list(range(layers))] if length <= 8192 else [[layer] for layer in range(layers)]
    kept, specs = [], []
    for part in sets:
        of = slice(part[0], part[-1] + 1)
        filters, found = prepare(
            jobs, pos_rows, first_w[of], filt_w2[of], filt_w3[of], cols[of], decay[of], tables, ids
        )
        kept.append(filters[:3])
        specs += [filters[3 + 2 * k : 5 + 2 * k] for k in range(len(part))]
        gathered = found if part is sets[0] else gathered
        jobs = []
    small_all = gathered[0].reshape(devices, -1, LANES)
    gains = jnp.swapaxes(small_all[:, : 2 * layers, :gain_cols], 0, 1).reshape(layers, 2, width)
    convs = jnp.swapaxes(
        small_all[:, 2 * layers : 5 * layers, :conv_cols], 0, 1
    ).reshape(layers, 3, width3)
    conv_cols_of = [
        jnp.pad(convs[layer].T, ((0, 0), (0, LANES - 3))).reshape(blocked + (LANES,))
        for layer in range(layers)
    ]
    plain = lambda parts: parts.reshape(-1, parts.shape[-1])
    weights = {(i, 0): plain(gathered[1 + i]) for i in range(4)}
    columns = {
        (i, layer): gathered[1 + 4 * layer + i] for layer in range(1, layers) for i in range(4)
    }

    def plane_jobs(layer):
        keys = [(3, layer)] if layer else []
        keys = [key for key in keys + [(0, layer + 1), (1, layer + 1), (2, layer + 1)] if key in columns]
        return keys, [plane_job(columns[key], plan) for key, plan in zip(keys, PLANE_PLANS)]

    saved = []
    for layer in range(layers):
        in_mat = weights[0, layer]
        normed, inv_std = layer_norm_parts(stream)
        norm_in = (normed * gains[layer, 0]).astype(bf16)
        mixed = contract(in_mat, norm_in, 0, 1).astype(bf16)
        mixed = mixed.reshape(blocked + (toks,))
        keys, jobs = plane_jobs(layer)
        (long_out, gated, sig_re, sig_im, rim), arrived = mix(
            jobs, layer, mixed, conv_cols_of[layer], specs[layer], skips, tables, ids
        )
        weights.update({key: plain(parts) for key, parts in zip(keys, arrived)})
        out_mat, fc_mat, proj_mat = (weights[i, layer] for i in (1, 2, 3))
        gated = gated.reshape(width, toks)
        middle = stream + contract(gated, out_mat, 0, 0)
        normed_mid, inv_mid = layer_norm_parts(middle)
        hidden_in = (normed_mid * gains[layer, 1]).astype(bf16)
        hidden_pre = product(hidden_in, fc_mat)
        hidden_act = lax.optimization_barrier(jax.nn.gelu(hidden_pre).astype(bf16))
        saved.append(
            (normed, inv_std, norm_in, mixed, rim, long_out, gated, (sig_re, sig_im))
            + (normed_mid, inv_mid, hidden_in, hidden_pre, hidden_act)
        )
        stream = middle + product(hidden_act, proj_mat)
    mixed_out, grad = lax.optimization_barrier((stream.astype(bf16), cotangent[0]))
    grad = grad.astype(f32)
    summed = {}
    left_over = []
    small_grads = [None] * layers
    taps_grads = [None] * layers

    def scattered(parts):
        return lax.psum_scatter(parts, ("batch", "seq"), scatter_dimension=0, tiled=False).astype(f32)

    def parts_of(grad_mat):
        return grad_mat.reshape(devices, -1, grad_mat.shape[1])

    for layer in reversed(range(layers)):
        in_mat, out_mat, fc_mat, proj_mat = (weights[i, layer] for i in range(4))
        (normed, inv_std, norm_in, mixed, rim, long_out, gated, sig) = saved[layer][:8]
        (normed_mid, inv_mid, hidden_in, hidden_pre, hidden_act) = saved[layer][8:]
        grad_top = grad.astype(bf16)
        grad_act = contract(grad_top, proj_mat, 1, 1)
        grad_proj = contract(hidden_act, grad_top, 0, 0).astype(bf16)
        grad_pre = jax.vjp(jax.nn.gelu, hidden_pre)[1](grad_act)[0].astype(bf16)
        grad_hidden = contract(grad_pre, fc_mat, 1, 1)
        grad_fc = contract(hidden_in, grad_pre, 0, 0).astype(bf16)
        grad_gain_mid = jnp.sum(grad_hidden * normed_mid, axis=0)
        grad_middle = grad + norm_back(grad_hidden * gains[layer, 1], normed_mid, inv_mid)
        grad_mix = grad_middle.astype(bf16)
        grad_gated = contract(out_mat, grad_mix, 1, 1).reshape(nblocks, chans, toks)
        grad_out = contract(gated, grad_mix, 1, 0).astype(bf16)
        grad_gated, grad_proj = lax.optimization_barrier((grad_gated, grad_proj))
        if layer == 0:
            pending = left_over + [((3, layer), parts_of(grad_proj)), ((2, layer), parts_of(grad_fc))]
            left_over = [((1, layer), parts_of(grad_out))]
        else:
            summed[3, layer] = scattered(parts_of(grad_proj))
            pending = left_over + [((2, layer), parts_of(grad_fc)), ((1, layer), parts_of(grad_out))]
            left_over = []
        (taps_grads[layer], grad_mixed, grad_conv), arrived = unmix(
            [reduce_job(parts, plan) for (_, parts), plan in zip(pending, REDUCE_PLANS)],
            layer, mixed, conv_cols_of[layer], rim, long_out, grad_gated, specs[layer], sig, skips, tables, ids
        )
        summed.update({key: total for (key, _), total in zip(pending, arrived)})
        grad_mixed = grad_mixed.reshape(width3, toks)
        grad_norm_in = contract(grad_mixed, in_mat, 0, 1)
        grad_in = contract(norm_in, grad_mixed, 0, 1).astype(bf16)
        grad_gain_in = jnp.sum(grad_norm_in * normed, axis=0)
        grad = grad_middle + norm_back(grad_norm_in * gains[layer, 0], normed, inv_std)
        left_over.append(((0, layer), parts_of(grad_in)))
        small_grads[layer] = (
            jnp.stack([grad_gain_in, grad_gain_mid]),
            jnp.swapaxes(grad_conv.reshape(width3, LANES)[:, :3], 0, 1),
        )

    def rows_for(values, cols):
        pieces = jnp.swapaxes(values.reshape(values.shape[0], devices, cols), 0, 1)
        return jnp.pad(pieces, ((0, 0), (0, 0), (0, LANES - cols)))

    small_rows = jnp.concatenate(
        [rows_for(small_grads[layer][0], gain_cols) for layer in range(layers)]
        + [rows_for(small_grads[layer][1], conv_cols) for layer in range(layers)],
        axis=1,
    )
    small_rows = jnp.pad(small_rows, ((0, 0), (0, -small_rows.shape[1] % 8), (0, 0)))
    hidden = filt_w2.shape[1]
    emb = filt_w1.shape[1]
    left_over.reverse()
    left_over.append(("small", small_rows))
    each, shared = hidden + 8, FEATURES + hidden
    by_column, by_all = [], []
    jobs = [reduce_job(parts, plan) for (_, parts), plan in zip(left_over, LAST_PLANS)]
    for part, acts in zip(sets, kept):
        of = slice(part[0], part[-1] + 1)
        (totals,), arrived = last(
            jobs, pos_rows, filt_w2[of], filt_w3[of], decay[of], acts, taps_grads[of], ids
        )
        if part is sets[0]:
            summed.update({key: total for (key, _), total in zip(left_over, arrived)})
        jobs = []
        by_column.append(totals[: len(part) * each].reshape(-1, each, LANES))
        by_all.append(totals[len(part) * each :].reshape(-1, shared, LANES))
    by_column, by_all = jnp.concatenate(by_column), jnp.concatenate(by_all)
    small_sum = summed["small"]
    block = [jnp.stack([summed[i, layer] for layer in range(layers)]) for i in range(4)]
    gains_grad = small_sum[: 2 * layers, :gain_cols].reshape(layers, 2, gain_cols)
    conv_grad = small_sum[2 * layers : 5 * layers, :conv_cols].reshape(layers, 3, conv_cols)
    return (
        mixed_out[None],
        grad[None],
        gains_grad,
        block[0],
        conv_grad,
        block[1],
        block[2],
        block[3],
        by_all[:, :emb, :hidden],
        by_all[:, emb, :hidden],
        by_all[:, FEATURES:, :hidden],
        by_all[:, emb, hidden : 2 * hidden],
        by_column[:, :hidden, :own_chans],
        by_column[:, hidden, :own_chans],
    )


def solution(mesh):
    both = ("batch", "seq")
    in_specs = (
        P("batch", "seq", None),
        P("batch", "seq", None),
        P(None, None, both),
        P(None, both, None),
        P(None, None, both),
        P(None, both, None),
        P(None, both, None),
        P(None, both, None),
        P(),
        P(),
        P(),
        P(),
        P(None, None, "seq"),
        P(None, "seq"),
        P(None, "seq"),
    )
    out_specs = in_specs[:14]
    return jax.shard_map(
        on_device, mesh=mesh, in_specs=in_specs, out_specs=out_specs, check_vma=False
    )
```

```python
import functools
import itertools
import math

import jax
import jax.numpy as jnp
import numpy as np
from jax import lax
from jax.experimental import pallas as pl
from jax.experimental.pallas import tpu as pltpu
from jax.sharding import PartitionSpec as P

MESH = pl.DeviceIdType.MESH
LANES = 128
VMEM_LIMIT = 58 * 1024 * 1024
GATHER_PLANS = [[0, 1, 3, 5, 7, 9, 12], [0, 1, 3, 5, 7, 9, 12], [0, 2, 4, 6, 8, 10, 12], [0, 2, 5, 8, 10, 12, 14], [0, 3, 6, 9, 12, 14, 16]]
COLUMN_PLANS = [[2, 5, 8, 11, 14], [2, 5, 8, 11, 14], [3, 7, 10, 13, 15], [4, 8, 12, 14, 16]]
PLANE_PLANS = [[0, 4, 7, 11], [0, 5, 8, 11], [0, 6, 9, 11]]
REDUCE_PLANS = [[0, 1, 2, 4, 5, 8, 9, 12], [0, 3, 3, 7, 7, 10, 10, 12]]
PLANE_REDUCE_PLANS = [[0, 1, 1, 7, 7, 11, 11, 12], [0, 1, 1, 9, 9, 12, 12, 12], [0, 1, 1, 11, 11, 12, 12, 12]]
CHAIN_PLANS = [[0, 1, 3, 6], [1, 2, 4, 7], [2, 3, 6, 9]]
LAST_PLANS = [[0, 1, 1, 4, 4, 7, 7, 9], [0, 2, 2, 5, 5, 7, 8, 9], [0, 2, 2, 5, 5, 7, 8, 9]]
f32 = jnp.float32
bf16 = jnp.bfloat16


def product(left_mat, right_mat):
    return jnp.dot(left_mat, right_mat, preferred_element_type=f32)


def contract(left_mat, right_mat, left_dim, right_dim):
    return lax.dot_general(
        left_mat, right_mat, (((left_dim,), (right_dim,)), ((), ())), preferred_element_type=f32
    )


def gelu(x):
    return x * (0.5 + 0.5 * jnp.tanh(x * (GELU_SCALE + GELU_SCALE * GELU_CUBE * (x * x))))


def gelu_slope(x):
    square = x * x
    turn = jnp.tanh(x * (GELU_SCALE + GELU_SCALE * GELU_CUBE * square))
    half = 0.5 + 0.5 * turn
    steep = GELU_SCALE + 3.0 * GELU_SCALE * GELU_CUBE * square
    return half * (1.0 + x * (1.0 - turn) * steep)


def layer_norm_parts(stream):
    mean_val = jnp.mean(stream, axis=-1, keepdims=True)
    centered = stream - mean_val
    inv_std = lax.rsqrt(jnp.mean(centered * centered, axis=-1, keepdims=True) + 1e-05)
    return (centered * inv_std, inv_std)


def norm_back(grad_normed, normed, inv_std):
    mean_grad = jnp.mean(grad_normed, axis=-1, keepdims=True)
    mean_cross = jnp.mean(grad_normed * normed, axis=-1, keepdims=True)
    return inv_std * (grad_normed - mean_grad - normed * mean_cross)


def split_bf16(table):
    high = table.astype(np.float32).astype(jnp.bfloat16)
    return high, (table - high.astype(np.float64)).astype(np.float32).astype(jnp.bfloat16)


def transform_tables(length):
    blocks = min(length // LANES, 32)
    inside = length // blocks
    n1 = np.arange(blocks)
    n2 = np.arange(inside)
    outer = 2 * np.pi * ((n1[:, None] * (4 * n1[None, :] + 1)) % (4 * blocks)) / (4 * blocks)
    eye = np.eye(8)
    forward = np.concatenate([np.cos(outer).T, -np.sin(outer).T], axis=0)
    left_fwd = np.kron(forward, eye)
    left_inv = np.kron(np.concatenate([np.cos(outer), -np.sin(outer)], axis=1), eye) / length
    inner = 2 * np.pi * ((n2[:, None] * n2[None, :]) % inside) / inside
    cos2, sin2 = np.cos(inner), np.sin(inner)
    right_fwd = np.block([[cos2, -sin2], [sin2, cos2]])
    right_inv = np.block([[cos2, sin2], [-sin2, cos2]])
    twist = 2 * np.pi * (n2[None, :] * (4 * n1[:, None] + 1)) / (4 * length)
    twist_cos = np.repeat(np.cos(twist), 8, axis=0).astype(np.float32)
    twist_sin = np.repeat(np.sin(twist), 8, axis=0).astype(np.float32)
    tables = []
    for table, axis in ((left_fwd, 1), (right_fwd, 0), (left_inv, 1), (right_inv, 0)):
        high, low = split_bf16(table)
        tables.append(jnp.asarray(np.concatenate([high, low, high], axis=axis)))
    return tuple(tables) + (jnp.asarray(twist_cos), jnp.asarray(twist_sin))


TABLES = 6


def in_two(value):
    high = value.astype(bf16)
    return high, (value - high.astype(f32)).astype(bf16)


def left_product(left, right):
    high, low = in_two(right)
    return product(left[...], jnp.concatenate([high, high, low], axis=0))


def right_product(left, right):
    high, low = in_two(left)
    return product(jnp.concatenate([high, high, low], axis=1), right[...])


def beside(parts):
    return jnp.concatenate(parts, axis=1) if len(parts) > 1 else parts[0]


def below(parts):
    return jnp.concatenate(parts, axis=0) if len(parts) > 1 else parts[0]


def to_points(xs, tables, exact):
    left, right, _, _, twist_cos, twist_sin = tables
    rows, inside = twist_cos.shape
    flat = []
    for x in xs:
        split = x.reshape(rows // 8, inside // LANES, 8, LANES)
        line = [split[:, k] for k in range(inside // LANES)]
        flat.append((jnp.concatenate(line, axis=2) if len(line) > 1 else line[0]).reshape(rows, inside))
    flat = beside(flat)
    if exact:
        flat = flat.astype(bf16)
        turned = product(left[:, : 2 * rows], jnp.concatenate([flat, flat], axis=0))
    else:
        turned = left_product(left, flat)
    cos, sin = twist_cos[...], twist_sin[...]
    both = []
    for k in range(len(xs)):
        re, im = [turned[part, k * inside : (k + 1) * inside] for part in (slice(0, rows), slice(rows, 2 * rows))]
        both.append(jnp.concatenate([re * cos + im * sin, im * cos - re * sin], axis=1))
    points = right_product(below(both), right)
    return [
        (points[k * rows : (k + 1) * rows, :inside], points[k * rows : (k + 1) * rows, inside:])
        for k in range(len(xs))
    ]


def from_points(pairs, tables):
    _, _, left, right, twist_cos, twist_sin = tables
    rows, inside = twist_cos.shape
    back = right_product(below([jnp.concatenate(pair, axis=1) for pair in pairs]), right)
    cos, sin = twist_cos[...], twist_sin[...]
    both = []
    for k in range(len(pairs)):
        re, im = back[k * rows : (k + 1) * rows, :inside], back[k * rows : (k + 1) * rows, inside:]
        both.append(jnp.concatenate([re * cos - im * sin, re * sin + im * cos], axis=0))
    found = left_product(left, beside(both))
    results = []
    for k in range(len(pairs)):
        flat = found[:, k * inside : (k + 1) * inside].reshape(rows // 8, 8, inside)
        split = [flat[:, None, :, q * LANES : (q + 1) * LANES] for q in range(inside // LANES)]
        line = jnp.concatenate(split, axis=1) if len(split) > 1 else split[0]
        results.append(line.reshape(-1, 8, LANES))
    return results


FEATURES = 48
SPAN = 512
GELU_SCALE = math.sqrt(2.0 / math.pi)
GELU_CUBE = 0.044715


def position_rows(length, emb_width):
    positions = np.arange(length, dtype=np.int64)
    bands = np.arange(1, (emb_width - 1) // 2 + 1, dtype=np.int64)
    angles = 2.0 * np.pi / length * ((bands[:, None] * positions[None, :]) % length)
    table = np.zeros((FEATURES, length), np.float32)
    table[0] = positions / length
    table[1 : 1 + bands.size] = np.cos(angles)
    table[1 + bands.size : emb_width] = np.sin(angles)
    table[emb_width] = 1.0
    return jnp.asarray(table)


def near_dot(left, right, left_dim, right_dim):
    left_high, left_low = in_two(left)
    right_high, right_low = in_two(right)
    return contract(
        jnp.concatenate([left_high, left_high, left_low], axis=left_dim),
        jnp.concatenate([right_high, right_low, right_high], axis=right_dim),
        left_dim,
        right_dim,
    )


def in_three(value):
    high = value.astype(bf16)
    rest = value - high.astype(f32)
    middle = rest.astype(bf16)
    return high, middle, (rest - middle.astype(f32)).astype(bf16)


def full_dot(left, right):
    a, b, c = in_three(left)
    d, e, f = in_three(right)
    return contract(
        jnp.concatenate([a, a, a, b, b, c], axis=0), jnp.concatenate([d, e, f, d, e, d], axis=0), 0, 0
    )


def sin_cos(x):
    turns = jnp.round(x * (2.0 / math.pi))
    r = ((x - turns * 1.5703125) - turns * 4.837512969970703125e-4) - turns * 7.54978995489188216e-8
    z = r * r
    sine = r + r * z * (-1.6666654611e-1 + z * (8.3321608736e-3 - z * 1.9515295891e-4))
    cosine = 1.0 - 0.5 * z + z * z * (
        4.166664568298827e-2 + z * (-1.388731625493765e-3 + z * 2.443315711809948e-5)
    )
    turn = lax.bitwise_and(turns.astype(jnp.int32), 3)
    odd = lax.bitwise_and(turn, 1) == 1
    first = jnp.where(odd, cosine, sine)
    second = jnp.where(odd, sine, cosine)
    return (
        jnp.where(turn >= 2, -first, first),
        jnp.where(jnp.logical_or(turn == 1, turn == 2), -second, second),
    )


def window_of(decay, start, shape, length):
    lane = lax.broadcasted_iota(jnp.int32, shape, 1) + start
    return jnp.exp(lane.astype(f32) * (-1.0 / length) * decay)


def filter_span(layer, start, pos, first_w, second_w, third_w, rates, acts, shaped, squares):
    length = pos.shape[1]
    at = pl.ds(start, SPAN)
    act, slope = sin_cos(full_dot(first_w[layer], pos[:, at]))
    acts[layer, 0, :, at] = act
    acts[layer, 1, :, at] = slope
    act, slope = sin_cos(full_dot(second_w[layer], act) + rates[layer, : act.shape[0], :1])
    acts[layer, 2, :, at] = act
    acts[layer, 3, :, at] = slope
    raw = near_dot(third_w[layer], act, 0, 0)
    value = raw * window_of(rates[layer, act.shape[0] :, :1], start, raw.shape, length)
    shaped[layer, :, at] = value
    squares[layer] += jnp.sum(value * value, axis=1, keepdims=True)


def filter_points(group, tables, shaped, squares, specs):
    layers, _, length = shaped.shape
    rows = pl.ds(pl.multiple_of(group * 8, 8), 8)
    xs = []
    for layer in range(layers):
        scale = lax.rsqrt(squares[layer, rows, :1] * (1.0 / length) + 1e-05) * length ** (-0.5)
        value = shaped[layer, rows, :] * scale
        line = [value[:, i * LANES : (i + 1) * LANES][None] for i in range(length // LANES)]
        xs.append(jnp.concatenate(line, axis=0))
    for layer, (re, im) in enumerate(to_points(xs, tables, False)):
        specs[2 * layer][group] = re
        specs[2 * layer + 1][group] = im


def filter_back_dot(layer, start, shaped, grad_taps, dots):
    at = pl.ds(start, SPAN)
    grad = taps_span(grad_taps, start)
    dots[layer] += jnp.sum(shaped[layer, :, at] * grad, axis=1, keepdims=True)


def taps_span(grad_taps, start):
    first = lax.div(start, LANES)
    pieces = []
    for i in range(SPAN // LANES):
        piece = grad_taps[:, first + i]
        pieces.append(piece.reshape(-1, LANES))
    return jnp.concatenate(pieces, axis=1)


def filter_back_span(
    layer, start, pos, second_w, third_w, rates, acts, shaped, squares, grad_taps, dots, grads
):
    length = pos.shape[1]
    at = pl.ds(start, SPAN)
    grad_third, grad_second, grad_first = grads
    mean_square = squares[layer][:, :1] * (1.0 / length)
    scale = lax.rsqrt(mean_square + 1e-05)
    cross = dots[layer][:, :1] * (1.0 / length) * scale * scale
    grad = taps_span(grad_taps, start)
    value = shaped[layer, :, at]
    grad = (grad - value * cross) * (scale * length ** (-0.5))
    grad = grad * window_of(rates[layer, second_w.shape[1] :, :1], start, grad.shape, length)
    grad_third[layer] += near_dot(acts[layer, 2, :, at], grad, 1, 1)
    second = near_dot(third_w[layer], grad, 1, 0) * acts[layer, 3, :, at]
    grad_second[layer] += near_dot(acts[layer, 0, :, at], second, 1, 1)
    first = near_dot(second_w[layer], second, 1, 0) * acts[layer, 1, :, at]
    grad_first[layer] += near_dot(pos[:, at], jnp.concatenate([first, second], axis=0), 1, 1)


class Place:
    def __init__(self, ns):
        self.nz = ns // 2
        self.b = lax.axis_index("batch")
        self.s = lax.axis_index("seq")
        self.z = lax.div(self.s, 2)
        self.c = lax.rem(self.s, 2)
        self.x_peer = (lax.bitwise_xor(self.b, 1), self.s)
        self.y_peer = (lax.bitwise_xor(self.b, 2), self.s)
        self.core_peer = (self.b, lax.bitwise_xor(self.s, 1))
        self.up_peer = (self.b, lax.min(self.s + 2, ns - 1))
        self.down_peer = (self.b, lax.max(self.s - 2, 0))


def remote(src, dst, send, recv, peer):
    return pltpu.make_async_remote_copy(
        src_ref=src, dst_ref=dst, send_sem=send, recv_sem=recv, device_id=peer, device_id_type=MESH
    )


def greet(place, seq_peers):
    bar = pltpu.get_barrier_semaphore()

    def hello(peer):
        pl.semaphore_signal(bar, inc=1, device_id=peer, device_id_type=MESH)

    hello(place.x_peer)
    hello(place.y_peer)
    if seq_peers:
        ns = 2 * place.nz
        for step in range(1, ns):
            hello((place.b, lax.rem(place.s + step, ns)))
        pl.semaphore_wait(bar, 2 + ns - 1)
    else:
        hello(place.core_peer)
        pl.when(place.z + 1 < place.nz)(lambda: hello(place.up_peer))
        pl.when(place.z > 0)(lambda: hello(place.down_peer))
        ends = jnp.where(place.z == 0, 1, 0) + jnp.where(place.z == place.nz - 1, 1, 0)
        pl.semaphore_wait(bar, 5 - ends)


class Job:
    def __init__(self, arrays, results, scratch, task, plan):
        self.arrays, self.results, self.scratch, self.task = arrays, results, scratch, task
        self.plan = plan


class Runner:
    def __init__(self, tasks, plans):
        self.tasks = [[task, list(plan)] for task, plan in zip(tasks, plans, strict=True)]
        self.now = 0

    def add(self, task, steps):
        self.tasks.insert(0, [task, list(range(self.now, self.now + steps))])

    def step(self, entry):
        if next(entry[0], "end") == "end":
            self.tasks.remove(entry)

    def phase(self):
        for entry in list(self.tasks):
            while entry[1] and entry[1][0] <= self.now:
                entry[1].pop(0)
                self.step(entry)
        self.now += 1

    def finish(self):
        while any(entry[1] for entry in self.tasks):
            self.phase()
        while self.tasks:
            for entry in list(self.tasks):
                self.step(entry)


def room(items):
    total = 0
    for item in items:
        if len(item.shape) < 2 or not jnp.issubdtype(item.dtype, jnp.floating):
            continue
        size = jnp.dtype(item.dtype).itemsize
        *outer, rows, lanes = item.shape
        tile = 32 // size
        total += math.prod(outer) * -(-rows // tile) * tile * -(-lanes // LANES) * LANES * size
    return total


def fused_call(name, body, arrays, results, scratch, jobs, seq_peers, ids):
    free = VMEM_LIMIT - room([*arrays, *results, *scratch])
    if body is not None and room([item for job in jobs for item in job.scratch]) > free:
        found, _ = fused_call(name, body, arrays, results, scratch, [], seq_peers, ids)
        alone = [fused_call(name + "_job", None, [], [], [], [job], seq_peers, ids)[1][0] for job in jobs]
        return found, alone
    collective_id = next(ids)
    ns = lax.axis_size("seq")
    stages = [pltpu.VMEM(a.shape, a.dtype) for a in [*arrays, *results]]
    stages.append(pltpu.SemaphoreType.DMA((max(1, len(stages)),)))
    counts = [len(arrays)] + [len(j.arrays) for j in jobs]
    counts += [len(results)] + [len(j.results) for j in jobs]
    counts += [len(scratch)] + [len(j.scratch) for j in jobs] + [len(stages)]
    n = 1 + len(jobs)

    def kernel(*refs):
        parts, start = [], 0
        for count in counts:
            parts.append(refs[start : start + count])
            start += count
        *held, sems = parts[3 * n]
        ins, outs = held[: len(arrays)], held[len(arrays) :]
        staged = Staged(parts[0], ins, outs, parts[n], sems)
        place = Place(ns)
        greet(place, seq_peers)
        tasks = [
            job.task(place, *parts[1 + k], *parts[n + 1 + k], parts[2 * n + 1 + k])
            for k, job in enumerate(jobs)
        ]
        runner = Runner(tasks, [job.plan for job in jobs])
        if body is not None:
            body(place, runner, ins, outs, parts[2 * n], staged)
        runner.finish()
        staged.finish()

    hbm = pl.BlockSpec(memory_space=pl.ANY)
    flat = lambda pick: [item for job in jobs for item in pick(job)]
    found = pl.pallas_call(
        kernel,
        out_shape=list(results) + flat(lambda j: j.results),
        in_specs=[hbm] * sum(counts[:n]),
        out_specs=[hbm] * sum(counts[n : 2 * n]),
        scratch_shapes=list(scratch) + flat(lambda j: j.scratch) + stages,
        compiler_params=pltpu.CompilerParams(
            collective_id=collective_id, has_side_effects=True, vmem_limit_bytes=VMEM_LIMIT
        ),
        name=name,
    )(*arrays, *flat(lambda j: j.arrays))
    return found[: counts[n]], found[counts[n] :]


class Staged:
    def __init__(self, sources, ins, outs, targets, sems):
        self.loads = [pltpu.make_async_copy(a, b, sems.at[k]) for k, (a, b) in enumerate(zip(sources, ins))]
        first = len(self.loads)
        self.stores = [
            pltpu.make_async_copy(a, b, sems.at[first + k]) for k, (a, b) in enumerate(zip(outs, targets))
        ]
        self.loading = set(range(first))
        self.storing = set()
        for load in self.loads:
            load.start()

    def need(self, *which):
        for k in which:
            if k in self.loading:
                self.loading.remove(k)
                self.loads[k].wait()

    def ready(self, *which):
        for k in which:
            self.storing.add(k)
            self.stores[k].start()

    def finish(self):
        self.need(*sorted(self.loading))
        self.ready(*[k for k in range(len(self.stores)) if k not in self.storing])
        for store in self.stores:
            store.wait()


def gather_sems(nz):
    return [
        pltpu.SemaphoreType.DMA((1,)),
        pltpu.SemaphoreType.DMA((2, nz)),
        pltpu.SemaphoreType.DMA((nz,)),
        pltpu.SemaphoreType.DMA((4, nz)),
        pltpu.SemaphoreType.DMA((4, nz)),
        pltpu.SemaphoreType.DMA((4,)),
        pltpu.SemaphoreType.DMA((4,)),
    ]


def gather_task(place, src, dst, sems):
    one, chain_send, chain_recv, send, recv, core_send, core_recv = sems
    b, z, c, nz = place.b, place.z, place.c, place.nz
    bx, by, bd = place.x_peer[0], place.y_peer[0], lax.bitwise_xor(b, 3)
    local = pltpu.make_async_copy(src, dst.at[b, z, c], one.at[0])

    def chain(source, shard, up):
        row = 0 if up else 1
        peer = place.up_peer if up else place.down_peer
        return remote(source, dst.at[b, shard, c], chain_send.at[row, shard], chain_recv.at[shard], peer)

    def across(source, shard, along):
        peer = place.y_peer if along else place.x_peer
        return remote(source, dst.at[b, shard, c], send.at[along, shard], recv.at[along, shard], peer)

    def onward(shard, along):
        peer = place.y_peer if along else place.x_peer
        part = dst.at[bx if along else by, shard, c]
        return remote(part, part, send.at[2 + along, shard], recv.at[2 + along, shard], peer)

    def core(batch, i):
        part = dst.at[batch, :, c]
        return remote(part, part, core_send.at[i], core_recv.at[i], place.core_peer)

    def pass_on(shard):
        across(src, shard, 0).wait_recv()
        across(src, shard, 1).wait_recv()
        even = lax.rem(shard, 2) == 0
        pl.when(even)(lambda: onward(shard, 1).start())
        pl.when(jnp.logical_not(even))(lambda: onward(shard, 0).start())

    def pass_on_from(hop):
        if hop == 0:
            pass_on(z)
        else:
            pl.when(z - hop >= 0)(lambda: pass_on(z - hop))
            pl.when(z + hop < nz)(lambda: pass_on(z + hop))

    local.start()
    pl.when(z + 1 < nz)(lambda: chain(src, z, True).start())
    pl.when(z > 0)(lambda: chain(src, z, False).start())
    across(src, z, 0).start()
    across(src, z, 1).start()
    yield
    for hop in range(1, nz):
        below, above = z - hop, z + hop

        @pl.when(below >= 0)
        def _():
            chain(src, below, True).wait_recv()
            part = dst.at[b, below, c]
            pl.when(z + 1 < nz)(lambda: chain(part, below, True).start())
            across(part, below, 0).start()
            across(part, below, 1).start()

        @pl.when(above < nz)
        def _():
            chain(src, above, False).wait_recv()
            part = dst.at[b, above, c]
            pl.when(z > 0)(lambda: chain(part, above, False).start())
            across(part, above, 0).start()
            across(part, above, 1).start()

        pass_on_from(hop - 1)
        yield
    local.wait()
    core(b, 0).start()
    pass_on_from(nz - 1)
    core(bx, 1).start()
    core(by, 2).start()
    yield
    for shard in range(nz):
        onward(shard, 1 - shard % 2).wait_recv()
    core(bd, 3).start()
    yield
    for hop in range(nz):
        pl.when(jnp.logical_and(z >= hop, z + 1 < nz))(lambda: chain(src, z - hop, True).wait_send())
        pl.when(jnp.logical_and(z + hop < nz, z > 0))(lambda: chain(src, z + hop, False).wait_send())
    for shard in range(nz):
        across(src, shard, 0).wait_send()
        across(src, shard, 1).wait_send()
        onward(shard, 1 - shard % 2).wait_send()
    for i in range(4):
        core(b, i).wait()
    yield


def gather_job(array, layer, plan):
    nz = lax.axis_size("seq") // 2
    result = jax.ShapeDtypeStruct((4, nz, 2) + array.shape[1:], array.dtype)
    task = lambda place, src, dst, sems: gather_task(place, src.at[layer], dst, sems)
    return Job([array], [result], gather_sems(nz), task, plan)


def column_task(place, src, dst, sems):
    one, chain_send, chain_recv = sems
    z, nz = place.z, place.nz
    local = pltpu.make_async_copy(src, dst.at[z], one.at[0])

    def chain(source, shard, up):
        row = 0 if up else 1
        peer = place.up_peer if up else place.down_peer
        return remote(source, dst.at[shard], chain_send.at[row, shard], chain_recv.at[shard], peer)

    local.start()
    pl.when(z + 1 < nz)(lambda: chain(src, z, True).start())
    pl.when(z > 0)(lambda: chain(src, z, False).start())
    yield
    for hop in range(1, nz):
        below, above = z - hop, z + hop

        @pl.when(below >= 0)
        def _():
            chain(src, below, True).wait_recv()
            pl.when(z + 1 < nz)(lambda: chain(dst.at[below], below, True).start())

        @pl.when(above < nz)
        def _():
            chain(src, above, False).wait_recv()
            pl.when(z > 0)(lambda: chain(dst.at[above], above, False).start())

        yield
    for hop in range(nz):
        pl.when(jnp.logical_and(z >= hop, z + 1 < nz))(lambda: chain(src, z - hop, True).wait_send())
        pl.when(jnp.logical_and(z + hop < nz, z > 0))(lambda: chain(src, z + hop, False).wait_send())
    local.wait()
    yield


def column_job(array, layer, plan):
    nz = lax.axis_size("seq") // 2
    result = jax.ShapeDtypeStruct((nz,) + array.shape[1:], array.dtype)
    sems = [
        pltpu.SemaphoreType.DMA((1,)),
        pltpu.SemaphoreType.DMA((2, nz)),
        pltpu.SemaphoreType.DMA((nz,)),
    ]
    task = lambda place, src, dst, sems: column_task(place, src.at[layer], dst, sems)
    return Job([array], [result], sems, task, plan)


def plane_task(place, src, dst, sems):
    one, send, recv, core_send, core_recv = sems
    b, c, nz = place.b, place.c, place.nz
    bx, by, bd = place.x_peer[0], place.y_peer[0], lax.bitwise_xor(b, 3)
    half = nz // 2
    local = pltpu.make_async_copy(src, dst.at[b, :, c], one.at[0])
    over_x = remote(src, dst.at[b, :, c], send.at[0], recv.at[0], place.x_peer)
    over_y = remote(src, dst.at[b, :, c], send.at[1], recv.at[1], place.y_peer)
    low, high = pl.ds(0, half), pl.ds(half, nz - half)
    far_y = remote(dst.at[bx, low, c], dst.at[bx, low, c], send.at[2], recv.at[2], place.y_peer)
    far_x = remote(dst.at[by, high, c], dst.at[by, high, c], send.at[3], recv.at[3], place.x_peer)

    def core(source, batch, i):
        return remote(source, dst.at[batch, :, c], core_send.at[i], core_recv.at[i], place.core_peer)

    over_x.start()
    over_y.start()
    core(src, b, 0).start()
    local.start()
    yield
    over_x.wait_recv()
    far_y.start()
    over_y.wait_recv()
    far_x.start()
    core(dst.at[bx, :, c], bx, 1).start()
    core(dst.at[by, :, c], by, 2).start()
    yield
    far_y.wait_recv()
    far_x.wait_recv()
    core(dst.at[bd, :, c], bd, 3).start()
    yield
    for copy in (over_x, over_y, far_y, far_x):
        copy.wait_send()
    local.wait()
    for i in range(4):
        core(src, b, i).wait()
    yield


def plane_job(array, plan):
    nz = array.shape[0]
    result = jax.ShapeDtypeStruct((4, nz, 2) + array.shape[1:], array.dtype)
    sems = [pltpu.SemaphoreType.DMA((1,))] + [pltpu.SemaphoreType.DMA((4,))] * 4
    return Job([array], [result], sems, plane_task, plan)


def reduce_scratch(nz, shape, dtype):
    half = (nz,) + shape
    return [
        pltpu.VMEM((4,) + half, dtype),
        pltpu.VMEM((4,) + half, dtype),
        pltpu.VMEM((5,) + half, dtype),
        pltpu.VMEM(shape, f32),
        pltpu.SemaphoreType.DMA((1,)),
        pltpu.SemaphoreType.DMA((3, nz)),
        pltpu.SemaphoreType.DMA((5, nz)),
        pltpu.SemaphoreType.DMA((5, nz)),
    ]


def far_first(place):
    nz = place.nz
    tables = [sorted(range(nz), key=lambda k: (-abs(k - z), k)) for z in range(nz)]
    order = []
    for j in range(nz):
        shard = jnp.int32(tables[0][j])
        for z in range(1, nz):
            shard = jnp.where(place.z == z, tables[z][j], shard)
        order.append(shard)
    return order


def reduce_task(place, src, out, scratch):
    acc, other, box, total, one, near, send, recv = scratch
    kind = acc.dtype
    b, z, c, nz = place.b, place.z, place.c, place.nz
    bx, by, bd = place.x_peer[0], place.y_peer[0], lax.bitwise_xor(b, 3)
    far, via_x, via_y, up, down = range(5)
    order = far_first(place)
    halves = [range(0, nz // 2), range(nz // 2, nz)]

    def add(target, shard, *lanes):
        value = acc[target, shard].astype(f32)
        for lane in lanes:
            value += box[lane, shard].astype(f32)
        acc[target, shard] = value.astype(kind)

    def move(part, shard, lane, peer):
        return remote(acc.at[part, shard], box.at[lane, shard], send.at[lane, shard], recv.at[lane, shard], peer)

    def mine(shard):
        return pltpu.make_async_copy(src.at[:, shard, c], acc.at[:, shard], near.at[0, shard])

    def core(shard):
        return remote(src.at[:, shard, 1 - c], other.at[:, shard], near.at[1, shard], near.at[2, shard], place.core_peer)

    for shard in order:
        core(shard).start()
        mine(shard).start()
    yield
    for half in halves:
        for j in half:
            shard = order[j]
            mine(shard).wait()
            core(shard).wait_recv()

            @pl.loop(0, 4)
            def _(part):
                acc[part, shard] = (
                    acc[part, shard].astype(f32) + other[part, shard].astype(f32)
                ).astype(kind)

            if j % 2 == 0:
                move(bd, shard, far, place.x_peer).start()
                move(bx, shard, via_x, place.x_peer).start()
            else:
                move(bd, shard, far, place.y_peer).start()
                move(by, shard, via_y, place.y_peer).start()
        yield
    for half in halves:
        for j in half:
            shard = order[j]
            move(bd, shard, far, place.x_peer).wait_recv()
            if j % 2 == 0:
                add(by, shard, far)
                move(by, shard, via_y, place.y_peer).start()
            else:
                add(bx, shard, far)
                move(bx, shard, via_x, place.x_peer).start()
        yield
    for half in halves:
        for j in half:
            shard = order[j]
            move(bx, shard, via_x, place.x_peer).wait_recv()
            move(by, shard, via_y, place.y_peer).wait_recv()
            add(b, shard, via_x, via_y)

            @pl.when(z < shard)
            def _():
                @pl.when(z > 0)
                def _():
                    move(b, shard, up, place.up_peer).wait_recv()
                    add(b, shard, up)

                move(b, shard, up, place.up_peer).start()

            @pl.when(z > shard)
            def _():
                @pl.when(z + 1 < nz)
                def _():
                    move(b, shard, down, place.down_peer).wait_recv()
                    add(b, shard, down)

                move(b, shard, down, place.down_peer).start()

        yield
    total[...] = acc[b, z].astype(f32)

    @pl.when(z > 0)
    def _():
        move(b, z, up, place.up_peer).wait_recv()
        total[...] += box[up, z].astype(f32)

    @pl.when(z + 1 < nz)
    def _():
        move(b, z, down, place.down_peer).wait_recv()
        total[...] += box[down, z].astype(f32)

    result = pltpu.make_async_copy(total, out, one.at[0])
    result.start()
    for shard in range(nz):
        core(shard).wait_send()
        for lane in (far, via_x, via_y):
            move(b, shard, lane, place.x_peer).wait_send()
        pl.when(z < shard)(lambda: move(b, shard, up, place.up_peer).wait_send())
        pl.when(z > shard)(lambda: move(b, shard, down, place.down_peer).wait_send())
    result.wait()
    yield


def plane_reduce_task(place, src, out, scratch):
    acc, other, box, one, near, send, recv = scratch
    kind = acc.dtype
    b, z, c, nz = place.b, place.z, place.c, place.nz
    bx, by, bd = place.x_peer[0], place.y_peer[0], lax.bitwise_xor(b, 3)
    far, via_x, via_y = range(3)
    order = far_first(place)
    halves = [range(0, nz // 2), range(nz // 2, nz)]

    def add(target, shard, *lanes):
        value = acc[target, shard].astype(f32)
        for lane in lanes:
            value += box[lane, shard].astype(f32)
        acc[target, shard] = value.astype(kind)

    def move(part, shard, lane, peer):
        return remote(acc.at[part, shard], box.at[lane, shard], send.at[lane, shard], recv.at[lane, shard], peer)

    def mine(shard):
        return pltpu.make_async_copy(src.at[:, shard, c], acc.at[:, shard], near.at[0, shard])

    def core(shard):
        return remote(src.at[:, shard, 1 - c], other.at[:, shard], near.at[1, shard], near.at[2, shard], place.core_peer)

    for shard in order:
        core(shard).start()
        mine(shard).start()
    yield
    for half in halves:
        for j in half:
            shard = order[j]
            mine(shard).wait()
            core(shard).wait_recv()

            @pl.loop(0, 4)
            def _(part):
                acc[part, shard] = (
                    acc[part, shard].astype(f32) + other[part, shard].astype(f32)
                ).astype(kind)

            if j % 2 == 0:
                move(bd, shard, far, place.x_peer).start()
                move(bx, shard, via_x, place.x_peer).start()
            else:
                move(bd, shard, far, place.y_peer).start()
                move(by, shard, via_y, place.y_peer).start()
        yield
    for half in halves:
        for j in half:
            shard = order[j]
            move(bd, shard, far, place.x_peer).wait_recv()
            if j % 2 == 0:
                add(by, shard, far)
                move(by, shard, via_y, place.y_peer).start()
            else:
                add(bx, shard, far)
                move(bx, shard, via_x, place.x_peer).start()
        yield
    for half in halves:
        for j in half:
            shard = order[j]
            move(bx, shard, via_x, place.x_peer).wait_recv()
            move(by, shard, via_y, place.y_peer).wait_recv()
            add(b, shard, via_x, via_y)
        yield
    result = pltpu.make_async_copy(acc.at[b], out, one.at[0])
    result.start()
    for shard in range(nz):
        core(shard).wait_send()
        for lane in (far, via_x, via_y):
            move(b, shard, lane, place.x_peer).wait_send()
    result.wait()
    yield


def chain_reduce_task(place, src, out, scratch):
    acc, box, total, one, send, recv = scratch
    kind = acc.dtype
    z, nz = place.z, place.nz
    up, down = range(2)
    order = far_first(place)
    halves = [range(0, nz // 2), range(nz // 2, nz)]

    def add(shard, lane):
        acc[shard] = (acc[shard].astype(f32) + box[lane, shard].astype(f32)).astype(kind)

    def move(shard, lane):
        peer = place.down_peer if lane else place.up_peer
        return remote(acc.at[shard], box.at[lane, shard], send.at[lane, shard], recv.at[lane, shard], peer)

    load = pltpu.make_async_copy(src, acc, one.at[0])
    load.start()
    yield
    load.wait()
    for half in halves:
        for j in half:
            shard = order[j]

            @pl.when(z < shard)
            def _():
                @pl.when(z > 0)
                def _():
                    move(shard, up).wait_recv()
                    add(shard, up)

                move(shard, up).start()

            @pl.when(z > shard)
            def _():
                @pl.when(z + 1 < nz)
                def _():
                    move(shard, down).wait_recv()
                    add(shard, down)

                move(shard, down).start()

        yield
    total[...] = acc[z].astype(f32)

    @pl.when(z > 0)
    def _():
        move(z, up).wait_recv()
        total[...] += box[up, z].astype(f32)

    @pl.when(z + 1 < nz)
    def _():
        move(z, down).wait_recv()
        total[...] += box[down, z].astype(f32)

    result = pltpu.make_async_copy(total, out, one.at[1])
    result.start()
    for shard in range(nz):
        pl.when(z < shard)(lambda: move(shard, up).wait_send())
        pl.when(z > shard)(lambda: move(shard, down).wait_send())
    result.wait()
    yield


def plane_reduce_job(array, plan):
    nz = lax.axis_size("seq") // 2
    shape = array.shape[1:]
    acc, other, box, _, one, near, _, _ = reduce_scratch(nz, shape, array.dtype)
    sems = pltpu.SemaphoreType.DMA((3, nz))
    return Job(
        [array.reshape((4, nz, 2) + shape)],
        [jax.ShapeDtypeStruct((nz,) + shape, array.dtype)],
        [acc, other, pltpu.VMEM((3, nz) + shape, array.dtype), one, near, sems, sems],
        plane_reduce_task,
        plan,
    )


def chain_reduce_job(array, plan):
    nz, *shape = array.shape
    shape = tuple(shape)
    sems = pltpu.SemaphoreType.DMA((2, nz))
    return Job(
        [array],
        [jax.ShapeDtypeStruct(shape, f32)],
        [
            pltpu.VMEM((nz,) + shape, array.dtype),
            pltpu.VMEM((2, nz) + shape, array.dtype),
            pltpu.VMEM(shape, f32),
            pltpu.SemaphoreType.DMA((2,)),
            sems,
            sems,
        ],
        chain_reduce_task,
        plan,
    )


def reduce_job(array, plan):
    nz = lax.axis_size("seq") // 2
    shape = array.shape[1:]
    return Job(
        [array.reshape((4, nz, 2) + shape)],
        [jax.ShapeDtypeStruct(shape, f32)],
        reduce_scratch(nz, shape, array.dtype),
        reduce_task,
        plan,
    )


def total_scratch(nz, shape, shared):
    return [
        pltpu.VMEM((4,) + shape, bf16),
        pltpu.VMEM((2, shared, LANES), bf16),
        pltpu.VMEM((nz + 1, shared, LANES), bf16),
        pltpu.VMEM(shape, f32),
        pltpu.SemaphoreType.DMA((2, 3)),
        pltpu.SemaphoreType.DMA((2, nz)),
    ]


def total_task(place, src, out, scratch):
    box, pair_box, lines, sums, pair, chain = scratch
    z, c, nz = place.z, place.c, place.nz
    rows = src.shape[0]
    shared = lines.shape[1]
    tail = pl.ds(rows - shared, shared)

    def swap(source, dst, i, peer):
        return remote(source, dst, pair.at[0, i], pair.at[1, i], peer)

    box[0] = src[...].astype(bf16)
    first = swap(box.at[0], box.at[2], 0, place.x_peer)
    first.start()
    yield
    first.wait()
    sums[...] = box[0].astype(f32) + box[2].astype(f32)
    box[1] = sums[...].astype(bf16)
    second = swap(box.at[1], box.at[3], 1, place.y_peer)
    second.start()
    yield
    second.wait()
    sums[...] = box[1].astype(f32) + box[3].astype(f32)
    pair_box[0] = sums[tail].astype(bf16)
    third = swap(pair_box.at[0], pair_box.at[1], 2, place.core_peer)
    third.start()
    yield
    third.wait()
    lines[nz] = (pair_box[0].astype(f32) + pair_box[1].astype(f32)).astype(bf16)

    def along(step):
        peer = lax.rem(z + step, nz)
        return remote(lines.at[nz], lines.at[z], chain.at[0, step], chain.at[1, step], (place.b, 2 * peer + c))

    for step in range(1, nz):
        along(step).start()
    lines[z] = lines[nz]
    yield
    for step in range(1, nz):
        along(step).wait_recv()
    value = lines[0].astype(f32)
    for shard in range(1, nz):
        value = value + lines[shard].astype(f32)
    out[: rows - shared] = sums[: rows - shared]
    out[tail] = value
    for step in range(1, nz):
        along(step).wait_send()
    yield


def prepare(jobs, pos_rows, first_w, second_w, third_w, rates, tables, ids):
    layers, hidden, own = third_w.shape
    length = pos_rows.shape[1]
    rows = (own // 8,) + tables[4].shape
    results = [
        jax.ShapeDtypeStruct((layers, 4, hidden, length), f32),
        jax.ShapeDtypeStruct((layers, own, length), f32),
        jax.ShapeDtypeStruct((layers, own, LANES), f32),
    ] + [jax.ShapeDtypeStruct(rows, f32)] * (2 * layers)

    def body(place, runner, ins, outs, scratch, staged):
        pos, first, second, third, rate = ins[:5]
        factors = ins[5:]
        acts, shaped, squares = outs[:3]
        specs = outs[3:]
        spans, groups = length // SPAN, own // 8
        squares[...] = jnp.zeros_like(squares)
        staged.need(0, 1, 2, 3, 4)
        for part in range(8):
            runner.phase()

            @pl.loop(part * spans // 8, (part + 1) * spans // 8)
            def _(i):
                for layer in range(layers):
                    filter_span(
                        layer, pl.multiple_of(i * SPAN, SPAN), pos, first, second, third, rate, acts, shaped, squares
                    )

        staged.ready(0, 1, 2)
        staged.need(*range(5, 5 + TABLES))
        for part in range(6):
            runner.phase()

            @pl.loop(part * groups // 6, (part + 1) * groups // 6)
            def _(group):
                filter_points(group, factors, shaped, squares, specs)

    return fused_call(
        "prepare",
        body,
        [pos_rows, first_w, second_w, third_w, rates, *tables],
        results,
        [],
        jobs,
        False,
        ids,
    )


def last(jobs, pos_rows, second_w, third_w, rates, kept, grad_taps, ids):
    layers, hidden, own = third_w.shape
    length = pos_rows.shape[1]
    nz = lax.axis_size("seq") // 2
    each, shared = hidden + 8, hidden
    payload = jax.ShapeDtypeStruct((layers * (each + shared), LANES), f32)

    def body(place, runner, ins, outs, scratch, staged):
        pos, second, third, rate, acts, shaped, squares = ins[:7]
        taps = ins[7:]
        dots, grad_third, grad_second, grad_first, payload_in = scratch[:5]
        for ref in (dots, grad_third, grad_second, grad_first, payload_in):
            ref[...] = jnp.zeros_like(ref)
        runner.phase()
        spans = length // SPAN
        staged.need(5, *range(7, 7 + layers))

        @pl.loop(0, spans)
        def _(i):
            for layer in range(layers):
                filter_back_dot(layer, pl.multiple_of(i * SPAN, SPAN), shaped, taps[layer], dots)

        staged.need(0, 1, 2, 3, 4, 6)
        for part in range(8):
            runner.phase()

            @pl.loop(part * spans // 8, (part + 1) * spans // 8)
            def _(i):
                for layer in range(layers):
                    filter_back_span(
                        layer, pl.multiple_of(i * SPAN, SPAN), pos, second, third, rate, acts, shaped, squares,
                        taps[layer], dots, (grad_third, grad_second, grad_first)
                    )

        for layer in range(layers):
            start = layer * each
            payload_in[start : start + hidden, :own] = grad_third[layer]
            lag = taps[layer][:, 0].reshape(own, LANES)
            pick = jnp.where(lax.broadcasted_iota(jnp.int32, (8, LANES), 1) == 0, 1.0, 0.0)
            payload_in[start + hidden : start + each, :own] = near_dot(pick, lag, 1, 1)
            start = layers * each + layer * shared
            payload_in[start : start + FEATURES, :hidden] = grad_first[layer][:, :hidden]
            payload_in[start + FEATURES : start + FEATURES + 8, :hidden] = pltpu.roll(
                grad_first[layer][FEATURES - 16 : FEATURES - 8], hidden, 1
            )[:, :hidden]
            payload_in[start : start + hidden, hidden : 2 * hidden] = grad_second[layer]
        runner.add(total_task(place, payload_in, outs[0], scratch[5:]), 4)

    return fused_call(
        "last",
        body,
        [pos_rows, second_w, third_w, rates, *kept, *grad_taps],
        [payload],
        [
            pltpu.VMEM((layers, own, LANES), f32),
            pltpu.VMEM((layers, hidden, own), f32),
            pltpu.VMEM((layers, hidden, hidden), f32),
            pltpu.VMEM((layers, FEATURES, 2 * hidden), f32),
            pltpu.VMEM(payload.shape, f32),
        ]
        + total_scratch(nz, payload.shape, layers * shared),
        jobs,
        True,
        ids,
    )


def conv_lanes(value, rim_near, rim_far):
    lane = lax.broadcasted_iota(jnp.int32, value.shape, 1)
    near = jnp.where(lane == 0, rim_near, pltpu.roll(value, 1, 1))
    far = jnp.where(lane == 0, rim_far, jnp.where(lane == 1, rim_near, pltpu.roll(value, 2, 1)))
    return near, far


def rows_of(ref, stream, block, count):
    value = ref[stream, pl.ds(block, count)].astype(f32)
    return value.reshape(-1, value.shape[-1])


def short_out(mixed, conv, rim, stream, block, count=1):
    value = rows_of(mixed, stream, block, count)
    side, edge = rows_of(conv, stream, block, count), rows_of(rim, stream, block, count)
    near, far = conv_lanes(value, edge[:, 1:2], edge[:, 0:1])
    return side[:, 0:1] * far + side[:, 1:2] * near + side[:, 2:3] * value


def by_blocks(nblocks, most):
    return max(k for k in range(1, most + 1) if nblocks % k == 0)


def edge_scratch(streams, nblocks, chans):
    rows = pltpu.VMEM((streams, 16, nblocks * chans), f32)
    return [rows, rows, pltpu.VMEM((streams, nblocks, chans, LANES), f32), pltpu.SemaphoreType.DMA((2,))]


def edge_copy(place, scratch, to_right):
    out, came, _, sems = scratch
    ns = 2 * place.nz
    peer = lax.min(place.s + 1, ns - 1) if to_right else lax.max(place.s - 1, 0)
    return remote(out, came, sems.at[0], sems.at[1], (place.b, peer))


def send_edge(place, scratch, tiles_of, first, to_right):
    out = scratch[0]
    row = lax.broadcasted_iota(jnp.int32, (16, LANES), 0)
    lane = lax.broadcasted_iota(jnp.int32, (16, LANES), 1)
    pick = jnp.where(jnp.logical_and(lane == row + first, row < 2), 1.0, 0.0).astype(bf16)
    for stream in range(out.shape[0]):
        high, low = in_two(tiles_of(stream).reshape(-1, LANES))
        out[stream] = contract(
            jnp.concatenate([pick, pick], axis=1), jnp.concatenate([high, low], axis=1), 1, 1
        )
    has = place.s + 1 < 2 * place.nz if to_right else place.s > 0
    pl.when(has)(lambda: edge_copy(place, scratch, to_right).start())


def take_edge(place, scratch, to_right):
    _, came, cols, _ = scratch
    _, nblocks, chans, _ = cols.shape
    comes = place.s > 0 if to_right else place.s + 1 < 2 * place.nz
    sends = place.s + 1 < 2 * place.nz if to_right else place.s > 0

    @pl.when(comes)
    def _():
        edge_copy(place, scratch, to_right).wait_recv()
        row = lax.broadcasted_iota(jnp.int32, (16, LANES), 0)
        lane = lax.broadcasted_iota(jnp.int32, (16, LANES), 1)
        spread = jnp.where(jnp.logical_and(lane == row, row < 2), 1.0, 0.0).astype(bf16)
        both = jnp.concatenate([spread, spread], axis=0)
        for stream in range(cols.shape[0]):
            pair = jnp.concatenate(in_two(came[stream]), axis=0)
            cols[stream] = contract(pair, both, 0, 0).reshape(nblocks, chans, LANES)

    @pl.when(jnp.logical_not(comes))
    def _():
        cols[...] = jnp.zeros_like(cols)

    pl.when(sends)(lambda: edge_copy(place, scratch, to_right).wait_send())


def sub_rows(chans):
    return 16 if chans % 16 == 0 else chans


def mix_body(place, runner, ins, outs, scratch, staged, layer):
    mixed, conv, spec_re, spec_im, skip = ins[:5]
    tables = ins[5:]
    long_out, gated, sig_re, sig_im, rim = outs
    signal, chan_in, chan_out, tok_in, send, recv = scratch[:6]
    edge = [scratch[6], scratch[7], rim, scratch[8]]
    toks = mixed.shape[3]
    ns, groups, quarters, chans, _ = signal.shape
    take = sub_rows(chans)

    def to_chan(g, step):
        peer = lax.rem(place.s + step, ns)
        return remote(
            signal.at[peer, g],
            chan_in.at[g, pl.ds(place.s * quarters, quarters)],
            send.at[0, g, step],
            recv.at[0, g, step],
            (place.b, peer),
        )

    def send_pieces(step, first, value):
        peer = lax.rem(place.s + step, ns)
        count = value.shape[0] // chans
        for k in range(count):
            for q in range(quarters):
                piece = value[k * chans : (k + 1) * chans, q * LANES : (q + 1) * LANES]
                signal[peer, first + k, q] = piece

        @pl.when(step < ns)
        def _():
            for k in range(count):
                to_chan(first + k, step).start()

        @pl.when(step == ns)
        def _():
            for k in range(count):
                for q in range(quarters):
                    chan_in[first + k, place.s * quarters + q] = signal[peer, first + k, q]

    def to_tok(g, step):
        peer = lax.rem(place.s + step, ns)
        return remote(
            chan_out.at[g, pl.ds(peer * quarters, quarters)],
            tok_in.at[place.s, g],
            send.at[1, g, step],
            recv.at[1, g, step],
            (place.b, peer),
        )

    staged.need(0)
    send_edge(place, edge, lambda k: mixed[k, :, :, toks - LANES :].astype(f32), LANES - 2, True)
    runner.phase()
    take_edge(place, edge, True)
    staged.ready(4)
    staged.need(1)
    share = by_blocks(groups, 3)
    for first in range(0, groups, share):

        @pl.loop(1, ns + 1)
        def _(step):
            peer = lax.rem(place.s + step, ns)
            block = peer * groups + first
            value = short_out(mixed, conv, rim, 1, block, share) * short_out(mixed, conv, rim, 2, block, share)
            send_pieces(step, first, value.astype(bf16))

    staged.need(2, 3, 4, *range(5, 5 + TABLES))
    runner.phase()
    for g in range(groups):

        @pl.loop(1, ns)
        def _(step):
            to_chan(g, step).wait_recv()

        @pl.loop(0, chans // take)
        def _(i):
            at = pl.ds(pl.multiple_of(i * take, take), take)
            block = chan_in[g, :, at, :].astype(f32)
            base = (g * chans) // 8 + i * (take // 8)
            xs = [block[:, 8 * j : 8 * j + 8, :] for j in range(take // 8)]
            products = []
            for j, (re, im) in enumerate(to_points(xs, tables, True)):
                sig_re[base + j] = re
                sig_im[base + j] = im
                tap_re, tap_im = spec_re[base + j], spec_im[base + j]
                products.append((re * tap_re - im * tap_im, re * tap_im + im * tap_re))
            found = from_points(products, tables)
            parts = [y + skip[layer, base + j][None] * xs[j] for j, y in enumerate(found)]
            chan_out[g, :, at, :] = jnp.concatenate(parts, axis=1).astype(bf16)

        @pl.loop(1, ns)
        def _(step):
            to_tok(g, step).start()

        for q in range(quarters):
            tok_in[place.s, g, q] = chan_out[g, place.s * quarters + q]
        runner.phase()

    staged.ready(2, 3)
    for g in range(groups):

        @pl.loop(1, ns)
        def _(step):
            to_tok(g, step).wait_recv()

        @pl.loop(0, ns, unroll=4)
        def _(owner):
            block = owner * groups + g
            value = jnp.concatenate([tok_in[owner, g, q] for q in range(quarters)], axis=1)
            long_out[block] = value
            gated[block] = (short_out(mixed, conv, rim, 0, block) * value.astype(f32)).astype(bf16)

        if g % 2:
            runner.phase()

    for g in range(groups):

        @pl.loop(1, ns)
        def _(step):
            to_chan(g, step).wait_send()
            to_tok(g, step).wait_send()


def mixer_scratch(ns, groups, quarters, chans):
    pieces = pltpu.VMEM((ns, groups, quarters, chans, LANES), bf16)
    lines = pltpu.VMEM((groups, ns * quarters, chans, LANES), bf16)
    sems = pltpu.SemaphoreType.DMA((2, groups, ns))
    return [pieces, lines, lines, pieces, sems, sems]


def mix(jobs, layer, mixed, conv, spec, skip, tables, ids):
    ns = lax.axis_size("seq")
    _, nblocks, chans, toks = mixed.shape
    groups, quarters = nblocks // ns, toks // LANES
    rows = jax.ShapeDtypeStruct((groups * chans // 8,) + tables[4].shape, f32)
    tokens = jax.ShapeDtypeStruct((nblocks, chans, toks), bf16)
    edges = edge_scratch(3, nblocks, chans)
    return fused_call(
        "mix",
        functools.partial(mix_body, layer=layer),
        [mixed, conv, *spec, skip, *tables],
        [tokens, tokens, rows, rows, jax.ShapeDtypeStruct(conv.shape, f32)],
        mixer_scratch(ns, groups, quarters, chans) + edges[:2] + edges[3:],
        jobs,
        True,
        ids,
    )


def unmix_body(place, runner, ins, outs, scratch, staged, layer):
    mixed, conv, rim, long_out, grad_gated, spec_re, spec_im, sig_re, sig_im, skip = ins[:10]
    tables = ins[10:]
    grad_taps, grad_mixed, grad_conv = outs
    pull, chan_in, chan_out, tok_in, send, recv, grad_short, partials = scratch[:8]
    edge = scratch[8:]
    toks = mixed.shape[3]
    runner.phase()
    staged.need(0, 1, 2, 4)
    ns, groups, quarters, chans, _ = pull.shape
    take = sub_rows(chans)

    def to_chan(g, step):
        peer = lax.rem(place.s + step, ns)
        return remote(
            pull.at[peer, g],
            chan_in.at[g, pl.ds(place.s * quarters, quarters)],
            send.at[0, g, step],
            recv.at[0, g, step],
            (place.b, peer),
        )

    def send_pieces(step, first, value):
        peer = lax.rem(place.s + step, ns)
        count = value.shape[0] // chans
        for k in range(count):
            for q in range(quarters):
                piece = value[k * chans : (k + 1) * chans, q * LANES : (q + 1) * LANES]
                pull[peer, first + k, q] = piece

        @pl.when(step < ns)
        def _():
            for k in range(count):
                to_chan(first + k, step).start()

        @pl.when(step == ns)
        def _():
            for k in range(count):
                for q in range(quarters):
                    chan_in[first + k, place.s * quarters + q] = pull[peer, first + k, q]

    def to_tok(g, step):
        peer = lax.rem(place.s + step, ns)
        return remote(
            chan_out.at[g, pl.ds(peer * quarters, quarters)],
            tok_in.at[place.s, g],
            send.at[1, g, step],
            recv.at[1, g, step],
            (place.b, peer),
        )

    share = by_blocks(groups, 3)
    for first in range(0, groups, share):

        @pl.loop(1, ns + 1)
        def _(step):
            block = lax.rem(place.s + step, ns) * groups + first
            gated = grad_gated[pl.ds(block, share)].reshape(share * chans, toks)
            send_pieces(step, first, (gated * short_out(mixed, conv, rim, 0, block, share)).astype(bf16))

    staged.need(5, 6, 7, 8, 9, *range(10, 10 + TABLES))
    runner.phase()
    for g in range(groups):

        @pl.loop(1, ns)
        def _(step):
            to_chan(g, step).wait_recv()

        @pl.loop(0, chans // take)
        def _(i):
            at = pl.ds(pl.multiple_of(i * take, take), take)
            block = chan_in[g, :, at, :].astype(f32)
            base = (g * chans) // 8 + i * (take // 8)
            count = take // 8
            xs = [block[:, 8 * j : 8 * j + 8, :] for j in range(count)]
            signals, taps = [], []
            for j, (re, im) in enumerate(to_points(xs, tables, True)):
                tap_re, tap_im = spec_re[base + j], spec_im[base + j]
                own_re, own_im = sig_re[base + j], sig_im[base + j]
                signals.append((tap_re * re + tap_im * im, tap_re * im - tap_im * re))
                taps.append((own_re * re + own_im * im, own_re * im - own_im * re))
            found = from_points(signals + taps, tables)
            parts = [found[j] + skip[layer, base + j][None] * xs[j] for j in range(count)]
            for j in range(count):
                grad_taps[base + j] = found[count + j]
            chan_out[g, :, at, :] = jnp.concatenate(parts, axis=1).astype(bf16)

        @pl.loop(1, ns)
        def _(step):
            to_tok(g, step).start()

        for q in range(quarters):
            tok_in[place.s, g, q] = chan_out[g, place.s * quarters + q]
        runner.phase()

    staged.ready(0)
    staged.need(3)

    @pl.loop(0, ns * groups, unroll=4)
    def _(block):
        grad_short[0, block] = grad_gated[block] * long_out[block].astype(f32)

    for g in range(groups):

        @pl.loop(1, ns)
        def _(step):
            to_tok(g, step).wait_recv()

        @pl.loop(0, ns, unroll=4)
        def _(owner):
            block = owner * groups + g
            value = jnp.concatenate(
                [tok_in[owner, g, q] for q in range(quarters)], axis=1
            ).astype(f32)
            grad_short[1, block] = value * short_out(mixed, conv, rim, 2, block)
            grad_short[2, block] = value * short_out(mixed, conv, rim, 1, block)

        if g % 2:
            runner.phase()

    send_edge(place, edge, lambda k: grad_short[k, :, :, :LANES], 0, False)
    many = by_blocks(ns * groups, 4)
    ones = jnp.ones((2 * LANES, LANES), bf16)
    for stream in range(3):

        @pl.loop(0, ns * groups // many, unroll=2)
        def _(i):
            at = pl.ds(i * many, many)
            grad = rows_of(grad_short, stream, i * many, many)
            value = rows_of(mixed, stream, i * many, many)
            side = rows_of(rim, stream, i * many, many)
            near, far = conv_lanes(value, side[:, 1:2], side[:, 0:1])
            for k, moved in enumerate((far, near, value)):
                terms = grad * moved
                partial = terms[:, :LANES]
                for q in range(1, quarters):
                    partial += terms[:, q * LANES : (q + 1) * LANES]
                partials[k, at] = partial.reshape(many, chans, LANES)

        sums = [
            product(jnp.concatenate(in_two(partials[k].reshape(-1, LANES)), axis=1), ones)
            for k in range(3)
        ]
        lane = lax.broadcasted_iota(jnp.int32, sums[0].shape, 1)
        found = jnp.where(lane == 0, sums[0], jnp.where(lane == 1, sums[1], sums[2]))
        grad_conv[stream] = found.reshape(ns * groups, chans, LANES)
    staged.ready(2)
    runner.phase()
    take_edge(place, edge, False)
    edge_cols = edge[2]
    for stream in range(3):

        @pl.loop(0, ns * groups // many, unroll=2)
        def _(i):
            value = rows_of(grad_short, stream, i * many, many)
            side, after = rows_of(conv, stream, i * many, many), rows_of(edge_cols, stream, i * many, many)
            lane = lax.broadcasted_iota(jnp.int32, value.shape, 1)
            near = jnp.where(lane == toks - 1, after[:, 0:1], pltpu.roll(value, toks - 1, 1))
            far = jnp.where(
                lane == toks - 1,
                after[:, 1:2],
                jnp.where(lane == toks - 2, after[:, 0:1], pltpu.roll(value, toks - 2, 1)),
            )
            total = side[:, 2:3] * value + side[:, 1:2] * near + side[:, 0:1] * far
            grad_mixed[stream, pl.ds(i * many, many)] = total.astype(bf16).reshape(many, chans, toks)

    for g in range(groups):

        @pl.loop(1, ns)
        def _(step):
            to_chan(g, step).wait_send()
            to_tok(g, step).wait_send()


def unmix(jobs, layer, mixed, conv, rim, long_out, grad_gated, spec, sig, skip, tables, ids):
    ns = lax.axis_size("seq")
    _, nblocks, chans, toks = mixed.shape
    groups, quarters = nblocks // ns, toks // LANES
    return fused_call(
        "unmix",
        functools.partial(unmix_body, layer=layer),
        [mixed, conv, rim, long_out, grad_gated, *spec, *sig, skip, *tables],
        [
            jax.ShapeDtypeStruct((groups * chans // 8, ns * quarters, 8, LANES), f32),
            jax.ShapeDtypeStruct(mixed.shape, bf16),
            jax.ShapeDtypeStruct(conv.shape, f32),
        ],
        mixer_scratch(ns, groups, quarters, chans)
        + [pltpu.VMEM(mixed.shape, f32), pltpu.VMEM(conv.shape, f32)]
        + edge_scratch(3, nblocks, chans),
        jobs,
        True,
        ids,
    )


def on_device(
    tokens,
    cotangent,
    norm_gains,
    w_in,
    short_conv,
    w_out,
    w_fc,
    w_proj,
    filt_w1,
    filt_b1,
    filt_w2,
    filt_b2,
    filt_w3,
    skip_gain,
    decay_rate,
):
    layers, _, width3 = w_in.shape
    width = width3 // 3
    ns = lax.axis_size("seq")
    devices = lax.axis_size("batch") * ns
    stream = tokens[0].astype(f32)
    toks = stream.shape[0]
    length = toks * ns
    own_chans = width // ns
    chans = 16 if own_chans % 16 == 0 else own_chans
    groups = own_chans // chans
    nblocks = ns * groups
    blocked = (3, nblocks, chans)
    tables = transform_tables(length)
    pos_rows = position_rows(length, filt_w1.shape[1])

    gain_cols, conv_cols = norm_gains.shape[2], short_conv.shape[2]
    small = jnp.concatenate(
        [
            jnp.pad(norm_gains.reshape(2 * layers, gain_cols).astype(f32), ((0, 0), (0, LANES - gain_cols))),
            jnp.pad(short_conv.reshape(3 * layers, conv_cols).astype(f32), ((0, 0), (0, LANES - conv_cols))),
        ],
        axis=0,
    )
    small = jnp.pad(small, ((0, -small.shape[0] % 8), (0, 0)))[None]

    first_w = jnp.pad(
        jnp.concatenate([filt_w1, filt_b1[:, None]], axis=1),
        ((0, 0), (0, FEATURES - filt_w1.shape[1] - 1), (0, 0)),
    )
    hidden = filt_w2.shape[1]
    both = jnp.concatenate([filt_b2, decay_rate], axis=1)
    rates = jnp.broadcast_to(both[:, :, None], both.shape + (LANES,))
    skips = jnp.broadcast_to(
        skip_gain.reshape(layers, -1, 8, 1), (layers, own_chans // 8, 8, LANES)
    )

    mats = (w_in, w_out, w_fc, w_proj)
    jobs = [gather_job(small, 0, GATHER_PLANS[0])]
    jobs += [gather_job(mat, 0, plan) for mat, plan in zip(mats, GATHER_PLANS[1:])]
    jobs += [
        column_job(mat, layer, plan)
        for layer in range(1, layers)
        for mat, plan in zip(mats, COLUMN_PLANS)
    ]
    ids = itertools.count()
    sets = [list(range(layers))] if length <= 8192 else [[layer] for layer in range(layers)]
    kept, specs = [], []
    for part in sets:
        of = slice(part[0], part[-1] + 1)
        filters, found = prepare(
            jobs, pos_rows, first_w[of], filt_w2[of], filt_w3[of], rates[of], tables, ids
        )
        kept.append(filters[:3])
        specs += [filters[3 + 2 * k : 5 + 2 * k] for k in range(len(part))]
        gathered = found if part is sets[0] else gathered
        jobs = []
    small_all = gathered[0].reshape(devices, -1, LANES)
    gains = jnp.swapaxes(small_all[:, : 2 * layers, :gain_cols], 0, 1).reshape(layers, 2, width)
    convs = jnp.swapaxes(
        small_all[:, 2 * layers : 5 * layers, :conv_cols], 0, 1
    ).reshape(layers, 3, width3)
    conv_cols_of = [
        jnp.pad(convs[layer].T, ((0, 0), (0, LANES - 3))).reshape(blocked + (LANES,))
        for layer in range(layers)
    ]
    plain = lambda parts: parts.reshape(-1, parts.shape[-1])
    weights = {(i, 0): plain(gathered[1 + i]) for i in range(4)}
    columns = {
        (i, layer): gathered[1 + 4 * layer + i] for layer in range(1, layers) for i in range(4)
    }

    def plane_jobs(layer):
        keys = [(3, layer)] if layer else []
        keys = [key for key in keys + [(0, layer + 1), (1, layer + 1), (2, layer + 1)] if key in columns]
        return keys, [plane_job(columns[key], plan) for key, plan in zip(keys, PLANE_PLANS)]

    saved = []
    for layer in range(layers):
        in_mat = weights[0, layer]
        normed, inv_std = layer_norm_parts(stream)
        norm_in = (normed * gains[layer, 0]).astype(bf16)
        mixed = contract(in_mat, norm_in, 0, 1).astype(bf16)
        mixed = mixed.reshape(blocked + (toks,))
        keys, jobs = plane_jobs(layer)
        (long_out, gated, sig_re, sig_im, rim), arrived = mix(
            jobs, layer, mixed, conv_cols_of[layer], specs[layer], skips, tables, ids
        )
        weights.update({key: plain(parts) for key, parts in zip(keys, arrived)})
        out_mat, fc_mat, proj_mat = (weights[i, layer] for i in (1, 2, 3))
        gated = gated.reshape(width, toks)
        middle = stream + contract(gated, out_mat, 0, 0)
        normed_mid, inv_mid = layer_norm_parts(middle)
        hidden_in = (normed_mid * gains[layer, 1]).astype(bf16)
        hidden_pre = product(hidden_in, fc_mat)
        hidden_act = lax.optimization_barrier(gelu(hidden_pre).astype(bf16))
        saved.append(
            (normed, inv_std, norm_in, mixed, rim, long_out, gated, (sig_re, sig_im))
            + (normed_mid, inv_mid, hidden_in, hidden_pre, hidden_act)
        )
        stream = middle + product(hidden_act, proj_mat)
    mixed_out, grad = lax.optimization_barrier((stream.astype(bf16), cotangent[0]))
    grad = grad.astype(f32)
    summed = {}
    left_over = []
    small_grads = [None] * layers
    taps_grads = [None] * layers

    def scattered(parts):
        return lax.psum_scatter(parts, ("batch", "seq"), scatter_dimension=0, tiled=False).astype(f32)

    def parts_of(grad_mat):
        return grad_mat.reshape(devices, -1, grad_mat.shape[1])

    for layer in reversed(range(layers)):
        in_mat, out_mat, fc_mat, proj_mat = (weights[i, layer] for i in range(4))
        (normed, inv_std, norm_in, mixed, rim, long_out, gated, sig) = saved[layer][:8]
        (normed_mid, inv_mid, hidden_in, hidden_pre, hidden_act) = saved[layer][8:]
        grad_top = grad.astype(bf16)
        grad_act = contract(grad_top, proj_mat, 1, 1)
        grad_proj = contract(hidden_act, grad_top, 0, 0).astype(bf16)
        grad_pre = (grad_act * gelu_slope(hidden_pre)).astype(bf16)
        grad_hidden = contract(grad_pre, fc_mat, 1, 1)
        grad_fc = contract(hidden_in, grad_pre, 0, 0).astype(bf16)
        grad_gain_mid = jnp.sum(grad_hidden * normed_mid, axis=0)
        grad_middle = grad + norm_back(grad_hidden * gains[layer, 1], normed_mid, inv_mid)
        grad_mix = grad_middle.astype(bf16)
        grad_gated = contract(out_mat, grad_mix, 1, 1).reshape(nblocks, chans, toks)
        grad_out = contract(gated, grad_mix, 1, 0).astype(bf16)
        grad_gated, grad_proj = lax.optimization_barrier((grad_gated, grad_proj))
        if layer == 0:
            pending = left_over + [((3, layer), parts_of(grad_proj)), ((2, layer), parts_of(grad_fc))]
            left_over = [((1, layer), parts_of(grad_out))]
        else:
            summed[3, layer] = scattered(parts_of(grad_proj))
            pending = left_over + [((2, layer), parts_of(grad_fc)), ((1, layer), parts_of(grad_out))]
            left_over = []
        (taps_grads[layer], grad_mixed, grad_conv), arrived = unmix(
            [reduce_job(parts, plan) for (_, parts), plan in zip(pending, REDUCE_PLANS)]
            if layer
            else [plane_reduce_job(parts, plan) for (_, parts), plan in zip(pending, PLANE_REDUCE_PLANS)],
            layer, mixed, conv_cols_of[layer], rim, long_out, grad_gated, specs[layer], sig, skips, tables, ids
        )
        if layer == 0:
            half_way = [(key, part) for (key, _), part in zip(pending, arrived)]
        else:
            summed.update({key: total for (key, _), total in zip(pending, arrived)})
        grad_mixed = grad_mixed.reshape(width3, toks)
        grad_norm_in = contract(grad_mixed, in_mat, 0, 1)
        grad_in = contract(norm_in, grad_mixed, 0, 1).astype(bf16)
        grad_gain_in = jnp.sum(grad_norm_in * normed, axis=0)
        grad = grad_middle + norm_back(grad_norm_in * gains[layer, 0], normed, inv_std)
        left_over.append(((0, layer), parts_of(grad_in)))
        small_grads[layer] = (
            jnp.stack([grad_gain_in, grad_gain_mid]),
            jnp.swapaxes(grad_conv.reshape(width3, LANES)[:, :3], 0, 1),
        )

    def rows_for(values, cols):
        pieces = jnp.swapaxes(values.reshape(values.shape[0], devices, cols), 0, 1)
        return jnp.pad(pieces, ((0, 0), (0, 0), (0, LANES - cols)))

    small_rows = jnp.concatenate(
        [rows_for(small_grads[layer][0], gain_cols) for layer in range(layers)]
        + [rows_for(small_grads[layer][1], conv_cols) for layer in range(layers)],
        axis=1,
    )
    small_rows = jnp.pad(small_rows, ((0, 0), (0, -small_rows.shape[1] % 8), (0, 0)))
    emb = filt_w1.shape[1]
    left_over.reverse()
    left_over.append(("small", small_rows))
    each, shared = hidden + 8, hidden
    by_column, by_all = [], []
    jobs = [reduce_job(parts, plan) for (_, parts), plan in zip(left_over, LAST_PLANS)]
    jobs += [chain_reduce_job(part, plan) for (_, part), plan in zip(half_way, CHAIN_PLANS)]
    for part, acts in zip(sets, kept):
        of = slice(part[0], part[-1] + 1)
        (totals,), arrived = last(
            jobs, pos_rows, filt_w2[of], filt_w3[of], rates[of], acts, taps_grads[of], ids
        )
        if part is sets[0]:
            summed.update({key: total for (key, _), total in zip(left_over + half_way, arrived)})
        jobs = []
        by_column.append(totals[: len(part) * each].reshape(-1, each, LANES))
        by_all.append(totals[len(part) * each :].reshape(-1, shared, LANES))
    by_column, by_all = jnp.concatenate(by_column), jnp.concatenate(by_all)
    small_sum = summed["small"]
    block = [jnp.stack([summed[i, layer] for layer in range(layers)]) for i in range(4)]
    gains_grad = small_sum[: 2 * layers, :gain_cols].reshape(layers, 2, gain_cols)
    conv_grad = small_sum[2 * layers : 5 * layers, :conv_cols].reshape(layers, 3, conv_cols)
    return (
        mixed_out[None],
        grad[None],
        gains_grad,
        block[0],
        conv_grad,
        block[1],
        block[2],
        block[3],
        by_all[:, :emb, :hidden],
        by_all[:, emb, :hidden],
        by_all[:, :, hidden : 2 * hidden],
        by_all[:, FEATURES + emb - 32, :hidden],
        by_column[:, :hidden, :own_chans],
        by_column[:, hidden, :own_chans],
    )


def solution(mesh):
    both = ("batch", "seq")
    in_specs = (
        P("batch", "seq", None),
        P("batch", "seq", None),
        P(None, None, both),
        P(None, both, None),
        P(None, None, both),
        P(None, both, None),
        P(None, both, None),
        P(None, both, None),
        P(),
        P(),
        P(),
        P(),
        P(None, None, "seq"),
        P(None, "seq"),
        P(None, "seq"),
    )
    out_specs = in_specs[:14]
    return jax.shard_map(
        on_device, mesh=mesh, in_specs=in_specs, out_specs=out_specs, check_vma=False
    )
```

```python
import functools
import itertools
import math

import jax
import jax.numpy as jnp
import numpy as np
from jax import lax
from jax.experimental import pallas as pl
from jax.experimental.pallas import tpu as pltpu
from jax.sharding import PartitionSpec as P

MESH = pl.DeviceIdType.MESH
LANES = 128
VMEM_LIMIT = 58 * 1024 * 1024
GATHER_PLANS = [[0, 1, 3, 5, 7, 9, 12], [0, 1, 3, 5, 7, 9, 12], [0, 2, 4, 6, 8, 10, 12], [0, 2, 5, 8, 10, 12, 14], [0, 3, 6, 9, 12, 14, 16]]
COLUMN_PLANS = [[2, 5, 8, 11, 14], [2, 5, 8, 11, 14], [3, 7, 10, 13, 15], [4, 8, 12, 14, 16]]
PLANE_PLANS = [[0, 4, 7, 11], [0, 5, 8, 11], [0, 6, 9, 11]]
PLANE_REDUCE_PLANS = [[0, 1, 1, 7, 7, 11, 11, 12], [0, 1, 1, 9, 9, 12, 12, 12], [0, 1, 1, 11, 11, 12, 12, 12]]
UNMIX_CHAIN_PLANS = [[0, 8, 10, 12], [0, 8, 10, 12]]
CHAIN_PLANS = [[0, 1, 3, 6], [1, 2, 4, 7], [2, 3, 6, 9]]
LAST_PLANS = [[0, 1, 1, 4, 4, 7, 7, 9], [0, 2, 2, 5, 5, 7, 8, 9], [0, 2, 2, 5, 5, 7, 8, 9]]
f32 = jnp.float32
bf16 = jnp.bfloat16


def product(left_mat, right_mat):
    return jnp.dot(left_mat, right_mat, preferred_element_type=f32)


def contract(left_mat, right_mat, left_dim, right_dim):
    return lax.dot_general(
        left_mat, right_mat, (((left_dim,), (right_dim,)), ((), ())), preferred_element_type=f32
    )


def gelu(x):
    return x * (0.5 + 0.5 * jnp.tanh(x * (GELU_SCALE + GELU_SCALE * GELU_CUBE * (x * x))))


def gelu_slope(x):
    square = x * x
    turn = jnp.tanh(x * (GELU_SCALE + GELU_SCALE * GELU_CUBE * square))
    half = 0.5 + 0.5 * turn
    steep = GELU_SCALE + 3.0 * GELU_SCALE * GELU_CUBE * square
    return half * (1.0 + x * (1.0 - turn) * steep)


def layer_norm_parts(stream):
    mean_val = jnp.mean(stream, axis=-1, keepdims=True)
    centered = stream - mean_val
    inv_std = lax.rsqrt(jnp.mean(centered * centered, axis=-1, keepdims=True) + 1e-05)
    return (centered * inv_std, inv_std)


def norm_back(grad_normed, normed, inv_std):
    mean_grad = jnp.mean(grad_normed, axis=-1, keepdims=True)
    mean_cross = jnp.mean(grad_normed * normed, axis=-1, keepdims=True)
    return inv_std * (grad_normed - mean_grad - normed * mean_cross)


def split_bf16(table):
    high = table.astype(np.float32).astype(jnp.bfloat16)
    return high, (table - high.astype(np.float64)).astype(np.float32).astype(jnp.bfloat16)


def transform_tables(length):
    blocks = min(length // LANES, 32)
    inside = length // blocks
    n1 = np.arange(blocks)
    n2 = np.arange(inside)
    outer = 2 * np.pi * ((n1[:, None] * (4 * n1[None, :] + 1)) % (4 * blocks)) / (4 * blocks)
    eye = np.eye(8)
    forward = np.concatenate([np.cos(outer).T, -np.sin(outer).T], axis=0)
    left_fwd = np.kron(forward, eye)
    left_inv = np.kron(np.concatenate([np.cos(outer), -np.sin(outer)], axis=1), eye) / length
    inner = 2 * np.pi * ((n2[:, None] * n2[None, :]) % inside) / inside
    cos2, sin2 = np.cos(inner), np.sin(inner)
    right_fwd = np.block([[cos2, -sin2], [sin2, cos2]])
    right_inv = np.block([[cos2, sin2], [-sin2, cos2]])
    twist = 2 * np.pi * (n2[None, :] * (4 * n1[:, None] + 1)) / (4 * length)
    twist_cos = np.repeat(np.cos(twist), 8, axis=0).astype(np.float32)
    twist_sin = np.repeat(np.sin(twist), 8, axis=0).astype(np.float32)
    tables = []
    for table, axis in ((left_fwd, 1), (right_fwd, 0), (left_inv, 1), (right_inv, 0)):
        high, low = split_bf16(table)
        tables.append(jnp.asarray(np.concatenate([high, low, high], axis=axis)))
    return tuple(tables) + (jnp.asarray(twist_cos), jnp.asarray(twist_sin))


TABLES = 6


def in_two(value):
    high = value.astype(bf16)
    return high, (value - high.astype(f32)).astype(bf16)


def left_product(left, right):
    high, low = in_two(right)
    return product(left[...], jnp.concatenate([high, high, low], axis=0))


def right_product(left, right):
    high, low = in_two(left)
    return product(jnp.concatenate([high, high, low], axis=1), right[...])


def beside(parts):
    return jnp.concatenate(parts, axis=1) if len(parts) > 1 else parts[0]


def below(parts):
    return jnp.concatenate(parts, axis=0) if len(parts) > 1 else parts[0]


def to_points(xs, tables, exact):
    left, right, _, _, twist_cos, twist_sin = tables
    rows, inside = twist_cos.shape
    flat = []
    for x in xs:
        split = x.reshape(rows // 8, inside // LANES, 8, LANES)
        line = [split[:, k] for k in range(inside // LANES)]
        flat.append((jnp.concatenate(line, axis=2) if len(line) > 1 else line[0]).reshape(rows, inside))
    flat = beside(flat)
    if exact:
        flat = flat.astype(bf16)
        turned = product(left[:, : 2 * rows], jnp.concatenate([flat, flat], axis=0))
    else:
        turned = left_product(left, flat)
    cos, sin = twist_cos[...], twist_sin[...]
    both = []
    for k in range(len(xs)):
        re, im = [turned[part, k * inside : (k + 1) * inside] for part in (slice(0, rows), slice(rows, 2 * rows))]
        both.append(jnp.concatenate([re * cos + im * sin, im * cos - re * sin], axis=1))
    points = right_product(below(both), right)
    return [
        (points[k * rows : (k + 1) * rows, :inside], points[k * rows : (k + 1) * rows, inside:])
        for k in range(len(xs))
    ]


def from_points(pairs, tables):
    _, _, left, right, twist_cos, twist_sin = tables
    rows, inside = twist_cos.shape
    back = right_product(below([jnp.concatenate(pair, axis=1) for pair in pairs]), right)
    cos, sin = twist_cos[...], twist_sin[...]
    both = []
    for k in range(len(pairs)):
        re, im = back[k * rows : (k + 1) * rows, :inside], back[k * rows : (k + 1) * rows, inside:]
        both.append(jnp.concatenate([re * cos - im * sin, re * sin + im * cos], axis=0))
    found = left_product(left, beside(both))
    results = []
    for k in range(len(pairs)):
        flat = found[:, k * inside : (k + 1) * inside].reshape(rows // 8, 8, inside)
        split = [flat[:, None, :, q * LANES : (q + 1) * LANES] for q in range(inside // LANES)]
        line = jnp.concatenate(split, axis=1) if len(split) > 1 else split[0]
        results.append(line.reshape(-1, 8, LANES))
    return results


FEATURES = 48
SPAN = 512
GELU_SCALE = math.sqrt(2.0 / math.pi)
GELU_CUBE = 0.044715


def position_rows(length, emb_width):
    positions = np.arange(length, dtype=np.int64)
    bands = np.arange(1, (emb_width - 1) // 2 + 1, dtype=np.int64)
    angles = 2.0 * np.pi / length * ((bands[:, None] * positions[None, :]) % length)
    table = np.zeros((FEATURES, length), np.float32)
    table[0] = positions / length
    table[1 : 1 + bands.size] = np.cos(angles)
    table[1 + bands.size : emb_width] = np.sin(angles)
    table[emb_width] = 1.0
    return jnp.asarray(table)


def near_dot(left, right, left_dim, right_dim):
    left_high, left_low = in_two(left)
    right_high, right_low = in_two(right)
    return contract(
        jnp.concatenate([left_high, left_high, left_low], axis=left_dim),
        jnp.concatenate([right_high, right_low, right_high], axis=right_dim),
        left_dim,
        right_dim,
    )


def in_three(value):
    high = value.astype(bf16)
    rest = value - high.astype(f32)
    middle = rest.astype(bf16)
    return high, middle, (rest - middle.astype(f32)).astype(bf16)


def full_dot(left, right):
    a, b, c = in_three(left)
    d, e, f = in_three(right)
    return contract(
        jnp.concatenate([a, a, a, b, b, c], axis=0), jnp.concatenate([d, e, f, d, e, d], axis=0), 0, 0
    )


def sin_cos(x):
    turns = jnp.round(x * (2.0 / math.pi))
    r = ((x - turns * 1.5703125) - turns * 4.837512969970703125e-4) - turns * 7.54978995489188216e-8
    z = r * r
    sine = r + r * z * (-1.6666654611e-1 + z * (8.3321608736e-3 - z * 1.9515295891e-4))
    cosine = 1.0 - 0.5 * z + z * z * (
        4.166664568298827e-2 + z * (-1.388731625493765e-3 + z * 2.443315711809948e-5)
    )
    turn = lax.bitwise_and(turns.astype(jnp.int32), 3)
    odd = lax.bitwise_and(turn, 1) == 1
    first = jnp.where(odd, cosine, sine)
    second = jnp.where(odd, sine, cosine)
    return (
        jnp.where(turn >= 2, -first, first),
        jnp.where(jnp.logical_or(turn == 1, turn == 2), -second, second),
    )


def window_of(decay, start, shape, length):
    lane = lax.broadcasted_iota(jnp.int32, shape, 1) + start
    return jnp.exp(lane.astype(f32) * (-1.0 / length) * decay)


def filter_span(layer, start, pos, first_w, second_w, third_w, rates, acts, shaped, squares):
    length = pos.shape[1]
    at = pl.ds(start, SPAN)
    act, slope = sin_cos(full_dot(first_w[layer], pos[:, at]))
    acts[layer, 0, :, at] = act
    acts[layer, 1, :, at] = slope
    act, slope = sin_cos(full_dot(second_w[layer], act) + rates[layer, : act.shape[0], :1])
    acts[layer, 2, :, at] = act
    acts[layer, 3, :, at] = slope
    raw = near_dot(third_w[layer], act, 0, 0)
    value = raw * window_of(rates[layer, act.shape[0] :, :1], start, raw.shape, length)
    shaped[layer, :, at] = value
    squares[layer] += jnp.sum(value * value, axis=1, keepdims=True)


def filter_points(group, tables, shaped, squares, specs):
    layers, _, length = shaped.shape
    rows = pl.ds(pl.multiple_of(group * 8, 8), 8)
    xs = []
    for layer in range(layers):
        scale = lax.rsqrt(squares[layer, rows, :1] * (1.0 / length) + 1e-05) * length ** (-0.5)
        value = shaped[layer, rows, :] * scale
        line = [value[:, i * LANES : (i + 1) * LANES][None] for i in range(length // LANES)]
        xs.append(jnp.concatenate(line, axis=0))
    for layer, (re, im) in enumerate(to_points(xs, tables, False)):
        specs[2 * layer][group] = re
        specs[2 * layer + 1][group] = im


def filter_back_dot(layer, start, shaped, grad_taps, dots):
    at = pl.ds(start, SPAN)
    grad = taps_span(grad_taps, start)
    dots[layer] += jnp.sum(shaped[layer, :, at] * grad, axis=1, keepdims=True)


def taps_span(grad_taps, start):
    first = lax.div(start, LANES)
    pieces = []
    for i in range(SPAN // LANES):
        piece = grad_taps[:, first + i]
        pieces.append(piece.reshape(-1, LANES))
    return jnp.concatenate(pieces, axis=1)


def filter_back_span(
    layer, start, pos, second_w, third_w, rates, acts, shaped, squares, grad_taps, dots, grads
):
    length = pos.shape[1]
    at = pl.ds(start, SPAN)
    grad_third, grad_second, grad_first = grads
    mean_square = squares[layer][:, :1] * (1.0 / length)
    scale = lax.rsqrt(mean_square + 1e-05)
    cross = dots[layer][:, :1] * (1.0 / length) * scale * scale
    grad = taps_span(grad_taps, start)
    value = shaped[layer, :, at]
    grad = (grad - value * cross) * (scale * length ** (-0.5))
    grad = grad * window_of(rates[layer, second_w.shape[1] :, :1], start, grad.shape, length)
    grad_third[layer] += near_dot(acts[layer, 2, :, at], grad, 1, 1)
    second = near_dot(third_w[layer], grad, 1, 0) * acts[layer, 3, :, at]
    grad_second[layer] += near_dot(acts[layer, 0, :, at], second, 1, 1)
    first = near_dot(second_w[layer], second, 1, 0) * acts[layer, 1, :, at]
    grad_first[layer] += near_dot(pos[:, at], jnp.concatenate([first, second], axis=0), 1, 1)


class Place:
    def __init__(self, ns):
        self.nz = ns // 2
        self.b = lax.axis_index("batch")
        self.s = lax.axis_index("seq")
        self.z = lax.div(self.s, 2)
        self.c = lax.rem(self.s, 2)
        self.x_peer = (lax.bitwise_xor(self.b, 1), self.s)
        self.y_peer = (lax.bitwise_xor(self.b, 2), self.s)
        self.core_peer = (self.b, lax.bitwise_xor(self.s, 1))
        self.up_peer = (self.b, lax.min(self.s + 2, ns - 1))
        self.down_peer = (self.b, lax.max(self.s - 2, 0))


def remote(src, dst, send, recv, peer):
    return pltpu.make_async_remote_copy(
        src_ref=src, dst_ref=dst, send_sem=send, recv_sem=recv, device_id=peer, device_id_type=MESH
    )


def greet(place, seq_peers):
    bar = pltpu.get_barrier_semaphore()

    def hello(peer):
        pl.semaphore_signal(bar, inc=1, device_id=peer, device_id_type=MESH)

    hello(place.x_peer)
    hello(place.y_peer)
    if seq_peers:
        ns = 2 * place.nz
        for step in range(1, ns):
            hello((place.b, lax.rem(place.s + step, ns)))
        pl.semaphore_wait(bar, 2 + ns - 1)
    else:
        hello(place.core_peer)
        pl.when(place.z + 1 < place.nz)(lambda: hello(place.up_peer))
        pl.when(place.z > 0)(lambda: hello(place.down_peer))
        ends = jnp.where(place.z == 0, 1, 0) + jnp.where(place.z == place.nz - 1, 1, 0)
        pl.semaphore_wait(bar, 5 - ends)


class Job:
    def __init__(self, arrays, results, scratch, task, plan):
        self.arrays, self.results, self.scratch, self.task = arrays, results, scratch, task
        self.plan = plan


class Runner:
    def __init__(self, tasks, plans):
        self.tasks = [[task, list(plan)] for task, plan in zip(tasks, plans, strict=True)]
        self.now = 0

    def add(self, task, steps):
        self.tasks.insert(0, [task, list(range(self.now, self.now + steps))])

    def step(self, entry):
        if next(entry[0], "end") == "end":
            self.tasks.remove(entry)

    def phase(self):
        for entry in list(self.tasks):
            while entry[1] and entry[1][0] <= self.now:
                entry[1].pop(0)
                self.step(entry)
        self.now += 1

    def finish(self):
        while any(entry[1] for entry in self.tasks):
            self.phase()
        while self.tasks:
            for entry in list(self.tasks):
                self.step(entry)


def room(items):
    total = 0
    for item in items:
        if len(item.shape) < 2 or not jnp.issubdtype(item.dtype, jnp.floating):
            continue
        size = jnp.dtype(item.dtype).itemsize
        *outer, rows, lanes = item.shape
        tile = 32 // size
        total += math.prod(outer) * -(-rows // tile) * tile * -(-lanes // LANES) * LANES * size
    return total


def fused_call(name, body, arrays, results, scratch, jobs, seq_peers, ids):
    free = VMEM_LIMIT - room([*arrays, *results, *scratch])
    if body is not None and room([item for job in jobs for item in job.scratch]) > free:
        found, _ = fused_call(name, body, arrays, results, scratch, [], seq_peers, ids)
        alone = [fused_call(name + "_job", None, [], [], [], [job], seq_peers, ids)[1][0] for job in jobs]
        return found, alone
    collective_id = next(ids)
    ns = lax.axis_size("seq")
    stages = [pltpu.VMEM(a.shape, a.dtype) for a in [*arrays, *results]]
    stages.append(pltpu.SemaphoreType.DMA((max(1, len(stages)),)))
    counts = [len(arrays)] + [len(j.arrays) for j in jobs]
    counts += [len(results)] + [len(j.results) for j in jobs]
    counts += [len(scratch)] + [len(j.scratch) for j in jobs] + [len(stages)]
    n = 1 + len(jobs)

    def kernel(*refs):
        parts, start = [], 0
        for count in counts:
            parts.append(refs[start : start + count])
            start += count
        *held, sems = parts[3 * n]
        ins, outs = held[: len(arrays)], held[len(arrays) :]
        staged = Staged(parts[0], ins, outs, parts[n], sems)
        place = Place(ns)
        greet(place, seq_peers)
        tasks = [
            job.task(place, *parts[1 + k], *parts[n + 1 + k], parts[2 * n + 1 + k])
            for k, job in enumerate(jobs)
        ]
        runner = Runner(tasks, [job.plan for job in jobs])
        if body is not None:
            body(place, runner, ins, outs, parts[2 * n], staged)
        runner.finish()
        staged.finish()

    hbm = pl.BlockSpec(memory_space=pl.ANY)
    flat = lambda pick: [item for job in jobs for item in pick(job)]
    found = pl.pallas_call(
        kernel,
        out_shape=list(results) + flat(lambda j: j.results),
        in_specs=[hbm] * sum(counts[:n]),
        out_specs=[hbm] * sum(counts[n : 2 * n]),
        scratch_shapes=list(scratch) + flat(lambda j: j.scratch) + stages,
        compiler_params=pltpu.CompilerParams(
            collective_id=collective_id, has_side_effects=True, vmem_limit_bytes=VMEM_LIMIT
        ),
        name=name,
    )(*arrays, *flat(lambda j: j.arrays))
    return found[: counts[n]], found[counts[n] :]


class Staged:
    def __init__(self, sources, ins, outs, targets, sems):
        self.loads = [pltpu.make_async_copy(a, b, sems.at[k]) for k, (a, b) in enumerate(zip(sources, ins))]
        first = len(self.loads)
        self.stores = [
            pltpu.make_async_copy(a, b, sems.at[first + k]) for k, (a, b) in enumerate(zip(outs, targets))
        ]
        self.loading = set(range(first))
        self.storing = set()
        for load in self.loads:
            load.start()

    def need(self, *which):
        for k in which:
            if k in self.loading:
                self.loading.remove(k)
                self.loads[k].wait()

    def ready(self, *which):
        for k in which:
            self.storing.add(k)
            self.stores[k].start()

    def finish(self):
        self.need(*sorted(self.loading))
        self.ready(*[k for k in range(len(self.stores)) if k not in self.storing])
        for store in self.stores:
            store.wait()


def gather_sems(nz):
    return [
        pltpu.SemaphoreType.DMA((1,)),
        pltpu.SemaphoreType.DMA((2, nz)),
        pltpu.SemaphoreType.DMA((nz,)),
        pltpu.SemaphoreType.DMA((4, nz)),
        pltpu.SemaphoreType.DMA((4, nz)),
        pltpu.SemaphoreType.DMA((4,)),
        pltpu.SemaphoreType.DMA((4,)),
    ]


def gather_task(place, src, dst, sems):
    one, chain_send, chain_recv, send, recv, core_send, core_recv = sems
    b, z, c, nz = place.b, place.z, place.c, place.nz
    bx, by, bd = place.x_peer[0], place.y_peer[0], lax.bitwise_xor(b, 3)
    local = pltpu.make_async_copy(src, dst.at[b, z, c], one.at[0])

    def chain(source, shard, up):
        row = 0 if up else 1
        peer = place.up_peer if up else place.down_peer
        return remote(source, dst.at[b, shard, c], chain_send.at[row, shard], chain_recv.at[shard], peer)

    def across(source, shard, along):
        peer = place.y_peer if along else place.x_peer
        return remote(source, dst.at[b, shard, c], send.at[along, shard], recv.at[along, shard], peer)

    def onward(shard, along):
        peer = place.y_peer if along else place.x_peer
        part = dst.at[bx if along else by, shard, c]
        return remote(part, part, send.at[2 + along, shard], recv.at[2 + along, shard], peer)

    def core(batch, i):
        part = dst.at[batch, :, c]
        return remote(part, part, core_send.at[i], core_recv.at[i], place.core_peer)

    def pass_on(shard):
        across(src, shard, 0).wait_recv()
        across(src, shard, 1).wait_recv()
        even = lax.rem(shard, 2) == 0
        pl.when(even)(lambda: onward(shard, 1).start())
        pl.when(jnp.logical_not(even))(lambda: onward(shard, 0).start())

    def pass_on_from(hop):
        if hop == 0:
            pass_on(z)
        else:
            pl.when(z - hop >= 0)(lambda: pass_on(z - hop))
            pl.when(z + hop < nz)(lambda: pass_on(z + hop))

    local.start()
    pl.when(z + 1 < nz)(lambda: chain(src, z, True).start())
    pl.when(z > 0)(lambda: chain(src, z, False).start())
    across(src, z, 0).start()
    across(src, z, 1).start()
    yield
    for hop in range(1, nz):
        below, above = z - hop, z + hop

        @pl.when(below >= 0)
        def _():
            chain(src, below, True).wait_recv()
            part = dst.at[b, below, c]
            pl.when(z + 1 < nz)(lambda: chain(part, below, True).start())
            across(part, below, 0).start()
            across(part, below, 1).start()

        @pl.when(above < nz)
        def _():
            chain(src, above, False).wait_recv()
            part = dst.at[b, above, c]
            pl.when(z > 0)(lambda: chain(part, above, False).start())
            across(part, above, 0).start()
            across(part, above, 1).start()

        pass_on_from(hop - 1)
        yield
    local.wait()
    core(b, 0).start()
    pass_on_from(nz - 1)
    core(bx, 1).start()
    core(by, 2).start()
    yield
    for shard in range(nz):
        onward(shard, 1 - shard % 2).wait_recv()
    core(bd, 3).start()
    yield
    for hop in range(nz):
        pl.when(jnp.logical_and(z >= hop, z + 1 < nz))(lambda: chain(src, z - hop, True).wait_send())
        pl.when(jnp.logical_and(z + hop < nz, z > 0))(lambda: chain(src, z + hop, False).wait_send())
    for shard in range(nz):
        across(src, shard, 0).wait_send()
        across(src, shard, 1).wait_send()
        onward(shard, 1 - shard % 2).wait_send()
    for i in range(4):
        core(b, i).wait()
    yield


def gather_job(array, layer, plan):
    nz = lax.axis_size("seq") // 2
    result = jax.ShapeDtypeStruct((4, nz, 2) + array.shape[1:], array.dtype)
    task = lambda place, src, dst, sems: gather_task(place, src.at[layer], dst, sems)
    return Job([array], [result], gather_sems(nz), task, plan)


def column_task(place, src, dst, sems):
    one, chain_send, chain_recv = sems
    z, nz = place.z, place.nz
    local = pltpu.make_async_copy(src, dst.at[z], one.at[0])

    def chain(source, shard, up):
        row = 0 if up else 1
        peer = place.up_peer if up else place.down_peer
        return remote(source, dst.at[shard], chain_send.at[row, shard], chain_recv.at[shard], peer)

    local.start()
    pl.when(z + 1 < nz)(lambda: chain(src, z, True).start())
    pl.when(z > 0)(lambda: chain(src, z, False).start())
    yield
    for hop in range(1, nz):
        below, above = z - hop, z + hop

        @pl.when(below >= 0)
        def _():
            chain(src, below, True).wait_recv()
            pl.when(z + 1 < nz)(lambda: chain(dst.at[below], below, True).start())

        @pl.when(above < nz)
        def _():
            chain(src, above, False).wait_recv()
            pl.when(z > 0)(lambda: chain(dst.at[above], above, False).start())

        yield
    for hop in range(nz):
        pl.when(jnp.logical_and(z >= hop, z + 1 < nz))(lambda: chain(src, z - hop, True).wait_send())
        pl.when(jnp.logical_and(z + hop < nz, z > 0))(lambda: chain(src, z + hop, False).wait_send())
    local.wait()
    yield


def column_job(array, layer, plan):
    nz = lax.axis_size("seq") // 2
    result = jax.ShapeDtypeStruct((nz,) + array.shape[1:], array.dtype)
    sems = [
        pltpu.SemaphoreType.DMA((1,)),
        pltpu.SemaphoreType.DMA((2, nz)),
        pltpu.SemaphoreType.DMA((nz,)),
    ]
    task = lambda place, src, dst, sems: column_task(place, src.at[layer], dst, sems)
    return Job([array], [result], sems, task, plan)


def plane_task(place, src, dst, sems):
    one, send, recv, core_send, core_recv = sems
    b, c, nz = place.b, place.c, place.nz
    bx, by, bd = place.x_peer[0], place.y_peer[0], lax.bitwise_xor(b, 3)
    half = nz // 2
    local = pltpu.make_async_copy(src, dst.at[b, :, c], one.at[0])
    over_x = remote(src, dst.at[b, :, c], send.at[0], recv.at[0], place.x_peer)
    over_y = remote(src, dst.at[b, :, c], send.at[1], recv.at[1], place.y_peer)
    low, high = pl.ds(0, half), pl.ds(half, nz - half)
    far_y = remote(dst.at[bx, low, c], dst.at[bx, low, c], send.at[2], recv.at[2], place.y_peer)
    far_x = remote(dst.at[by, high, c], dst.at[by, high, c], send.at[3], recv.at[3], place.x_peer)

    def core(source, batch, i):
        return remote(source, dst.at[batch, :, c], core_send.at[i], core_recv.at[i], place.core_peer)

    over_x.start()
    over_y.start()
    core(src, b, 0).start()
    local.start()
    yield
    over_x.wait_recv()
    far_y.start()
    over_y.wait_recv()
    far_x.start()
    core(dst.at[bx, :, c], bx, 1).start()
    core(dst.at[by, :, c], by, 2).start()
    yield
    far_y.wait_recv()
    far_x.wait_recv()
    core(dst.at[bd, :, c], bd, 3).start()
    yield
    for copy in (over_x, over_y, far_y, far_x):
        copy.wait_send()
    local.wait()
    for i in range(4):
        core(src, b, i).wait()
    yield


def plane_job(array, plan):
    nz = array.shape[0]
    result = jax.ShapeDtypeStruct((4, nz, 2) + array.shape[1:], array.dtype)
    sems = [pltpu.SemaphoreType.DMA((1,))] + [pltpu.SemaphoreType.DMA((4,))] * 4
    return Job([array], [result], sems, plane_task, plan)


def reduce_scratch(nz, shape, dtype):
    half = (nz,) + shape
    return [
        pltpu.VMEM((4,) + half, dtype),
        pltpu.VMEM((4,) + half, dtype),
        pltpu.VMEM((5,) + half, dtype),
        pltpu.VMEM(shape, f32),
        pltpu.SemaphoreType.DMA((1,)),
        pltpu.SemaphoreType.DMA((3, nz)),
        pltpu.SemaphoreType.DMA((5, nz)),
        pltpu.SemaphoreType.DMA((5, nz)),
    ]


def far_first(place):
    nz = place.nz
    tables = [sorted(range(nz), key=lambda k: (-abs(k - z), k)) for z in range(nz)]
    order = []
    for j in range(nz):
        shard = jnp.int32(tables[0][j])
        for z in range(1, nz):
            shard = jnp.where(place.z == z, tables[z][j], shard)
        order.append(shard)
    return order


def reduce_task(place, src, out, scratch):
    acc, other, box, total, one, near, send, recv = scratch
    kind = acc.dtype
    b, z, c, nz = place.b, place.z, place.c, place.nz
    bx, by, bd = place.x_peer[0], place.y_peer[0], lax.bitwise_xor(b, 3)
    far, via_x, via_y, up, down = range(5)
    order = far_first(place)
    halves = [range(0, nz // 2), range(nz // 2, nz)]

    def add(target, shard, *lanes):
        value = acc[target, shard].astype(f32)
        for lane in lanes:
            value += box[lane, shard].astype(f32)
        acc[target, shard] = value.astype(kind)

    def move(part, shard, lane, peer):
        return remote(acc.at[part, shard], box.at[lane, shard], send.at[lane, shard], recv.at[lane, shard], peer)

    def mine(shard):
        return pltpu.make_async_copy(src.at[:, shard, c], acc.at[:, shard], near.at[0, shard])

    def core(shard):
        return remote(src.at[:, shard, 1 - c], other.at[:, shard], near.at[1, shard], near.at[2, shard], place.core_peer)

    for shard in order:
        core(shard).start()
        mine(shard).start()
    yield
    for half in halves:
        for j in half:
            shard = order[j]
            mine(shard).wait()
            core(shard).wait_recv()

            @pl.loop(0, 4)
            def _(part):
                acc[part, shard] = (
                    acc[part, shard].astype(f32) + other[part, shard].astype(f32)
                ).astype(kind)

            if j % 2 == 0:
                move(bd, shard, far, place.x_peer).start()
                move(bx, shard, via_x, place.x_peer).start()
            else:
                move(bd, shard, far, place.y_peer).start()
                move(by, shard, via_y, place.y_peer).start()
        yield
    for half in halves:
        for j in half:
            shard = order[j]
            move(bd, shard, far, place.x_peer).wait_recv()
            if j % 2 == 0:
                add(by, shard, far)
                move(by, shard, via_y, place.y_peer).start()
            else:
                add(bx, shard, far)
                move(bx, shard, via_x, place.x_peer).start()
        yield
    for half in halves:
        for j in half:
            shard = order[j]
            move(bx, shard, via_x, place.x_peer).wait_recv()
            move(by, shard, via_y, place.y_peer).wait_recv()
            add(b, shard, via_x, via_y)

            @pl.when(z < shard)
            def _():
                @pl.when(z > 0)
                def _():
                    move(b, shard, up, place.up_peer).wait_recv()
                    add(b, shard, up)

                move(b, shard, up, place.up_peer).start()

            @pl.when(z > shard)
            def _():
                @pl.when(z + 1 < nz)
                def _():
                    move(b, shard, down, place.down_peer).wait_recv()
                    add(b, shard, down)

                move(b, shard, down, place.down_peer).start()

        yield
    total[...] = acc[b, z].astype(f32)

    @pl.when(z > 0)
    def _():
        move(b, z, up, place.up_peer).wait_recv()
        total[...] += box[up, z].astype(f32)

    @pl.when(z + 1 < nz)
    def _():
        move(b, z, down, place.down_peer).wait_recv()
        total[...] += box[down, z].astype(f32)

    result = pltpu.make_async_copy(total, out, one.at[0])
    result.start()
    for shard in range(nz):
        core(shard).wait_send()
        for lane in (far, via_x, via_y):
            move(b, shard, lane, place.x_peer).wait_send()
        pl.when(z < shard)(lambda: move(b, shard, up, place.up_peer).wait_send())
        pl.when(z > shard)(lambda: move(b, shard, down, place.down_peer).wait_send())
    result.wait()
    yield


def plane_reduce_task(place, src, out, scratch):
    acc, other, box, one, near, send, recv = scratch
    kind = acc.dtype
    b, z, c, nz = place.b, place.z, place.c, place.nz
    bx, by, bd = place.x_peer[0], place.y_peer[0], lax.bitwise_xor(b, 3)
    far, via_x, via_y = range(3)
    order = far_first(place)
    halves = [range(0, nz // 2), range(nz // 2, nz)]

    def add(target, shard, *lanes):
        value = acc[target, shard].astype(f32)
        for lane in lanes:
            value += box[lane, shard].astype(f32)
        acc[target, shard] = value.astype(kind)

    def move(part, shard, lane, peer):
        return remote(acc.at[part, shard], box.at[lane, shard], send.at[lane, shard], recv.at[lane, shard], peer)

    def mine(shard):
        return pltpu.make_async_copy(src.at[:, shard, c], acc.at[:, shard], near.at[0, shard])

    def core(shard):
        return remote(src.at[:, shard, 1 - c], other.at[:, shard], near.at[1, shard], near.at[2, shard], place.core_peer)

    for shard in order:
        core(shard).start()
        mine(shard).start()
    yield
    for half in halves:
        for j in half:
            shard = order[j]
            mine(shard).wait()
            core(shard).wait_recv()

            @pl.loop(0, 4)
            def _(part):
                acc[part, shard] = (
                    acc[part, shard].astype(f32) + other[part, shard].astype(f32)
                ).astype(kind)

            if j % 2 == 0:
                move(bd, shard, far, place.x_peer).start()
                move(bx, shard, via_x, place.x_peer).start()
            else:
                move(bd, shard, far, place.y_peer).start()
                move(by, shard, via_y, place.y_peer).start()
        yield
    for half in halves:
        for j in half:
            shard = order[j]
            move(bd, shard, far, place.x_peer).wait_recv()
            if j % 2 == 0:
                add(by, shard, far)
                move(by, shard, via_y, place.y_peer).start()
            else:
                add(bx, shard, far)
                move(bx, shard, via_x, place.x_peer).start()
        yield
    for half in halves:
        for j in half:
            shard = order[j]
            move(bx, shard, via_x, place.x_peer).wait_recv()
            move(by, shard, via_y, place.y_peer).wait_recv()
            add(b, shard, via_x, via_y)
        yield
    result = pltpu.make_async_copy(acc.at[b], out, one.at[0])
    result.start()
    for shard in range(nz):
        core(shard).wait_send()
        for lane in (far, via_x, via_y):
            move(b, shard, lane, place.x_peer).wait_send()
    result.wait()
    yield


def chain_reduce_task(place, src, out, scratch):
    acc, box, total, one, send, recv = scratch
    kind = acc.dtype
    z, nz = place.z, place.nz
    up, down = range(2)
    order = far_first(place)
    halves = [range(0, nz // 2), range(nz // 2, nz)]

    def add(shard, lane):
        acc[shard] = (acc[shard].astype(f32) + box[lane, shard].astype(f32)).astype(kind)

    def move(shard, lane):
        peer = place.down_peer if lane else place.up_peer
        return remote(acc.at[shard], box.at[lane, shard], send.at[lane, shard], recv.at[lane, shard], peer)

    load = pltpu.make_async_copy(src, acc, one.at[0])
    load.start()
    yield
    load.wait()
    for half in halves:
        for j in half:
            shard = order[j]

            @pl.when(z < shard)
            def _():
                @pl.when(z > 0)
                def _():
                    move(shard, up).wait_recv()
                    add(shard, up)

                move(shard, up).start()

            @pl.when(z > shard)
            def _():
                @pl.when(z + 1 < nz)
                def _():
                    move(shard, down).wait_recv()
                    add(shard, down)

                move(shard, down).start()

        yield
    total[...] = acc[z].astype(f32)

    @pl.when(z > 0)
    def _():
        move(z, up).wait_recv()
        total[...] += box[up, z].astype(f32)

    @pl.when(z + 1 < nz)
    def _():
        move(z, down).wait_recv()
        total[...] += box[down, z].astype(f32)

    result = pltpu.make_async_copy(total, out, one.at[1])
    result.start()
    for shard in range(nz):
        pl.when(z < shard)(lambda: move(shard, up).wait_send())
        pl.when(z > shard)(lambda: move(shard, down).wait_send())
    result.wait()
    yield


def plane_reduce_job(array, plan):
    nz = lax.axis_size("seq") // 2
    shape = array.shape[1:]
    acc, other, box, _, one, near, _, _ = reduce_scratch(nz, shape, array.dtype)
    sems = pltpu.SemaphoreType.DMA((3, nz))
    return Job(
        [array.reshape((4, nz, 2) + shape)],
        [jax.ShapeDtypeStruct((nz,) + shape, array.dtype)],
        [acc, other, pltpu.VMEM((3, nz) + shape, array.dtype), one, near, sems, sems],
        plane_reduce_task,
        plan,
    )


def chain_reduce_job(array, plan):
    nz, *shape = array.shape
    shape = tuple(shape)
    sems = pltpu.SemaphoreType.DMA((2, nz))
    return Job(
        [array],
        [jax.ShapeDtypeStruct(shape, f32)],
        [
            pltpu.VMEM((nz,) + shape, array.dtype),
            pltpu.VMEM((2, nz) + shape, array.dtype),
            pltpu.VMEM(shape, f32),
            pltpu.SemaphoreType.DMA((2,)),
            sems,
            sems,
        ],
        chain_reduce_task,
        plan,
    )


def reduce_job(array, plan):
    nz = lax.axis_size("seq") // 2
    shape = array.shape[1:]
    return Job(
        [array.reshape((4, nz, 2) + shape)],
        [jax.ShapeDtypeStruct(shape, f32)],
        reduce_scratch(nz, shape, array.dtype),
        reduce_task,
        plan,
    )


def total_scratch(nz, shape, shared):
    return [
        pltpu.VMEM((4,) + shape, bf16),
        pltpu.VMEM((2, shared, LANES), bf16),
        pltpu.VMEM((nz + 1, shared, LANES), bf16),
        pltpu.VMEM(shape, f32),
        pltpu.SemaphoreType.DMA((2, 3)),
        pltpu.SemaphoreType.DMA((2, nz)),
    ]


def total_task(place, src, out, scratch):
    box, pair_box, lines, sums, pair, chain = scratch
    z, c, nz = place.z, place.c, place.nz
    rows = src.shape[0]
    shared = lines.shape[1]
    tail = pl.ds(rows - shared, shared)

    def swap(source, dst, i, peer):
        return remote(source, dst, pair.at[0, i], pair.at[1, i], peer)

    box[0] = src[...].astype(bf16)
    first = swap(box.at[0], box.at[2], 0, place.x_peer)
    first.start()
    yield
    first.wait()
    sums[...] = box[0].astype(f32) + box[2].astype(f32)
    box[1] = sums[...].astype(bf16)
    second = swap(box.at[1], box.at[3], 1, place.y_peer)
    second.start()
    yield
    second.wait()
    sums[...] = box[1].astype(f32) + box[3].astype(f32)
    pair_box[0] = sums[tail].astype(bf16)
    third = swap(pair_box.at[0], pair_box.at[1], 2, place.core_peer)
    third.start()
    yield
    third.wait()
    lines[nz] = (pair_box[0].astype(f32) + pair_box[1].astype(f32)).astype(bf16)

    def along(step):
        peer = lax.rem(z + step, nz)
        return remote(lines.at[nz], lines.at[z], chain.at[0, step], chain.at[1, step], (place.b, 2 * peer + c))

    for step in range(1, nz):
        along(step).start()
    lines[z] = lines[nz]
    yield
    for step in range(1, nz):
        along(step).wait_recv()
    value = lines[0].astype(f32)
    for shard in range(1, nz):
        value = value + lines[shard].astype(f32)
    out[: rows - shared] = sums[: rows - shared]
    out[tail] = value
    for step in range(1, nz):
        along(step).wait_send()
    yield


def prepare(jobs, pos_rows, first_w, second_w, third_w, rates, tables, ids):
    layers, hidden, own = third_w.shape
    length = pos_rows.shape[1]
    rows = (own // 8,) + tables[4].shape
    results = [
        jax.ShapeDtypeStruct((layers, 4, hidden, length), f32),
        jax.ShapeDtypeStruct((layers, own, length), f32),
        jax.ShapeDtypeStruct((layers, own, LANES), f32),
    ] + [jax.ShapeDtypeStruct(rows, f32)] * (2 * layers)

    def body(place, runner, ins, outs, scratch, staged):
        pos, first, second, third, rate = ins[:5]
        factors = ins[5:]
        acts, shaped, squares = outs[:3]
        specs = outs[3:]
        spans, groups = length // SPAN, own // 8
        squares[...] = jnp.zeros_like(squares)
        staged.need(0, 1, 2, 3, 4)
        for part in range(8):
            runner.phase()

            @pl.loop(part * spans // 8, (part + 1) * spans // 8)
            def _(i):
                for layer in range(layers):
                    filter_span(
                        layer, pl.multiple_of(i * SPAN, SPAN), pos, first, second, third, rate, acts, shaped, squares
                    )

        staged.ready(0, 1, 2)
        staged.need(*range(5, 5 + TABLES))
        for part in range(6):
            runner.phase()

            @pl.loop(part * groups // 6, (part + 1) * groups // 6)
            def _(group):
                filter_points(group, factors, shaped, squares, specs)

    return fused_call(
        "prepare",
        body,
        [pos_rows, first_w, second_w, third_w, rates, *tables],
        results,
        [],
        jobs,
        False,
        ids,
    )


def last(jobs, pos_rows, second_w, third_w, rates, kept, grad_taps, ids):
    layers, hidden, own = third_w.shape
    length = pos_rows.shape[1]
    nz = lax.axis_size("seq") // 2
    each, shared = hidden + 8, hidden
    payload = jax.ShapeDtypeStruct((layers * (each + shared), LANES), f32)

    def body(place, runner, ins, outs, scratch, staged):
        pos, second, third, rate, acts, shaped, squares = ins[:7]
        taps = ins[7:]
        dots, grad_third, grad_second, grad_first, payload_in = scratch[:5]
        for ref in (dots, grad_third, grad_second, grad_first, payload_in):
            ref[...] = jnp.zeros_like(ref)
        runner.phase()
        spans = length // SPAN
        staged.need(5, *range(7, 7 + layers))

        @pl.loop(0, spans)
        def _(i):
            for layer in range(layers):
                filter_back_dot(layer, pl.multiple_of(i * SPAN, SPAN), shaped, taps[layer], dots)

        staged.need(0, 1, 2, 3, 4, 6)
        for part in range(8):
            runner.phase()

            @pl.loop(part * spans // 8, (part + 1) * spans // 8)
            def _(i):
                for layer in range(layers):
                    filter_back_span(
                        layer, pl.multiple_of(i * SPAN, SPAN), pos, second, third, rate, acts, shaped, squares,
                        taps[layer], dots, (grad_third, grad_second, grad_first)
                    )

        for layer in range(layers):
            start = layer * each
            payload_in[start : start + hidden, :own] = grad_third[layer]
            lag = taps[layer][:, 0].reshape(own, LANES)
            pick = jnp.where(lax.broadcasted_iota(jnp.int32, (8, LANES), 1) == 0, 1.0, 0.0)
            payload_in[start + hidden : start + each, :own] = near_dot(pick, lag, 1, 1)
            start = layers * each + layer * shared
            payload_in[start : start + FEATURES, :hidden] = grad_first[layer][:, :hidden]
            payload_in[start + FEATURES : start + FEATURES + 8, :hidden] = pltpu.roll(
                grad_first[layer][FEATURES - 16 : FEATURES - 8], hidden, 1
            )[:, :hidden]
            payload_in[start : start + hidden, hidden : 2 * hidden] = grad_second[layer]
        runner.add(total_task(place, payload_in, outs[0], scratch[5:]), 4)

    return fused_call(
        "last",
        body,
        [pos_rows, second_w, third_w, rates, *kept, *grad_taps],
        [payload],
        [
            pltpu.VMEM((layers, own, LANES), f32),
            pltpu.VMEM((layers, hidden, own), f32),
            pltpu.VMEM((layers, hidden, hidden), f32),
            pltpu.VMEM((layers, FEATURES, 2 * hidden), f32),
            pltpu.VMEM(payload.shape, f32),
        ]
        + total_scratch(nz, payload.shape, layers * shared),
        jobs,
        True,
        ids,
    )


def conv_lanes(value, rim_near, rim_far):
    lane = lax.broadcasted_iota(jnp.int32, value.shape, 1)
    near = jnp.where(lane == 0, rim_near, pltpu.roll(value, 1, 1))
    far = jnp.where(lane == 0, rim_far, jnp.where(lane == 1, rim_near, pltpu.roll(value, 2, 1)))
    return near, far


def rows_of(ref, stream, block, count):
    value = ref[stream, pl.ds(block, count)].astype(f32)
    return value.reshape(-1, value.shape[-1])


def short_out(mixed, conv, rim, stream, block, count=1):
    value = rows_of(mixed, stream, block, count)
    side, edge = rows_of(conv, stream, block, count), rows_of(rim, stream, block, count)
    near, far = conv_lanes(value, edge[:, 1:2], edge[:, 0:1])
    return side[:, 0:1] * far + side[:, 1:2] * near + side[:, 2:3] * value


def by_blocks(nblocks, most):
    return max(k for k in range(1, most + 1) if nblocks % k == 0)


def edge_scratch(streams, nblocks, chans):
    rows = pltpu.VMEM((streams, 16, nblocks * chans), f32)
    return [rows, rows, pltpu.VMEM((streams, nblocks, chans, LANES), f32), pltpu.SemaphoreType.DMA((2,))]


def edge_copy(place, scratch, to_right):
    out, came, _, sems = scratch
    ns = 2 * place.nz
    peer = lax.min(place.s + 1, ns - 1) if to_right else lax.max(place.s - 1, 0)
    return remote(out, came, sems.at[0], sems.at[1], (place.b, peer))


def send_edge(place, scratch, tiles_of, first, to_right):
    out = scratch[0]
    row = lax.broadcasted_iota(jnp.int32, (16, LANES), 0)
    lane = lax.broadcasted_iota(jnp.int32, (16, LANES), 1)
    pick = jnp.where(jnp.logical_and(lane == row + first, row < 2), 1.0, 0.0).astype(bf16)
    for stream in range(out.shape[0]):
        high, low = in_two(tiles_of(stream).reshape(-1, LANES))
        out[stream] = contract(
            jnp.concatenate([pick, pick], axis=1), jnp.concatenate([high, low], axis=1), 1, 1
        )
    has = place.s + 1 < 2 * place.nz if to_right else place.s > 0
    pl.when(has)(lambda: edge_copy(place, scratch, to_right).start())


def take_edge(place, scratch, to_right):
    _, came, cols, _ = scratch
    _, nblocks, chans, _ = cols.shape
    comes = place.s > 0 if to_right else place.s + 1 < 2 * place.nz
    sends = place.s + 1 < 2 * place.nz if to_right else place.s > 0

    @pl.when(comes)
    def _():
        edge_copy(place, scratch, to_right).wait_recv()
        row = lax.broadcasted_iota(jnp.int32, (16, LANES), 0)
        lane = lax.broadcasted_iota(jnp.int32, (16, LANES), 1)
        spread = jnp.where(jnp.logical_and(lane == row, row < 2), 1.0, 0.0).astype(bf16)
        both = jnp.concatenate([spread, spread], axis=0)
        for stream in range(cols.shape[0]):
            pair = jnp.concatenate(in_two(came[stream]), axis=0)
            cols[stream] = contract(pair, both, 0, 0).reshape(nblocks, chans, LANES)

    @pl.when(jnp.logical_not(comes))
    def _():
        cols[...] = jnp.zeros_like(cols)

    pl.when(sends)(lambda: edge_copy(place, scratch, to_right).wait_send())


def sub_rows(chans):
    return 16 if chans % 16 == 0 else chans


def mix_body(place, runner, ins, outs, scratch, staged, layer):
    mixed, conv, spec_re, spec_im, skip = ins[:5]
    tables = ins[5:]
    long_out, gated, sig_re, sig_im, rim = outs
    signal, chan_in, chan_out, tok_in, send, recv = scratch[:6]
    edge = [scratch[6], scratch[7], rim, scratch[8]]
    toks = mixed.shape[3]
    ns, groups, quarters, chans, _ = signal.shape
    take = sub_rows(chans)

    def to_chan(g, step):
        peer = lax.rem(place.s + step, ns)
        return remote(
            signal.at[peer, g],
            chan_in.at[g, pl.ds(place.s * quarters, quarters)],
            send.at[0, g, step],
            recv.at[0, g, step],
            (place.b, peer),
        )

    def send_pieces(step, first, value):
        peer = lax.rem(place.s + step, ns)
        count = value.shape[0] // chans
        for k in range(count):
            for q in range(quarters):
                piece = value[k * chans : (k + 1) * chans, q * LANES : (q + 1) * LANES]
                signal[peer, first + k, q] = piece

        @pl.when(step < ns)
        def _():
            for k in range(count):
                to_chan(first + k, step).start()

        @pl.when(step == ns)
        def _():
            for k in range(count):
                for q in range(quarters):
                    chan_in[first + k, place.s * quarters + q] = signal[peer, first + k, q]

    def to_tok(g, step):
        peer = lax.rem(place.s + step, ns)
        return remote(
            chan_out.at[g, pl.ds(peer * quarters, quarters)],
            tok_in.at[place.s, g],
            send.at[1, g, step],
            recv.at[1, g, step],
            (place.b, peer),
        )

    staged.need(0)
    send_edge(place, edge, lambda k: mixed[k, :, :, toks - LANES :].astype(f32), LANES - 2, True)
    runner.phase()
    take_edge(place, edge, True)
    staged.ready(4)
    staged.need(1)
    share = by_blocks(groups, 3)
    for first in range(0, groups, share):

        @pl.loop(1, ns + 1)
        def _(step):
            peer = lax.rem(place.s + step, ns)
            block = peer * groups + first
            value = short_out(mixed, conv, rim, 1, block, share) * short_out(mixed, conv, rim, 2, block, share)
            send_pieces(step, first, value.astype(bf16))

    staged.need(2, 3, 4, *range(5, 5 + TABLES))
    runner.phase()
    for g in range(groups):

        @pl.loop(1, ns)
        def _(step):
            to_chan(g, step).wait_recv()

        @pl.loop(0, chans // take)
        def _(i):
            at = pl.ds(pl.multiple_of(i * take, take), take)
            block = chan_in[g, :, at, :].astype(f32)
            base = (g * chans) // 8 + i * (take // 8)
            xs = [block[:, 8 * j : 8 * j + 8, :] for j in range(take // 8)]
            products = []
            for j, (re, im) in enumerate(to_points(xs, tables, True)):
                sig_re[base + j] = re
                sig_im[base + j] = im
                tap_re, tap_im = spec_re[base + j], spec_im[base + j]
                products.append((re * tap_re - im * tap_im, re * tap_im + im * tap_re))
            found = from_points(products, tables)
            parts = [y + skip[layer, base + j][None] * xs[j] for j, y in enumerate(found)]
            chan_out[g, :, at, :] = jnp.concatenate(parts, axis=1).astype(bf16)

        @pl.loop(1, ns)
        def _(step):
            to_tok(g, step).start()

        for q in range(quarters):
            tok_in[place.s, g, q] = chan_out[g, place.s * quarters + q]
        runner.phase()

    staged.ready(2, 3)
    for g in range(groups):

        @pl.loop(1, ns)
        def _(step):
            to_tok(g, step).wait_recv()

        @pl.loop(0, ns, unroll=4)
        def _(owner):
            block = owner * groups + g
            value = jnp.concatenate([tok_in[owner, g, q] for q in range(quarters)], axis=1)
            long_out[block] = value
            gated[block] = (short_out(mixed, conv, rim, 0, block) * value.astype(f32)).astype(bf16)

        if g % 2:
            runner.phase()

    for g in range(groups):

        @pl.loop(1, ns)
        def _(step):
            to_chan(g, step).wait_send()
            to_tok(g, step).wait_send()


def mixer_scratch(ns, groups, quarters, chans):
    pieces = pltpu.VMEM((ns, groups, quarters, chans, LANES), bf16)
    lines = pltpu.VMEM((groups, ns * quarters, chans, LANES), bf16)
    sems = pltpu.SemaphoreType.DMA((2, groups, ns))
    return [pieces, lines, lines, pieces, sems, sems]


def mix(jobs, layer, mixed, conv, spec, skip, tables, ids):
    ns = lax.axis_size("seq")
    _, nblocks, chans, toks = mixed.shape
    groups, quarters = nblocks // ns, toks // LANES
    rows = jax.ShapeDtypeStruct((groups * chans // 8,) + tables[4].shape, f32)
    tokens = jax.ShapeDtypeStruct((nblocks, chans, toks), bf16)
    edges = edge_scratch(3, nblocks, chans)
    return fused_call(
        "mix",
        functools.partial(mix_body, layer=layer),
        [mixed, conv, *spec, skip, *tables],
        [tokens, tokens, rows, rows, jax.ShapeDtypeStruct(conv.shape, f32)],
        mixer_scratch(ns, groups, quarters, chans) + edges[:2] + edges[3:],
        jobs,
        True,
        ids,
    )


def unmix_body(place, runner, ins, outs, scratch, staged, layer):
    mixed, conv, rim, long_out, grad_gated, spec_re, spec_im, sig_re, sig_im, skip = ins[:10]
    tables = ins[10:]
    grad_taps, grad_mixed, grad_conv = outs
    pull, chan_in, chan_out, tok_in, send, recv, grad_short, partials = scratch[:8]
    edge = scratch[8:]
    toks = mixed.shape[3]
    runner.phase()
    staged.need(0, 1, 2, 4)
    ns, groups, quarters, chans, _ = pull.shape
    take = sub_rows(chans)

    def to_chan(g, step):
        peer = lax.rem(place.s + step, ns)
        return remote(
            pull.at[peer, g],
            chan_in.at[g, pl.ds(place.s * quarters, quarters)],
            send.at[0, g, step],
            recv.at[0, g, step],
            (place.b, peer),
        )

    def send_pieces(step, first, value):
        peer = lax.rem(place.s + step, ns)
        count = value.shape[0] // chans
        for k in range(count):
            for q in range(quarters):
                piece = value[k * chans : (k + 1) * chans, q * LANES : (q + 1) * LANES]
                pull[peer, first + k, q] = piece

        @pl.when(step < ns)
        def _():
            for k in range(count):
                to_chan(first + k, step).start()

        @pl.when(step == ns)
        def _():
            for k in range(count):
                for q in range(quarters):
                    chan_in[first + k, place.s * quarters + q] = pull[peer, first + k, q]

    def to_tok(g, step):
        peer = lax.rem(place.s + step, ns)
        return remote(
            chan_out.at[g, pl.ds(peer * quarters, quarters)],
            tok_in.at[place.s, g],
            send.at[1, g, step],
            recv.at[1, g, step],
            (place.b, peer),
        )

    share = by_blocks(groups, 3)
    for first in range(0, groups, share):

        @pl.loop(1, ns + 1)
        def _(step):
            block = lax.rem(place.s + step, ns) * groups + first
            gated = grad_gated[pl.ds(block, share)].reshape(share * chans, toks)
            send_pieces(step, first, (gated * short_out(mixed, conv, rim, 0, block, share)).astype(bf16))

    staged.need(5, 6, 7, 8, 9, *range(10, 10 + TABLES))
    runner.phase()
    for g in range(groups):

        @pl.loop(1, ns)
        def _(step):
            to_chan(g, step).wait_recv()

        @pl.loop(0, chans // take)
        def _(i):
            at = pl.ds(pl.multiple_of(i * take, take), take)
            block = chan_in[g, :, at, :].astype(f32)
            base = (g * chans) // 8 + i * (take // 8)
            count = take // 8
            xs = [block[:, 8 * j : 8 * j + 8, :] for j in range(count)]
            signals, taps = [], []
            for j, (re, im) in enumerate(to_points(xs, tables, True)):
                tap_re, tap_im = spec_re[base + j], spec_im[base + j]
                own_re, own_im = sig_re[base + j], sig_im[base + j]
                signals.append((tap_re * re + tap_im * im, tap_re * im - tap_im * re))
                taps.append((own_re * re + own_im * im, own_re * im - own_im * re))
            found = from_points(signals + taps, tables)
            parts = [found[j] + skip[layer, base + j][None] * xs[j] for j in range(count)]
            for j in range(count):
                grad_taps[base + j] = found[count + j]
            chan_out[g, :, at, :] = jnp.concatenate(parts, axis=1).astype(bf16)

        @pl.loop(1, ns)
        def _(step):
            to_tok(g, step).start()

        for q in range(quarters):
            tok_in[place.s, g, q] = chan_out[g, place.s * quarters + q]
        runner.phase()

    staged.ready(0)
    staged.need(3)

    @pl.loop(0, ns * groups, unroll=4)
    def _(block):
        grad_short[0, block] = grad_gated[block] * long_out[block].astype(f32)

    for g in range(groups):

        @pl.loop(1, ns)
        def _(step):
            to_tok(g, step).wait_recv()

        @pl.loop(0, ns, unroll=4)
        def _(owner):
            block = owner * groups + g
            value = jnp.concatenate(
                [tok_in[owner, g, q] for q in range(quarters)], axis=1
            ).astype(f32)
            grad_short[1, block] = value * short_out(mixed, conv, rim, 2, block)
            grad_short[2, block] = value * short_out(mixed, conv, rim, 1, block)

        if g % 2:
            runner.phase()

    send_edge(place, edge, lambda k: grad_short[k, :, :, :LANES], 0, False)
    many = by_blocks(ns * groups, 4)
    ones = jnp.ones((2 * LANES, LANES), bf16)
    for stream in range(3):

        @pl.loop(0, ns * groups // many, unroll=2)
        def _(i):
            at = pl.ds(i * many, many)
            grad = rows_of(grad_short, stream, i * many, many)
            value = rows_of(mixed, stream, i * many, many)
            side = rows_of(rim, stream, i * many, many)
            near, far = conv_lanes(value, side[:, 1:2], side[:, 0:1])
            for k, moved in enumerate((far, near, value)):
                terms = grad * moved
                partial = terms[:, :LANES]
                for q in range(1, quarters):
                    partial += terms[:, q * LANES : (q + 1) * LANES]
                partials[k, at] = partial.reshape(many, chans, LANES)

        sums = [
            product(jnp.concatenate(in_two(partials[k].reshape(-1, LANES)), axis=1), ones)
            for k in range(3)
        ]
        lane = lax.broadcasted_iota(jnp.int32, sums[0].shape, 1)
        found = jnp.where(lane == 0, sums[0], jnp.where(lane == 1, sums[1], sums[2]))
        grad_conv[stream] = found.reshape(ns * groups, chans, LANES)
    staged.ready(2)
    runner.phase()
    take_edge(place, edge, False)
    edge_cols = edge[2]
    for stream in range(3):

        @pl.loop(0, ns * groups // many, unroll=2)
        def _(i):
            value = rows_of(grad_short, stream, i * many, many)
            side, after = rows_of(conv, stream, i * many, many), rows_of(edge_cols, stream, i * many, many)
            lane = lax.broadcasted_iota(jnp.int32, value.shape, 1)
            near = jnp.where(lane == toks - 1, after[:, 0:1], pltpu.roll(value, toks - 1, 1))
            far = jnp.where(
                lane == toks - 1,
                after[:, 1:2],
                jnp.where(lane == toks - 2, after[:, 0:1], pltpu.roll(value, toks - 2, 1)),
            )
            total = side[:, 2:3] * value + side[:, 1:2] * near + side[:, 0:1] * far
            grad_mixed[stream, pl.ds(i * many, many)] = total.astype(bf16).reshape(many, chans, toks)

    for g in range(groups):

        @pl.loop(1, ns)
        def _(step):
            to_chan(g, step).wait_send()
            to_tok(g, step).wait_send()


def unmix(jobs, layer, mixed, conv, rim, long_out, grad_gated, spec, sig, skip, tables, ids):
    ns = lax.axis_size("seq")
    _, nblocks, chans, toks = mixed.shape
    groups, quarters = nblocks // ns, toks // LANES
    return fused_call(
        "unmix",
        functools.partial(unmix_body, layer=layer),
        [mixed, conv, rim, long_out, grad_gated, *spec, *sig, skip, *tables],
        [
            jax.ShapeDtypeStruct((groups * chans // 8, ns * quarters, 8, LANES), f32),
            jax.ShapeDtypeStruct(mixed.shape, bf16),
            jax.ShapeDtypeStruct(conv.shape, f32),
        ],
        mixer_scratch(ns, groups, quarters, chans)
        + [pltpu.VMEM(mixed.shape, f32), pltpu.VMEM(conv.shape, f32)]
        + edge_scratch(3, nblocks, chans),
        jobs,
        True,
        ids,
    )


def on_device(
    tokens,
    cotangent,
    norm_gains,
    w_in,
    short_conv,
    w_out,
    w_fc,
    w_proj,
    filt_w1,
    filt_b1,
    filt_w2,
    filt_b2,
    filt_w3,
    skip_gain,
    decay_rate,
):
    layers, _, width3 = w_in.shape
    width = width3 // 3
    ns = lax.axis_size("seq")
    devices = lax.axis_size("batch") * ns
    stream = tokens[0].astype(f32)
    toks = stream.shape[0]
    length = toks * ns
    own_chans = width // ns
    chans = 16 if own_chans % 16 == 0 else own_chans
    groups = own_chans // chans
    nblocks = ns * groups
    blocked = (3, nblocks, chans)
    tables = transform_tables(length)
    pos_rows = position_rows(length, filt_w1.shape[1])

    gain_cols, conv_cols = norm_gains.shape[2], short_conv.shape[2]
    small = jnp.concatenate(
        [
            jnp.pad(norm_gains.reshape(2 * layers, gain_cols).astype(f32), ((0, 0), (0, LANES - gain_cols))),
            jnp.pad(short_conv.reshape(3 * layers, conv_cols).astype(f32), ((0, 0), (0, LANES - conv_cols))),
        ],
        axis=0,
    )
    small = jnp.pad(small, ((0, -small.shape[0] % 8), (0, 0)))[None]

    first_w = jnp.pad(
        jnp.concatenate([filt_w1, filt_b1[:, None]], axis=1),
        ((0, 0), (0, FEATURES - filt_w1.shape[1] - 1), (0, 0)),
    )
    hidden = filt_w2.shape[1]
    both = jnp.concatenate([filt_b2, decay_rate], axis=1)
    rates = jnp.broadcast_to(both[:, :, None], both.shape + (LANES,))
    skips = jnp.broadcast_to(
        skip_gain.reshape(layers, -1, 8, 1), (layers, own_chans // 8, 8, LANES)
    )

    mats = (w_in, w_out, w_fc, w_proj)
    jobs = [gather_job(small, 0, GATHER_PLANS[0])]
    jobs += [gather_job(mat, 0, plan) for mat, plan in zip(mats, GATHER_PLANS[1:])]
    jobs += [
        column_job(mat, layer, plan)
        for layer in range(1, layers)
        for mat, plan in zip(mats, COLUMN_PLANS)
    ]
    ids = itertools.count()
    sets = [list(range(layers))] if length <= 8192 else [[layer] for layer in range(layers)]
    kept, specs = [], []
    for part in sets:
        of = slice(part[0], part[-1] + 1)
        filters, found = prepare(
            jobs, pos_rows, first_w[of], filt_w2[of], filt_w3[of], rates[of], tables, ids
        )
        kept.append(filters[:3])
        specs += [filters[3 + 2 * k : 5 + 2 * k] for k in range(len(part))]
        gathered = found if part is sets[0] else gathered
        jobs = []
    small_all = gathered[0].reshape(devices, -1, LANES)
    gains = jnp.swapaxes(small_all[:, : 2 * layers, :gain_cols], 0, 1).reshape(layers, 2, width)
    convs = jnp.swapaxes(
        small_all[:, 2 * layers : 5 * layers, :conv_cols], 0, 1
    ).reshape(layers, 3, width3)
    conv_cols_of = [
        jnp.pad(convs[layer].T, ((0, 0), (0, LANES - 3))).reshape(blocked + (LANES,))
        for layer in range(layers)
    ]
    plain = lambda parts: parts.reshape(-1, parts.shape[-1])
    weights = {(i, 0): plain(gathered[1 + i]) for i in range(4)}
    columns = {
        (i, layer): gathered[1 + 4 * layer + i] for layer in range(1, layers) for i in range(4)
    }

    def plane_jobs(layer):
        keys = [(3, layer)] if layer else []
        keys = [key for key in keys + [(0, layer + 1), (1, layer + 1), (2, layer + 1)] if key in columns]
        return keys, [plane_job(columns[key], plan) for key, plan in zip(keys, PLANE_PLANS)]

    saved = []
    for layer in range(layers):
        in_mat = weights[0, layer]
        normed, inv_std = layer_norm_parts(stream)
        norm_in = (normed * gains[layer, 0]).astype(bf16)
        mixed = contract(in_mat, norm_in, 0, 1).astype(bf16)
        mixed = mixed.reshape(blocked + (toks,))
        keys, jobs = plane_jobs(layer)
        (long_out, gated, sig_re, sig_im, rim), arrived = mix(
            jobs, layer, mixed, conv_cols_of[layer], specs[layer], skips, tables, ids
        )
        weights.update({key: plain(parts) for key, parts in zip(keys, arrived)})
        out_mat, fc_mat, proj_mat = (weights[i, layer] for i in (1, 2, 3))
        gated = gated.reshape(width, toks)
        middle = stream + contract(gated, out_mat, 0, 0)
        normed_mid, inv_mid = layer_norm_parts(middle)
        hidden_in = (normed_mid * gains[layer, 1]).astype(bf16)
        hidden_pre = product(hidden_in, fc_mat)
        hidden_act = gelu(hidden_pre).astype(bf16)
        saved.append(
            (normed, inv_std, norm_in, mixed, rim, long_out, gated, (sig_re, sig_im))
            + (normed_mid, inv_mid, hidden_in, hidden_pre, hidden_act)
        )
        stream = middle + product(hidden_act, proj_mat)
    mixed_out, grad = lax.optimization_barrier((stream.astype(bf16), cotangent[0]))
    grad = grad.astype(f32)
    summed = {}
    left_over, half_way = [], []
    small_grads = [None] * layers
    taps_grads = [None] * layers

    def scattered(parts):
        return lax.psum_scatter(parts, ("batch", "seq"), scatter_dimension=0, tiled=False).astype(f32)

    def parts_of(grad_mat):
        return grad_mat.reshape(devices, -1, grad_mat.shape[1])

    for layer in reversed(range(layers)):
        in_mat, out_mat, fc_mat, proj_mat = (weights[i, layer] for i in range(4))
        (normed, inv_std, norm_in, mixed, rim, long_out, gated, sig) = saved[layer][:8]
        (normed_mid, inv_mid, hidden_in, hidden_pre, hidden_act) = saved[layer][8:]
        grad_top = grad.astype(bf16)
        grad_act = contract(grad_top, proj_mat, 1, 1)
        grad_proj = contract(hidden_act, grad_top, 0, 0).astype(bf16)
        grad_pre = (grad_act * gelu_slope(hidden_pre)).astype(bf16)
        grad_hidden = contract(grad_pre, fc_mat, 1, 1)
        grad_fc = contract(hidden_in, grad_pre, 0, 0).astype(bf16)
        grad_gain_mid = jnp.sum(grad_hidden * normed_mid, axis=0)
        grad_middle = grad + norm_back(grad_hidden * gains[layer, 1], normed_mid, inv_mid)
        grad_mix = grad_middle.astype(bf16)
        grad_gated = contract(out_mat, grad_mix, 1, 1).reshape(nblocks, chans, toks)
        grad_out = contract(gated, grad_mix, 1, 0).astype(bf16)
        grad_gated, grad_proj = lax.optimization_barrier((grad_gated, grad_proj))
        if layer == 0:
            pending = left_over + [((3, layer), parts_of(grad_proj)), ((2, layer), parts_of(grad_fc))]
            left_over = [((1, layer), parts_of(grad_out))]
        else:
            summed[3, layer] = scattered(parts_of(grad_proj))
            pending = left_over + [((2, layer), parts_of(grad_fc)), ((1, layer), parts_of(grad_out))]
            left_over = []
        (taps_grads[layer], grad_mixed, grad_conv), arrived = unmix(
            [plane_reduce_job(parts, plan) for (_, parts), plan in zip(pending, PLANE_REDUCE_PLANS)]
            + [chain_reduce_job(part, plan) for (_, part), plan in zip(half_way, UNMIX_CHAIN_PLANS)],
            layer, mixed, conv_cols_of[layer], rim, long_out, grad_gated, specs[layer], sig, skips, tables, ids
        )
        summed.update({key: total for (key, _), total in zip(half_way, arrived[len(pending) :])})
        half_way = [(key, part) for (key, _), part in zip(pending, arrived)]
        grad_mixed = grad_mixed.reshape(width3, toks)
        grad_norm_in = contract(grad_mixed, in_mat, 0, 1)
        grad_in = contract(norm_in, grad_mixed, 0, 1).astype(bf16)
        grad_gain_in = jnp.sum(grad_norm_in * normed, axis=0)
        grad = grad_middle + norm_back(grad_norm_in * gains[layer, 0], normed, inv_std)
        left_over.append(((0, layer), parts_of(grad_in)))
        small_grads[layer] = (
            jnp.stack([grad_gain_in, grad_gain_mid]),
            jnp.swapaxes(grad_conv.reshape(width3, LANES)[:, :3], 0, 1),
        )

    def rows_for(values, cols):
        pieces = jnp.swapaxes(values.reshape(values.shape[0], devices, cols), 0, 1)
        return jnp.pad(pieces, ((0, 0), (0, 0), (0, LANES - cols)))

    small_rows = jnp.concatenate(
        [rows_for(small_grads[layer][0], gain_cols) for layer in range(layers)]
        + [rows_for(small_grads[layer][1], conv_cols) for layer in range(layers)],
        axis=1,
    )
    small_rows = jnp.pad(small_rows, ((0, 0), (0, -small_rows.shape[1] % 8), (0, 0)))
    emb = filt_w1.shape[1]
    left_over.reverse()
    left_over.append(("small", small_rows))
    each, shared = hidden + 8, hidden
    by_column, by_all = [], []
    jobs = [reduce_job(parts, plan) for (_, parts), plan in zip(left_over, LAST_PLANS)]
    jobs += [chain_reduce_job(part, plan) for (_, part), plan in zip(half_way, CHAIN_PLANS)]
    for part, acts in zip(sets, kept):
        of = slice(part[0], part[-1] + 1)
        (totals,), arrived = last(
            jobs, pos_rows, filt_w2[of], filt_w3[of], rates[of], acts, taps_grads[of], ids
        )
        if part is sets[0]:
            summed.update({key: total for (key, _), total in zip(left_over + half_way, arrived)})
        jobs = []
        by_column.append(totals[: len(part) * each].reshape(-1, each, LANES))
        by_all.append(totals[len(part) * each :].reshape(-1, shared, LANES))
    by_column, by_all = jnp.concatenate(by_column), jnp.concatenate(by_all)
    small_sum = summed["small"]
    block = [jnp.stack([summed[i, layer] for layer in range(layers)]) for i in range(4)]
    gains_grad = small_sum[: 2 * layers, :gain_cols].reshape(layers, 2, gain_cols)
    conv_grad = small_sum[2 * layers : 5 * layers, :conv_cols].reshape(layers, 3, conv_cols)
    return (
        mixed_out[None],
        grad[None],
        gains_grad,
        block[0],
        conv_grad,
        block[1],
        block[2],
        block[3],
        by_all[:, :emb, :hidden],
        by_all[:, emb, :hidden],
        by_all[:, :, hidden : 2 * hidden],
        by_all[:, FEATURES + emb - 32, :hidden],
        by_column[:, :hidden, :own_chans],
        by_column[:, hidden, :own_chans],
    )


def solution(mesh):
    both = ("batch", "seq")
    in_specs = (
        P("batch", "seq", None),
        P("batch", "seq", None),
        P(None, None, both),
        P(None, both, None),
        P(None, None, both),
        P(None, both, None),
        P(None, both, None),
        P(None, both, None),
        P(),
        P(),
        P(),
        P(),
        P(None, None, "seq"),
        P(None, "seq"),
        P(None, "seq"),
    )
    out_specs = in_specs[:14]
    return jax.shard_map(
        on_device, mesh=mesh, in_specs=in_specs, out_specs=out_specs, check_vma=False
    )
```
